32 devices in a mesh: dp: 8 (over y, x, core), mp: 4 (over z).
Axes of the slice: x: 2, y: 2, z: 4, core: 2. Of those that a mesh axis runs over, the one named last changes fastest.
Arguments:
- tokens: bfloat16 [4096, 768], P('dp'), may hold values from -6 to 6
- memory: bfloat16 [8, 1500, 768], P('dp', 'mp'), may hold values from -6 to 6
- lengths: int32 [8], P('dp'), may hold values from 1 to 448, as said below
- cotangent: bfloat16 [4096, 768], P('dp'), may hold values from -6 to 6
- ln_gain: float32 [3, 768], replicated, may hold values from 0.1 to 1.9
- ln_bias: float32 [3, 768], replicated, may hold values from -3 to 3
- self_in: bfloat16 [3, 768, 768], P(None, None, 'mp'), may hold values from -0.21875 to 0.21875
- self_bias: bfloat16 [2, 768], P(None, 'mp'), may hold values from -3 to 3
- self_out: bfloat16 [768, 768], P('mp'), may hold values from -0.875 to 0.875
- self_out_bias: bfloat16 [768], replicated, may hold values from -3 to 3
- cross_q: bfloat16 [768, 768], P(None, 'mp'), may hold values from -0.21875 to 0.21875
- cross_kv: bfloat16 [2, 768, 768], P(None, None, 'mp'), may hold values from -0.21875 to 0.21875
- cross_bias: bfloat16 [2, 768], P(None, 'mp'), may hold values from -3 to 3
- cross_out: bfloat16 [768, 768], P('mp'), may hold values from -2.5 to 2.5
- cross_out_bias: bfloat16 [768], replicated, may hold values from -3 to 3
- mlp_in: bfloat16 [768, 3072], P(None, 'mp'), may hold values from -0.21875 to 0.21875
- mlp_in_bias: bfloat16 [3072], P('mp'), may hold values from -3 to 3
- mlp_out: bfloat16 [3072, 768], P('mp'), may hold values from -0.109375 to 0.109375
- mlp_out_bias: bfloat16 [768], replicated, may hold values from -3 to 3
Outputs:
- mixed: bfloat16 [4096, 768], P('dp')
- input_grad: bfloat16 [4096, 768], P('dp')
- memory_grad: bfloat16 [8, 1500, 768], P('dp', 'mp')
- ln_gain_grad: float32 [3, 768], replicated
- ln_bias_grad: float32 [3, 768], replicated
- self_in_grad: float32 [3, 768, 768], P(None, 'dp', 'mp')
- self_bias_grad: float32 [2, 768], P(None, 'mp')
- self_out_grad: float32 [768, 768], P('mp', 'dp')
- self_out_bias_grad: float32 [768], replicated
- cross_q_grad: float32 [768, 768], P('dp', 'mp')
- cross_kv_grad: float32 [2, 768, 768], P(None, 'dp', 'mp')
- cross_bias_grad: float32 [2, 768], P(None, 'mp')
- cross_out_grad: float32 [768, 768], P('mp', 'dp')
- cross_out_bias_grad: float32 [768], replicated
- mlp_in_grad: float32 [768, 3072], P('dp', 'mp')
- mlp_in_bias_grad: float32 [3072], P('mp')
- mlp_out_grad: float32 [3072, 768], P('mp', 'dp')
- mlp_out_bias_grad: float32 [768], replicated
The draws below stay inside these ranges and needn't reach their ends.
Inputs may be any that keep to these rules, and one draw needn't show every extreme that they name: `lengths`: the 1 clips of each group fit its 512 slots; some clip has exactly 448 tokens.
All inputs are finite; a program needn't handle non-finite values.
Results may differ from the reference program's by a relative error of at most 0.03.
Values may be sent and summed in bfloat16 or wider, within the bound.
A program may use at most 128 MiB of HBM per device.

```python
import jax
import jax.numpy as jnp
from jax import lax

D = 768
HEADS = 12
HD = 64
FF = 3072
FRAMES = 1500
MAXLEN = 448
CLIPS_DEV = 1
TOK_DEV = 512
CLIPS = 8
TOKENS = 4096
N_DP = 8


def draw_lengths(key, part):
    group_count = CLIPS // CLIPS_DEV
    drawn = jax.random.randint(jax.random.fold_in(key, 11), (group_count, CLIPS_DEV), min(48, MAXLEN // 2), min(112, MAXLEN) + 1)
    short = jax.random.randint(jax.random.fold_in(key, 12), (group_count, CLIPS_DEV), 1, 6)
    picked = jax.random.randint(jax.random.fold_in(key, 13), (group_count,), 0, 8) == 0
    chosen = jax.random.randint(jax.random.fold_in(key, 14), (), 0, group_count)
    groups = jnp.arange(group_count, dtype=jnp.int32)
    long_group = picked | (groups == chosen)
    long_len = jax.random.randint(jax.random.fold_in(key, 15), (group_count,), 2 * MAXLEN // 3, MAXLEN + 1)
    long_len = jnp.where(groups == chosen, MAXLEN, long_len)
    slot = jax.random.randint(jax.random.fold_in(key, 16), (group_count,), 0, CLIPS_DEV)
    is_slot = jnp.arange(CLIPS_DEV, dtype=jnp.int32)[None, :] == slot[:, None]
    grid = jnp.where(long_group[:, None], jnp.where(is_slot, long_len[:, None], short), drawn)
    return grid.reshape(CLIPS).astype(jnp.int32)


def levels(stream_key, extent, shards, low, largest):
    level, own = 1.0, jax.random.fold_in(stream_key, 6)
    for position, shards_of in shards:
        draws = jnp.exp(jax.random.uniform(jax.random.fold_in(own, position), (shards_of,), jnp.float32, low / len(shards), largest / len(shards)))
        level = level * jnp.repeat(draws, extent[position] // shards_of).reshape([-1 if axis == position else 1 for axis in range(len(extent))])
    return level


def bell_draw(own_key, shape, spread, bound, cuts=(), kind=jnp.bfloat16):
    level = levels(own_key, shape, cuts, -0.22, 0.18) if cuts else 1.0
    array = jax.random.normal(own_key, shape, jnp.float32) * spread * level
    return jnp.minimum(jnp.maximum(array, -bound), bound).astype(kind)


def setup_inputs(seed: int = 0) -> dict:
    streams_of = jax.random.split(jax.random.key(seed), 20)
    return {
        "tokens": bell_draw(streams_of[0], (TOKENS, D), 1.0, 6.0, ((0, 8),)),
        "memory": bell_draw(streams_of[1], (CLIPS, FRAMES, D), 1.0, 6.0, ((0, 8), (1, 4))),
        "lengths": draw_lengths(jax.random.fold_in(streams_of[19], 71), 0),
        "cotangent": bell_draw(streams_of[3], (TOKENS, D), 1.0, 6.0, ((0, 8),)),
        "ln_gain": jnp.clip(1.0 + 0.18 * jax.random.normal(streams_of[4], (3, D), jnp.float32), 0.1, 1.9),
        "ln_bias": bell_draw(streams_of[5], (3, D), 0.5, 3.0, (), jnp.float32),
        "self_in": bell_draw(streams_of[6], (3, D, D), D ** -0.5, 0.21875, ((2, 4),)),
        "self_bias": bell_draw(streams_of[7], (2, D), 0.5, 3.0, ((1, 4),)),
        "self_out": bell_draw(streams_of[8], (D, D), (D // 16) ** -0.5, 0.875, ((0, 4),)),
        "self_out_bias": bell_draw(streams_of[9], (D,), 0.5, 3.0),
        "cross_q": bell_draw(streams_of[10], (D, D), D ** -0.5, 0.21875, ((1, 4),)),
        "cross_kv": bell_draw(streams_of[11], (2, D, D), D ** -0.5, 0.21875, ((2, 4),)),
        "cross_bias": bell_draw(streams_of[12], (2, D), 0.5, 3.0, ((1, 4),)),
        "cross_out": bell_draw(streams_of[13], (D, D), (max(D // 128, 1)) ** -0.5, 2.5, ((0, 4),)),
        "cross_out_bias": bell_draw(streams_of[14], (D,), 0.5, 3.0),
        "mlp_in": bell_draw(streams_of[15], (D, FF), D ** -0.5, 0.21875, ((1, 4),)),
        "mlp_in_bias": bell_draw(streams_of[16], (FF,), 0.5, 3.0, ((0, 4),)),
        "mlp_out": bell_draw(streams_of[17], (FF, D), FF ** -0.5, 0.109375, ((0, 4),)),
        "mlp_out_bias": bell_draw(streams_of[18], (D,), 0.5, 3.0),
    }


@jax.custom_vjp
def low(v):
    return lax.optimization_barrier(v.astype(jnp.bfloat16)).astype(jnp.float32)

@jax.custom_vjp
def low_back(v):
    return v

def low_keep(v):
    return (low(v), None)

def low_pass(kept, grad):
    return (grad,)

def back_keep(v):
    return (v, None)

def back_low(kept, grad):
    return (low(grad),)
low.defvjp(low_keep, low_pass)
low_back.defvjp(back_keep, back_low)
HIGH = lax.Precision.HIGHEST

def product(left, right):
    return jnp.matmul(left, right, precision=HIGH)

def rounded(values):
    return low(low_back(values))

def normalize(values, gain, shift):
    average = lax.optimization_barrier(jnp.mean(values, axis=-1, keepdims=True))
    centred = values - average
    variance = lax.optimization_barrier(jnp.mean(centred * centred, axis=-1, keepdims=True))
    return centred * lax.rsqrt(variance + 1e-05) * gain + shift

def softmax_rows(scores):
    row_max = lax.optimization_barrier(jnp.max(scores, axis=-1, keepdims=True))
    shifted = jnp.exp(scores - row_max)
    return shifted / lax.optimization_barrier(jnp.sum(shifted, axis=-1, keepdims=True))

def one_group(weights_all, tokens_in, memory_in, clip_lengths):
    ln_gain, ln_bias, self_in, self_bias, self_out, self_out_bias, cross_q, cross_kv, cross_bias, cross_out, cross_out_bias, mlp_in, mlp_in_bias, mlp_out, mlp_out_bias = weights_all
    row_count = tokens_in.shape[0]
    clip_count = clip_lengths.shape[0]
    clip_ends = jnp.cumsum(clip_lengths)
    positions = jnp.arange(row_count, dtype=jnp.int32)
    clip_of = lax.optimization_barrier(jnp.sum((positions[:, None] >= clip_ends[None, :]).astype(jnp.int32), axis=1))
    valid_rows = (clip_of < clip_count).astype(jnp.float32)[:, None]
    allowed = (clip_of[:, None] == clip_of[None, :]) & (positions[None, :] <= positions[:, None]) & (clip_of[:, None] < clip_count)
    normed_one = low(normalize(tokens_in, ln_gain[0], ln_bias[0]))
    queries = rounded(product(normed_one, self_in[0]) + self_bias[0]).reshape(row_count, HEADS, HD)
    keys_self = rounded(product(normed_one, self_in[1])).reshape(row_count, HEADS, HD)
    values_self = rounded(product(normed_one, self_in[2]) + self_bias[1]).reshape(row_count, HEADS, HD)
    scores = jnp.einsum('thd,shd->hts', queries, keys_self, precision=HIGH) * 0.125
    scores = low_back(jnp.where(allowed[None], scores, -1000000000.0))
    probs = low(softmax_rows(scores))
    self_att = jnp.einsum('hts,shd->thd', probs, values_self, precision=HIGH).reshape(row_count, D) * valid_rows
    self_att = rounded(self_att)
    mixed_one = tokens_in + low_back(product(self_att, self_out) + self_out_bias)
    normed_two = low(normalize(mixed_one, ln_gain[1], ln_bias[1]))
    cross_queries = rounded(product(normed_two, cross_q) + cross_bias[0]).reshape(row_count, HEADS, HD)
    cross_keys = rounded(jnp.einsum('cfd,de->cfe', memory_in, cross_kv[0], precision=HIGH))
    cross_values = rounded(jnp.einsum('cfd,de->cfe', memory_in, cross_kv[1], precision=HIGH) + cross_bias[1])

    def per_clip(running, clip_item):
        clip_index, clip_keys, clip_values = clip_item
        clip_scores = jnp.einsum('thd,fhd->htf', cross_queries, clip_keys.reshape(-1, HEADS, HD), precision=HIGH) * 0.125
        clip_probs = low(softmax_rows(low_back(clip_scores)))
        clip_result = jnp.einsum('htf,fhd->thd', clip_probs, clip_values.reshape(-1, HEADS, HD), precision=HIGH).reshape(row_count, D)
        return (jnp.where((clip_of == clip_index)[:, None], clip_result, running), None)
    cross_sum, _ = lax.scan(jax.checkpoint(per_clip), jnp.zeros((row_count, D), jnp.float32), (jnp.arange(clip_count, dtype=jnp.int32), cross_keys, cross_values))
    cross_att = rounded(cross_sum)
    mixed_two = mixed_one + low_back(product(cross_att, cross_out) + cross_out_bias)
    normed_three = low(normalize(mixed_two, ln_gain[2], ln_bias[2]))
    hidden = low_back(product(normed_three, mlp_in) + mlp_in_bias)
    active = low(jax.nn.gelu(hidden, approximate=False))
    return mixed_two + low_back(product(active, mlp_out) + mlp_out_bias)

def reference(tokens, memory, lengths, cotangent, ln_gain, ln_bias, self_in, self_bias, self_out, self_out_bias, cross_q, cross_kv, cross_bias, cross_out, cross_out_bias, mlp_in, mlp_in_bias, mlp_out, mlp_out_bias):
    weights_all = tuple((w.astype(jnp.float32) for w in (ln_gain, ln_bias, self_in, self_bias, self_out, self_out_bias, cross_q, cross_kv, cross_bias, cross_out, cross_out_bias, mlp_in, mlp_in_bias, mlp_out, mlp_out_bias)))
    tokens_f = tokens.astype(jnp.float32).reshape(N_DP, TOK_DEV, D)
    memory_f = memory.astype(jnp.float32).reshape(N_DP, CLIPS_DEV, FRAMES, D)
    length_grid = lengths.reshape(N_DP, CLIPS_DEV)

    def whole(tokens_all, memory_all, weights_in):

        def one(pieces):
            return one_group(weights_in, pieces[0], pieces[1], pieces[2])
        return lax.map(jax.checkpoint(one), (tokens_all, memory_all, length_grid))
    result, pullback = jax.vjp(whole, tokens_f, memory_f, weights_all)
    grad_tokens, grad_memory, grads = pullback(cotangent.astype(jnp.float32).reshape(N_DP, TOK_DEV, D))
    return (result.reshape(TOKENS, D).astype(jnp.bfloat16), grad_tokens.reshape(TOKENS, D).astype(jnp.bfloat16), grad_memory.reshape(CLIPS, FRAMES, D).astype(jnp.bfloat16), grads[0], grads[1], grads[2], grads[3], grads[4], grads[5], grads[6], grads[7], grads[8], grads[9], grads[10], grads[11], grads[12], grads[13], grads[14])
```

```python
import math

import jax
import jax.numpy as jnp
from jax import lax
from jax.experimental import pallas as pl
from jax.experimental.pallas import tpu as pltpu
from jax.sharding import PartitionSpec as P

HD = 64
D, HW, T, TA, FQ, FP, AB, RB = 768, 192, 512, 448, 375, 384, 112, 128
NH = HW // HD
FT = 4 * FP
BF, F32 = jnp.bfloat16, jnp.float32
VMEM_LIMIT = 62 << 20


def nn(a, b):
    return lax.dot_general(a, b, (((1,), (0,)), ((), ())), preferred_element_type=F32)


def nt(a, b):
    return lax.dot_general(a, b, (((1,), (1,)), ((), ())), preferred_element_type=F32)


def tn(a, b):
    return lax.dot_general(a, b, (((0,), (0,)), ((), ())), preferred_element_type=F32)


def ds(start, size, step=16):
    return pl.ds(pl.multiple_of(start, step), size)


def layer_kernel(
    tok, mem, lens, cot, rep, qb, w_si, w_so, w_cq, w_ck, w_co, w_mi, w_mo,
    mixed_o, igrad_o, mgrad_o, grads_o, small_o,
    T_, G_, len_, qb_, si, so, cq, ck, co, mi, mo, slab,
    x1, q_, k_, v_, ps_, satt, m1, x2, cq_, K_, V_, pc_, catt, m2, x3, act, gh,
    ups, dO, dsb, gkv, gcq, upo, dOs, gqkv,
    pS, pR, zS, zR, fin,
    mtS, mtR, mtZ, mtZr, mtF,
    gb, gR, gFr, gC, gO, sb, sR,
    lsem, ssem, rsem,
):
    d, z = lax.axis_index("dp"), lax.axis_index("mp")
    c = lax.rem(d, 2)
    p = z // 2
    chip = d // 2
    native = c == p
    foreign = jnp.logical_not(native)
    flip = lambda a, bit: a + bit * (1 - 2 * lax.rem(a // bit, 2))
    z1, z2 = flip(z, 1), flip(z, 2)
    z3 = flip(z2, 1)
    q = jnp.where(native, z, z2)
    dc, dx, dy = flip(d, 1), flip(d, 2), flip(d, 4)
    dd = flip(dx, 4)
    C, Zp, Fz, F3, CF, CF3 = (dc, z), (d, z1), (d, z2), (d, z3), (dc, z2), (dc, z3)
    X, Y, XY = (dx, z), (dy, z), (dd, z)
    plane = ((X, dx // 2), (Y, dy // 2), (XY, dd // 2))
    MESH = pl.DeviceIdType.MESH
    barrier = pltpu.get_barrier_semaphore()
    all_peers = (C, Zp, Fz, F3, CF, CF3, X, Y, XY)
    for peer in all_peers:
        pl.semaphore_signal(barrier, inc=1, device_id=peer, device_id_type=MESH)
    pl.semaphore_wait(barrier, len(all_peers))

    counter = [0, 0]
    drains = []

    def remote(src, dst, dev, when=None):
        i = counter[0]
        counter[0] += 1
        copy = pltpu.make_async_remote_copy(
            src_ref=src, dst_ref=dst, send_sem=ssem.at[i], recv_sem=rsem.at[i],
            device_id=dev, device_id_type=MESH,
        )
        drains.append((copy, when))
        return copy

    def local(src, dst):
        i = counter[1]
        counter[1] += 1
        return pltpu.make_async_copy(src, dst, lsem.at[i])

    rc_tok = remote(tok, T_, C, "n")
    rc_len = remote(lens, len_, C, "n")
    rc_cot = remote(cot, G_, C, "n")
    rc_qb = remote(qb, qb_, Fz, "n")
    weights = {}

    def weight(name, src, dst, size, lead):
        def at(ref, k):
            rows = ds(k * size, size)
            return ref.at[:, rows, :] if lead else ref.at[rows, :]

        first = remote(at(src, chip), at(dst, chip), Fz, "n")
        spread = [remote(at(dst, chip), at(dst, chip), dev, "f") for dev, _ in plane]
        weights[name] = (first, spread, local(src, dst))

    weight("si", w_si, si, 192, True)
    weight("ck", w_ck, ck, 192, True)
    weight("cq", w_cq, cq, 192, False)
    weight("so", w_so, so, 48, False)
    weight("co", w_co, co, 48, False)
    weight("mo", w_mo, mo, 192, False)
    weight("mi", w_mi, mi, 192, False)
    lc_tok, lc_cot, lc_len, lc_qb = local(tok, T_), local(cot, G_), local(lens, len_), local(qb, qb_)
    rc_mem = remote(mem, slab.at[z], Fz, "f")
    lc_mem = local(mem, slab.at[z])
    rc_mz0 = remote(slab.at[z], slab.at[z], Zp, "n")
    rc_mz2 = remote(slab.at[z2], slab.at[z2], Zp, "n")
    rc_mc = [remote(slab.at[zz], slab.at[zz], C, "n") for zz in (z, z2, z1, z3)]

    def spread_weight(name):
        first, spread, loc = weights[name]
        first.wait_recv()
        for copy in spread:
            copy.start()

    def need_weight(name):
        first, spread, loc = weights[name]

        @pl.when(native)
        def _():
            loc.wait()

        @pl.when(foreign)
        def _():
            for copy in spread:
                copy.wait_recv()

    @pl.when(native)
    def _():
        rc_tok.start()
        rc_len.start()
        weights["si"][0].start()
        rc_qb.start()
        weights["si"][2].start()
        lc_tok.start()
        lc_len.start()
        lc_qb.start()
        lc_mem.start()
        for name in ("ck", "cq", "so", "co"):
            weights[name][0].start()
            weights[name][2].start()
        rc_cot.start()
        lc_cot.start()
        weights["mo"][2].start()
        weights["mi"][2].start()
        lc_mem.wait()
        rc_mz0.start()
        rc_mc[0].start()
        lc_tok.wait()
        lc_len.wait()
        lc_qb.wait()

    @pl.when(foreign)
    def _():
        rc_mem.start()
        rc_tok.wait_recv()
        rc_len.wait_recv()

    def normed(values):
        average = jnp.mean(values, axis=-1, keepdims=True)
        centred = values - average
        variance = jnp.mean(centred * centred, axis=-1, keepdims=True)
        inv = lax.rsqrt(variance + 1e-05)
        return centred * inv, inv

    def loop(count, fn):
        def step(i, carry):
            fn(i)
            return carry

        lax.fori_loop(0, count, step, 0)

    gain = lambda i: rep[i : i + 1, :]
    shift = lambda i: rep[3 + i : 4 + i, :]

    def ln0(i):
        rows = ds(i * RB, RB)
        n, _ = normed(T_[rows, :].astype(F32))
        x1[rows, :] = (n * gain(0) + shift(0)).astype(BF)

    loop(T // RB, ln0)

    @pl.when(foreign)
    def _():
        spread_weight("si")
        rc_qb.wait_recv()

    need_weight("si")

    def heads_to(ref, rows, values):
        for h in range(NH):
            ref[h, rows, :] = values[:, h * HD : (h + 1) * HD].astype(BF)

    def qkv(i):
        rows = ds(i * RB, RB)
        x = x1[rows, :]
        heads_to(q_, rows, nn(x, si[0]) + qb_[0:1, 0:HW])
        heads_to(k_, rows, nn(x, si[1]))
        heads_to(v_, rows, nn(x, si[2]) + qb_[1:2, 0:HW])

    loop(T // RB, qkv)

    @pl.when(foreign)
    def _():
        for name in ("ck", "cq", "so", "co"):
            spread_weight(name)

    @pl.when(native)
    def _():
        rc_mem.wait_recv()
        rc_mz2.start()
        rc_mc[1].start()

    length = len_[0:1, 0:1]

    def row_ids(start):
        return (start + lax.broadcasted_iota(jnp.int32, (AB, 1), 0)).astype(F32)

    self_cols = lax.broadcasted_iota(jnp.int32, (1, TA), 1).astype(F32)

    def self_fwd(i):
        start = i * AB
        rows = ds(start, AB)
        ids = row_ids(start)
        valid = ids < length
        allowed = (self_cols <= ids) & valid
        outs = []
        for h in range(NH):
            s = nt(q_[h, rows, :], k_[h, 0:TA, :]) * 0.125
            s = jnp.where(allowed, s, -1000000000.0)
            e = jnp.exp(s - jnp.max(s, axis=-1, keepdims=True))
            pb = (e * (1.0 / jnp.sum(e, axis=-1, keepdims=True))).astype(BF)
            ps_[h, rows, :] = pb
            outs.append(nn(pb, v_[h, 0:TA, :]))
        att = jnp.where(valid, jnp.concatenate(outs, axis=1), 0.0)
        satt[rows, :] = att.astype(BF)

    satt[TA:T, :] = jnp.zeros((T - TA, HW), BF)
    catt[TA:T, :] = jnp.zeros((T - TA, HW), BF)
    gcq[TA:T, :] = jnp.zeros((T - TA, HW), BF)
    gqkv[TA:T, :] = jnp.zeros((T - TA, 3 * HW), BF)
    loop(TA // AB, self_fwd)

    mine, other = c * (T // 2), (1 - c) * (T // 2)
    slots = {}

    def sum_start(k, block):
        for copy in slots.get(k, ()):
            copy.wait_send()
            drains[:] = [item for item in drains if item[0] is not copy]
        to_core = [remote(pS.at[k, j], pR.at[k, j], C) for j in range(2)]
        to_chip = [remote(zS.at[k, j], zR.at[k, j], Zp) for j in range(2)]
        for j in range(2):
            pS[k, j] = block(other + j * RB).astype(BF)
            to_core[j].start()
        for j in range(2):
            own = block(mine + j * RB)
            to_core[j].wait_recv()
            zS[k, j] = (own + pR[k, j].astype(F32)).astype(BF)
            to_chip[j].start()
        slots[k] = to_core + to_chip
        return to_chip

    def sum_take(k, to_chip, j):
        to_chip[j].wait_recv()
        return zS[k, j].astype(F32) + zR[k, j].astype(F32)

    def share(ref):
        own = ds(mine, T // 2)
        copy = remote(ref.at[own, :], ref.at[own, :], C)
        return copy

    need_weight("so")
    ar1 = sum_start(0, lambda start: nn(satt[ds(start, RB), :], so[...]))

    @pl.when(native)
    def _():
        weights["mo"][0].start()
        weights["mi"][0].start()

    need_weight("ck")

    def project(zz):
        def part(i):
            rows = ds(i * RB, RB)
            out = ds(zz * FP + i * RB, RB)
            m = slab[zz, rows, :]
            heads_to(K_, out, nn(m, ck[0]))
            heads_to(V_, out, nn(m, ck[1]) + qb_[3:4, 0:HW])

        loop(FP // RB, part)

    for slot, zz in enumerate((z, z2, z1, z3)):
        @pl.when(native)
        def _():
            if slot == 2:
                rc_mz0.wait_recv()
                rc_mc[2].start()
            if slot == 3:
                rc_mz2.wait_recv()
                rc_mc[3].start()

        @pl.when(foreign)
        def _():
            rc_mc[slot].wait_recv()

        project(zz)

    need_weight("cq")
    share_x2 = share(x2)
    for j in range(2):
        own = ds(mine + j * RB, RB)
        local_rows = slice(j * RB, (j + 1) * RB)
        value = T_[own, :].astype(F32) + sum_take(0, ar1, j) + rep[6:7, :]
        m1[local_rows, :] = value
        n, _ = normed(value)
        x2[own, :] = (n * gain(1) + shift(1)).astype(BF)
    share_x2.start()

    def cross_q(half):
        def part(i):
            rows = ds(half + i * RB, RB)
            heads_to(cq_, rows, nn(x2[rows, :], cq[...]) + qb_[2:3, 0:HW])

        loop(2, part)

    cross_q(mine)
    share_x2.wait_recv()
    cross_q(other)

    frame = lax.broadcasted_iota(jnp.int32, (1, FT), 1)
    frame_ok = lax.rem(frame, FP) < FQ

    def cross_fwd(i):
        start = i * AB
        rows = ds(start, AB)
        valid = row_ids(start) < length
        outs = []
        for h in range(NH):
            s = nt(cq_[h, rows, :], K_[h]) * 0.125
            s = jnp.where(frame_ok, s, -3e38)
            e = jnp.exp(s - jnp.max(s, axis=-1, keepdims=True))
            pb = (e * (1.0 / jnp.sum(e, axis=-1, keepdims=True))).astype(BF)
            pc_[h, rows, :] = pb
            outs.append(nn(pb, V_[h]))
        att = jnp.where(valid, jnp.concatenate(outs, axis=1), 0.0)
        catt[rows, :] = att.astype(BF)

    loop(TA // AB, cross_fwd)
    need_weight("co")
    ar2 = sum_start(1, lambda start: nn(catt[ds(start, RB), :], co[...]))

    @pl.when(native)
    def _():
        lc_cot.wait()

    @pl.when(foreign)
    def _():
        rc_cot.wait_recv()
        spread_weight("mo")
        spread_weight("mi")

    need_weight("mo")

    def grad_active(i):
        rows = ds(i * RB, RB)
        fin[rows, :] = nt(G_[rows, :], mo[...])

    loop(T // RB, grad_active)
    share_x3 = share(x3)
    for j in range(2):
        own = ds(mine + j * RB, RB)
        local_rows = slice(j * RB, (j + 1) * RB)
        value = m1[local_rows, :] + sum_take(1, ar2, j) + rep[7:8, :]
        m2[local_rows, :] = value
        n, _ = normed(value)
        x3[own, :] = (n * gain(2) + shift(2)).astype(BF)
    share_x3.start()
    need_weight("mi")

    def mlp(half):
        def part(i):
            rows = ds(half + i * RB, RB)
            hidden = nn(x3[rows, :], mi[...]) + qb_[4:5, :]
            phi = 0.5 * (1.0 + lax.erf(hidden * (0.5**0.5)))
            density = jnp.exp(-0.5 * hidden * hidden) * (1.0 / math.sqrt(2.0 * math.pi))
            act[rows, :] = (hidden * phi).astype(BF)
            gh[rows, :] = (fin[rows, :] * (phi + hidden * density)).astype(BF)

        loop(2, part)

    mlp(mine)
    share_x3.wait_recv()
    mlp(other)
    ar3 = sum_start(0, lambda start: nt(gh[ds(start, RB), :], mi[...]))
    arm = sum_start(2, lambda start: nn(act[ds(start, RB), :], mo[...]))

    gsends = {}

    def plane_send(m):
        gsends[m] = [
            remote(gb.at[m, ds(kk * 192, 192), :], gR.at[m, s], dev)
            for s, (dev, kk) in enumerate(plane)
        ]
        for copy in gsends[m]:
            copy.start()

    def grad_mi(i):
        cols = slice(i * 256, (i + 1) * 256)
        gb[0, cols, :] = tn(x3[:, cols], gh[...]).astype(BF)

    def grad_mo(i):
        cols = slice(i * 256, (i + 1) * 256)
        gb[1, cols, :] = tn(G_[:, cols], act[...]).astype(BF)

    for i in range(3):
        grad_mi(i)
    plane_send(0)

    def colsum(values):
        return jnp.sum(values, axis=0, keepdims=True)

    mi_bias = colsum(gh[...].astype(F32))
    zero_row = jnp.zeros((1, D), F32)
    g_gain, g_shift = [zero_row] * 3, [zero_row] * 3
    b_out = [zero_row] * 3

    def norm_back(i, value, upstream, gi):
        n, inv = normed(value)
        a = upstream * gain(gi)
        g_gain[gi] = g_gain[gi] + colsum(upstream * n)
        g_shift[gi] = g_shift[gi] + colsum(upstream)
        return inv * (a - jnp.mean(a, axis=-1, keepdims=True) - n * jnp.mean(a * n, axis=-1, keepdims=True))

    share_ups = share(ups)
    for j in range(2):
        own = ds(mine + j * RB, RB)
        local_rows = slice(j * RB, (j + 1) * RB)
        g = G_[own, :].astype(F32)
        b_out[2] = b_out[2] + colsum(g)
        value = g + norm_back(j, m2[local_rows, :], sum_take(0, ar3, j), 2)
        low = value.astype(BF)
        b_out[1] = b_out[1] + colsum(low.astype(F32))
        ups[own, :] = low
        fin[local_rows, :] = value
    share_ups.start()

    def cross_dO(half, count, size):
        def part(i):
            start = half + i * size
            rows = ds(start, size)
            values = nt(ups[rows, :], co[...])
            ids = (start + lax.broadcasted_iota(jnp.int32, (size, 1), 0)).astype(F32)
            heads_to(dO, rows, jnp.where(ids < length, values, 0.0))

        loop(count, part)

    cross_dO(mine, 2, RB)
    share_ups.wait_recv()
    cross_dO(other, 2, RB)

    def cross_bwd(i):
        rows = ds(i * AB, AB)
        outs = []
        for h in range(NH):
            dp_ = nt(dO[h, rows, :], V_[h])
            pr = pc_[h, rows, :].astype(F32)
            dsv = (pr * (dp_ - jnp.sum(pr * dp_, axis=-1, keepdims=True))).astype(BF)
            dsb[h, rows, :] = dsv
            outs.append(nn(dsv, K_[h]) * 0.125)
        gcq[rows, :] = jnp.concatenate(outs, axis=1).astype(BF)

    loop(TA // AB, cross_bwd)
    ar4 = sum_start(1, lambda start: nt(gcq[ds(start, RB), :], cq[...]))

    def kv_grad(i):
        rows = ds(i * FP, FP)
        ks = [tn(dsb[h, :, ds(i * FP, FP, 128)], cq_[h, 0:TA, :]) * 0.125 for h in range(NH)]
        vs = [tn(pc_[h, :, ds(i * FP, FP, 128)], dO[h, 0:TA, :]) for h in range(NH)]
        gkv[0, rows, :] = jnp.concatenate(ks, axis=1).astype(BF)
        gkv[1, rows, :] = jnp.concatenate(vs, axis=1).astype(BF)

    loop(4, kv_grad)

    share_upo = share(upo)
    for j in range(2):
        own = ds(mine + j * RB, RB)
        local_rows = slice(j * RB, (j + 1) * RB)
        value = fin[local_rows, :] + norm_back(j, m1[local_rows, :], sum_take(1, ar4, j), 1)
        low = value.astype(BF)
        b_out[0] = b_out[0] + colsum(low.astype(F32))
        upo[own, :] = low
        fin[T // 2 + j * RB : T // 2 + (j + 1) * RB, :] = value
    share_upo.start()

    def mem_term(zz):
        rows = ds(zz * FP, FP)
        return nt(gkv[0, rows, :], ck[0]) + nt(gkv[1, rows, :], ck[1])

    q1, q2 = flip(q, 1), flip(q, 2)
    q3 = flip(q2, 1)
    mt_core = [remote(mtS.at[j], mtR.at[j], C) for j in range(2)]
    mt_chip = remote(mtZ, mtZr, Zp)
    mt_out = remote(mtF, mgrad_o, CF, "f")
    for j, zz in enumerate((q2, q3)):
        mtS[j] = mem_term(zz).astype(BF)
        mt_core[j].start()

    def self_dO(half):
        def part(i):
            start = half + i * RB
            rows = ds(start, RB)
            values = nt(upo[rows, :], so[...])
            ids = (start + lax.broadcasted_iota(jnp.int32, (RB, 1), 0)).astype(F32)
            heads_to(dOs, rows, jnp.where(ids < length, values, 0.0))

        loop(2, part)

    self_dO(mine)
    share_upo.wait_recv()
    self_dO(other)

    def self_bwd(i):
        rows = ds(i * AB, AB)
        outs = []
        for h in range(NH):
            dp_ = nt(dOs[h, rows, :], v_[h, 0:TA, :])
            pr = ps_[h, rows, :].astype(F32)
            dsv = (pr * (dp_ - jnp.sum(pr * dp_, axis=-1, keepdims=True))).astype(BF)
            dsb[h, rows, 0:TA] = dsv
            outs.append(nn(dsv, k_[h, 0:TA, :]) * 0.125)
        gqkv[rows, 0:HW] = jnp.concatenate(outs, axis=1).astype(BF)

    loop(TA // AB, self_bwd)
    kv = [tn(dsb[h, :, 0:TA], q_[h, 0:TA, :]) * 0.125 for h in range(NH)]
    kv += [tn(ps_[h], dOs[h, 0:TA, :]) for h in range(NH)]
    gqkv[0:TA, HW:] = jnp.concatenate(kv, axis=1).astype(BF)

    def first_term(start):
        rows = ds(start, RB)
        x = gqkv[rows, :]
        return nt(x[:, 0:HW], si[0]) + nt(x[:, HW : 2 * HW], si[1]) + nt(x[:, 2 * HW :], si[2])

    ar5 = sum_start(0, first_term)

    for i in range(3):
        grad_mo(i)
    plane_send(1)
    for i in range(3):
        cols = slice(i * 256, (i + 1) * 256)
        left = tn(x1[:, cols], gqkv[...])
        right = tn(upo[:, cols], satt[...])
        gb[3, cols, :] = jnp.concatenate([left, right], axis=1).astype(BF)
    plane_send(3)
    for i in range(3):
        cols = slice(i * 256, (i + 1) * 256)
        a = tn(x2[:, cols], gcq[...])
        b = sum(tn(slab[s, :, cols], gkv[0, s * FP : (s + 1) * FP, :]) for s in range(4))
        e = sum(tn(slab[s, :, cols], gkv[1, s * FP : (s + 1) * FP, :]) for s in range(4))
        f = tn(ups[:, cols], catt[...])
        gb[2, cols, :] = jnp.concatenate([a, b, e, f], axis=1).astype(BF)
    plane_send(2)

    own_term = mem_term(q)
    next_term = mem_term(q1)
    mt_core[1].wait_recv()
    mtZ[...] = (next_term + mtR[1].astype(F32)).astype(BF)
    mt_chip.start()
    mt_core[0].wait_recv()
    own_term = own_term + mtR[0].astype(F32)
    mt_chip.wait_recv()
    mtF[...] = (own_term + mtZr[...].astype(F32)).astype(BF)

    @pl.when(native)
    def _():
        mgrad_o[...] = mtF[...]

    @pl.when(foreign)
    def _():
        mt_out.start()

    block = lax.rem(z, 2)
    outs = []

    def give(slot, out_ref, stage):
        own = ds(mine, T // 2)
        rows = ds(mine + block * RB, RB)
        src = stage.at[slot, ds(block * RB, RB), :]
        from_n = [remote(src, out_ref.at[rows, :], dev, "n") for dev in (Fz, F3)]
        from_f = [remote(src, out_ref.at[rows, :], dev, "f") for dev in (CF, CF3)]
        to_core = remote(stage.at[slot], out_ref.at[own, :], C, "f")

        @pl.when(native)
        def _():
            for copy in from_n:
                copy.start()
            out_ref[own, :] = stage[slot]

        @pl.when(foreign)
        def _():
            to_core.start()
            for copy in from_f:
                copy.start()

        outs.append((from_n, from_f, to_core))

    for j in range(2):
        local_rows = slice(j * RB, (j + 1) * RB)
        value = m2[local_rows, :] + sum_take(2, arm, j) + rep[8:9, :]
        gO[0, local_rows, :] = value.astype(BF)
    give(0, mixed_o, gO)

    for j in range(2):
        own = ds(mine + j * RB, RB)
        local_rows = slice(j * RB, (j + 1) * RB)
        value = fin[T // 2 + j * RB : T // 2 + (j + 1) * RB, :] + norm_back(j, T_[own, :].astype(F32), sum_take(0, ar5, j), 0)
        gO[1, local_rows, :] = value.astype(BF)
    give(1, igrad_o, gO)

    gs = gqkv[...].astype(F32)
    quarter = jnp.concatenate(
        [
            colsum(gs[:, 0:HW]),
            colsum(gs[:, 2 * HW :]),
            colsum(gcq[...].astype(F32)),
            colsum(gkv[1].astype(F32)),
        ],
        axis=1,
    )
    row = lax.broadcasted_iota(jnp.int32, (24, 1), 0)
    packed = jnp.zeros((24, D), F32)
    full_rows = g_gain + g_shift + b_out
    for i, values in enumerate(full_rows):
        packed = packed + jnp.where(row == i, values * 0.5, 0.0)
    packed = packed + jnp.where(row == 9 + q, quarter, 0.0) + jnp.where(row == 13 + q, mi_bias, 0.0)
    sb[0] = packed
    for i, dev in enumerate((C, Zp, Fz, X, Y)):
        copy = remote(sb.at[i], sR.at[i], dev)
        copy.start()
        copy.wait_recv()
        sb[i + 1] = sb[i] + sR[i]
    total = sb[5]
    small_o[0:9, :] = total[0:9, :]
    small_o[9:10, :] = colsum(jnp.where(row == 9 + z, total, 0.0))
    small_o[10:11, :] = colsum(jnp.where(row == 13 + z, total, 0.0))
    small_o[11:16, :] = jnp.zeros((5, D), F32)

    finals = {}
    own_piece = ds(chip * 192, 192)
    for m in (0, 1, 3, 2):
        finals[m] = (
            remote(gb.at[m, own_piece, :], gFr.at[m], Fz, "f"),
            remote(gC.at[m], grads_o.at[m], C, "n"),
        )

    def piece_sum(m):
        piece = gb[m, own_piece, :].astype(F32)
        for s in range(3):
            gsends[m][s].wait_recv()
            piece = piece + gR[m, s].astype(F32)
        return piece

    @pl.when(foreign)
    def _():
        for m in (0, 1, 3, 2):
            gb[m, own_piece, :] = piece_sum(m).astype(BF)
            finals[m][0].start()

    @pl.when(native)
    def _():
        for m in (0, 1, 3, 2):
            piece = piece_sum(m)
            finals[m][0].wait_recv()
            both = piece + gFr[m].astype(F32)
            gC[m] = jnp.where(c == 0, both[96:192, :], both[0:96, :])
            finals[m][1].start()
            grads_o[m] = jnp.where(c == 0, both[0:96, :], both[96:192, :])

    @pl.when(foreign)
    def _():
        for m in (0, 1, 3, 2):
            finals[m][1].wait_recv()
        mt_out.wait_recv()
        for from_n, from_f, to_core in outs:
            for copy in from_n + from_f:
                copy.wait_recv()

    @pl.when(native)
    def _():
        for from_n, from_f, to_core in outs:
            to_core.wait_recv()

    for copy, when in drains:
        if when is None:
            copy.wait_send()

    @pl.when(native)
    def _():
        for copy, when in drains:
            if when == "n":
                copy.wait_send()

    @pl.when(foreign)
    def _():
        for copy, when in drains:
            if when == "f":
                copy.wait_send()


def fused(
    tokens, memory, lengths, cotangent, ln_gain, ln_bias, self_in, self_bias, self_out,
    self_out_bias, cross_q, cross_kv, cross_bias, cross_out, cross_out_bias, mlp_in,
    mlp_in_bias, mlp_out, mlp_out_bias,
):
    lens = jnp.broadcast_to(lengths.astype(F32)[:, None], (8, 128))
    row = lambda v: v.astype(F32)[None, :]
    rep = jnp.concatenate(
        [ln_gain, ln_bias, row(self_out_bias), row(cross_out_bias), row(mlp_out_bias), jnp.zeros((7, D), F32)]
    )
    four = jnp.pad(jnp.concatenate([self_bias, cross_bias]).astype(F32), ((0, 0), (0, D - HW)))
    qb = jnp.concatenate([four, row(mlp_in_bias), jnp.zeros((3, D), F32)])
    mem = jnp.pad(memory[0], ((0, FP - FQ), (0, 0)))
    vmem = pltpu.VMEM
    half = T // 2
    scratch = [
        vmem((T, D), BF), vmem((T, D), BF), vmem((8, 128), F32), vmem((8, D), F32),
        vmem((3, D, HW), BF), vmem((HW, D), BF), vmem((D, HW), BF), vmem((2, D, HW), BF), vmem((HW, D), BF),
        vmem((D, D), BF), vmem((D, D), BF), vmem((4, FP, D), BF),
        vmem((T, D), BF), vmem((NH, T, HD), BF), vmem((NH, T, HD), BF), vmem((NH, T, HD), BF),
        vmem((NH, TA, TA), BF), vmem((T, HW), BF), vmem((half, D), F32), vmem((T, D), BF),
        vmem((NH, T, HD), BF), vmem((NH, FT, HD), BF), vmem((NH, FT, HD), BF), vmem((NH, TA, FT), BF),
        vmem((T, HW), BF), vmem((half, D), F32), vmem((T, D), BF), vmem((T, D), BF), vmem((T, D), BF),
        vmem((T, D), BF), vmem((NH, T, HD), BF), vmem((NH, TA, FT), BF), vmem((2, FT, HW), BF),
        vmem((T, HW), BF), vmem((T, D), BF), vmem((NH, T, HD), BF), vmem((T, 3 * HW), BF),
        vmem((3, 2, RB, D), BF), vmem((3, 2, RB, D), BF), vmem((3, 2, RB, D), BF), vmem((3, 2, RB, D), BF),
        vmem((T, D), F32),
        vmem((2, FP, D), BF), vmem((2, FP, D), BF), vmem((FP, D), BF), vmem((FP, D), BF), vmem((FP, D), BF),
        vmem((4, D, D), BF), vmem((4, 3, 192, D), BF), vmem((4, 192, D), BF), vmem((4, 96, D), F32),
        vmem((2, half, D), BF), vmem((6, 24, D), F32), vmem((5, 24, D), F32),
        pltpu.SemaphoreType.DMA((16,)), pltpu.SemaphoreType.DMA((150,)), pltpu.SemaphoreType.DMA((150,)),
    ]
    hbm = pl.BlockSpec(memory_space=pl.ANY)
    on_chip = pl.BlockSpec(memory_space=pltpu.VMEM)
    mixed, igrad, mgrad, grads, small = pl.pallas_call(
        layer_kernel,
        out_shape=[
            jax.ShapeDtypeStruct((T, D), BF),
            jax.ShapeDtypeStruct((T, D), BF),
            jax.ShapeDtypeStruct((FP, D), BF),
            jax.ShapeDtypeStruct((4, 96, D), F32),
            jax.ShapeDtypeStruct((16, D), F32),
        ],
        in_specs=[hbm] * 4 + [on_chip] + [hbm] * 8,
        out_specs=[on_chip] * 5,
        scratch_shapes=scratch,
        compiler_params=pltpu.CompilerParams(
            collective_id=0, has_side_effects=True, vmem_limit_bytes=VMEM_LIMIT
        ),
    )(tokens, mem, lens, cotangent, rep, qb, self_in, self_out, cross_q, cross_kv, cross_out, mlp_in, mlp_out)
    g_mi, g_mo, g_cross, g_self = grads[0], grads[1], grads[2], grads[3]
    cut = lambda a, i: a[:, i * HW : (i + 1) * HW]
    quarter = small[9].reshape(4, HW)
    return (
        mixed,
        igrad,
        mgrad[None, :FQ],
        small[0:3],
        small[3:6],
        jnp.stack([cut(g_self, 0), cut(g_self, 1), cut(g_self, 2)]),
        quarter[0:2],
        cut(g_self, 3).T,
        small[6],
        cut(g_cross, 0),
        jnp.stack([cut(g_cross, 1), cut(g_cross, 2)]),
        quarter[2:4],
        cut(g_cross, 3).T,
        small[7],
        g_mi,
        small[10],
        g_mo.T,
        small[8],
    )


def matmul(left, right):
    return jnp.dot(left, right, preferred_element_type=jnp.float32)


def einsum_f(form, left, right):
    return jnp.einsum(form, left, right, preferred_element_type=jnp.float32)


def norm_parts(values):
    average = jnp.mean(values, axis=-1, keepdims=True)
    centred = values - average
    variance = jnp.mean(centred * centred, axis=-1, keepdims=True)
    scale_inv = lax.rsqrt(variance + 1e-05)
    return (centred * scale_inv, scale_inv)


def norm_back(normed, scale_inv, gain, upstream):
    scaled = upstream * gain
    inner = (
        scaled
        - jnp.mean(scaled, axis=-1, keepdims=True)
        - normed * jnp.mean(scaled * normed, axis=-1, keepdims=True)
    )
    return (scale_inv * inner, jnp.sum(upstream * normed, axis=0), jnp.sum(upstream, axis=0))


def softmax_parts(scores):
    row_max = jnp.max(scores, axis=-1, keepdims=True)
    shifted = jnp.exp(scores - row_max)
    totals = jnp.sum(shifted, axis=-1, keepdims=True)
    return (shifted / totals, row_max[..., 0] + jnp.log(totals[..., 0]))


def gelu_exact(values):
    return jax.nn.gelu(values, approximate=False)


def self_forward(queries, keys_self, values_self, allowed, valid_mask):
    row_count, head_width = queries.shape
    head_count = head_width // HD
    query_heads = queries.reshape(row_count, head_count, HD)
    key_heads = keys_self.reshape(row_count, head_count, HD)
    value_heads = values_self.reshape(row_count, head_count, HD)
    scores = einsum_f("thd,shd->hts", query_heads, key_heads) * 0.125
    scores = jnp.where(allowed[None], scores, -1000000000.0)
    probs, log_total = softmax_parts(scores)
    attended = einsum_f("hts,shd->thd", probs.astype(jnp.bfloat16), value_heads).reshape(
        row_count, head_width
    )
    attended = jnp.where(valid_mask, attended, 0.0)
    return (attended.astype(jnp.bfloat16), log_total)


def self_backward(queries, keys_self, values_self, allowed, log_total, grad_out):
    row_count, head_width = queries.shape
    head_count = head_width // HD
    query_heads = queries.reshape(row_count, head_count, HD)
    key_heads = keys_self.reshape(row_count, head_count, HD)
    value_heads = values_self.reshape(row_count, head_count, HD)
    scores = einsum_f("thd,shd->hts", query_heads, key_heads) * 0.125
    scores = jnp.where(allowed[None], scores, -1000000000.0)
    probs = jnp.exp(scores - log_total[..., None])
    grad_heads = grad_out.reshape(row_count, head_count, HD)
    grad_values = einsum_f("hts,thd->shd", probs.astype(jnp.bfloat16), grad_heads)
    grad_probs = einsum_f("thd,shd->hts", grad_heads, value_heads)
    grad_scores = (
        probs * (grad_probs - jnp.sum(probs * grad_probs, axis=-1, keepdims=True))
    ).astype(jnp.bfloat16)
    grad_queries = einsum_f("hts,shd->thd", grad_scores, key_heads) * 0.125
    grad_keys = einsum_f("hts,thd->shd", grad_scores, query_heads) * 0.125
    return (
        grad_queries.reshape(row_count, head_width).astype(jnp.bfloat16),
        grad_keys.reshape(row_count, head_width).astype(jnp.bfloat16),
        grad_values.reshape(row_count, head_width).astype(jnp.bfloat16),
    )


def cross_forward(query_heads, memory_pairs, clip_of):
    row_count, head_count, _ = query_heads.shape
    head_width = head_count * HD
    clip_count = memory_pairs.shape[0]

    def per_clip(carry, clip_item):
        attended, log_rows = carry
        clip_index, clip_pairs = clip_item
        key_heads = clip_pairs[:, :head_width].reshape(-1, head_count, HD)
        value_heads = clip_pairs[:, head_width:].reshape(-1, head_count, HD)
        scores = einsum_f("thd,fhd->htf", query_heads, key_heads) * 0.125
        probs, log_total = softmax_parts(scores)
        result = einsum_f("htf,fhd->thd", probs.astype(jnp.bfloat16), value_heads).reshape(
            row_count, head_width
        )
        member = clip_of == clip_index
        return (
            (
                jnp.where(member[:, None], result, attended),
                jnp.where(member[None, :], log_total, log_rows),
            ),
            None,
        )

    start_carry = (
        jnp.zeros((row_count, head_width), jnp.float32),
        jnp.zeros((head_count, row_count), jnp.float32),
    )
    (attended, log_rows), _ = lax.scan(
        per_clip, start_carry, (jnp.arange(clip_count, dtype=jnp.int32), memory_pairs)
    )
    return (attended.astype(jnp.bfloat16), log_rows)


def cross_backward(query_heads, memory_pairs, clip_of, log_rows, grad_out):
    row_count, head_count, _ = query_heads.shape
    head_width = head_count * HD
    clip_count = memory_pairs.shape[0]

    def per_clip(grad_query, clip_item):
        clip_index, clip_pairs = clip_item
        frames = clip_pairs.shape[0]
        member = clip_of == clip_index
        key_heads = clip_pairs[:, :head_width].reshape(frames, head_count, HD)
        value_heads = clip_pairs[:, head_width:].reshape(frames, head_count, HD)
        scores = einsum_f("thd,fhd->htf", query_heads, key_heads) * 0.125
        probs = jnp.where(member[None, :, None], jnp.exp(scores - log_rows[:, :, None]), 0.0)
        grad_heads = jnp.where(member[:, None], grad_out, jnp.zeros_like(grad_out)).reshape(
            row_count, head_count, HD
        )
        grad_values = einsum_f("htf,thd->fhd", probs.astype(jnp.bfloat16), grad_heads)
        grad_probs = einsum_f("thd,fhd->htf", grad_heads, value_heads)
        grad_scores = (
            probs * (grad_probs - jnp.sum(probs * grad_probs, axis=-1, keepdims=True))
        ).astype(jnp.bfloat16)
        grad_query = grad_query + einsum_f("htf,fhd->thd", grad_scores, key_heads) * 0.125
        grad_keys = einsum_f("htf,thd->fhd", grad_scores, query_heads) * 0.125
        grad_pairs = jnp.concatenate(
            [grad_keys.reshape(frames, head_width), grad_values.reshape(frames, head_width)], axis=1
        )
        return (grad_query, grad_pairs.astype(jnp.bfloat16))

    grad_query, grad_pairs = lax.scan(
        per_clip,
        jnp.zeros((row_count, head_count, HD), jnp.float32),
        (jnp.arange(clip_count, dtype=jnp.int32), memory_pairs),
    )
    return (grad_query.reshape(row_count, head_width).astype(jnp.bfloat16), grad_pairs)


def body(
    tokens,
    memory,
    lengths,
    cotangent,
    ln_gain,
    ln_bias,
    self_in,
    self_bias,
    self_out,
    self_out_bias,
    cross_q,
    cross_kv,
    cross_bias,
    cross_out,
    cross_out_bias,
    mlp_in,
    mlp_in_bias,
    mlp_out,
    mlp_out_bias,
):
    row_count = tokens.shape[0]
    clip_count = lengths.shape[0]
    head_width = self_in.shape[2]
    head_count = head_width // HD
    clip_ends = jnp.cumsum(lengths)
    positions = jnp.arange(row_count, dtype=jnp.int32)
    clip_of = jnp.sum((positions[:, None] >= clip_ends[None, :]).astype(jnp.int32), axis=1)
    valid_mask = (clip_of < clip_count)[:, None]
    allowed = (
        (clip_of[:, None] == clip_of[None, :])
        & (positions[None, :] <= positions[:, None])
        & (clip_of[:, None] < clip_count)
    )
    inputs = tokens.astype(jnp.float32)
    normed_one, scale_one = norm_parts(inputs)
    first_in = (normed_one * ln_gain[0] + ln_bias[0]).astype(jnp.bfloat16)
    queries = (matmul(first_in, self_in[0]) + self_bias[0]).astype(jnp.bfloat16)
    keys_self = matmul(first_in, self_in[1]).astype(jnp.bfloat16)
    values_self = (matmul(first_in, self_in[2]) + self_bias[1]).astype(jnp.bfloat16)
    self_att, log_self = self_forward(queries, keys_self, values_self, allowed, valid_mask)
    mixed_one = inputs + lax.psum(matmul(self_att, self_out), "mp") + self_out_bias
    normed_two, scale_two = norm_parts(mixed_one)
    second_in = (normed_two * ln_gain[1] + ln_bias[1]).astype(jnp.bfloat16)
    cross_queries = (matmul(second_in, cross_q) + cross_bias[0]).astype(jnp.bfloat16)
    slab = lax.all_gather(memory, "mp", axis=1, tiled=True)
    slab_keys = einsum_f("cfd,de->cfe", slab, cross_kv[0]).astype(jnp.bfloat16)
    slab_values = (einsum_f("cfd,de->cfe", slab, cross_kv[1]) + cross_bias[1]).astype(jnp.bfloat16)
    memory_pairs = jnp.concatenate([slab_keys, slab_values], axis=2)
    query_heads = cross_queries.reshape(row_count, head_count, HD)
    cross_att, log_cross = cross_forward(query_heads, memory_pairs, clip_of)
    mixed_two = (
        mixed_one
        + lax.psum(matmul(cross_att, cross_out).astype(jnp.bfloat16), "mp").astype(jnp.float32)
        + cross_out_bias
    )
    normed_three, scale_three = norm_parts(mixed_two)
    third_in = (normed_three * ln_gain[2] + ln_bias[2]).astype(jnp.bfloat16)
    hidden = matmul(third_in, mlp_in) + mlp_in_bias
    active, gelu_back = jax.vjp(gelu_exact, hidden)
    active_low = active.astype(jnp.bfloat16)
    mixed = (
        mixed_two
        + lax.psum(matmul(active_low, mlp_out).astype(jnp.bfloat16), "mp").astype(jnp.float32)
        + mlp_out_bias
    ).astype(jnp.bfloat16)
    upstream = cotangent.astype(jnp.float32)
    grad_mlp_out = einsum_f("tf,td->fd", active_low, cotangent)
    grad_mlp_out_bias = jnp.sum(upstream, axis=0)
    grad_active = einsum_f("td,fd->tf", cotangent, mlp_out)
    grad_hidden = gelu_back(grad_active)[0].astype(jnp.bfloat16)
    grad_mlp_in = einsum_f("td,tf->df", third_in, grad_hidden)
    grad_mlp_in_bias = jnp.sum(grad_hidden.astype(jnp.float32), axis=0)
    grad_third = lax.psum(
        einsum_f("tf,df->td", grad_hidden, mlp_in).astype(jnp.bfloat16), "mp"
    ).astype(jnp.float32)
    back_three, gain_three, shift_three = norm_back(
        normed_three, scale_three, ln_gain[2], grad_third
    )
    grad_two = upstream + back_three
    up_two = grad_two.astype(jnp.bfloat16)
    grad_cross_out = einsum_f("tk,td->kd", cross_att, up_two)
    grad_cross_out_bias = jnp.sum(up_two.astype(jnp.float32), axis=0)
    grad_cross_att = einsum_f("td,kd->tk", up_two, cross_out).astype(jnp.bfloat16)
    grad_cross_att = jnp.where(valid_mask, grad_cross_att, jnp.zeros_like(grad_cross_att))
    grad_cross_queries, grad_pairs = cross_backward(
        query_heads, memory_pairs, clip_of, log_cross, grad_cross_att
    )
    grad_cross_q = einsum_f("td,tk->dk", second_in, grad_cross_queries)
    grad_query_bias = jnp.sum(grad_cross_queries.astype(jnp.float32), axis=0)
    grad_keys_cross = grad_pairs[:, :, :head_width]
    grad_values_cross = grad_pairs[:, :, head_width:]
    grad_cross_kv = jnp.stack(
        [
            einsum_f("cfd,cfe->de", slab, grad_keys_cross),
            einsum_f("cfd,cfe->de", slab, grad_values_cross),
        ]
    )
    grad_value_bias = jnp.sum(grad_values_cross.astype(jnp.float32), axis=(0, 1))
    memory_terms = einsum_f("cfe,de->cfd", grad_keys_cross, cross_kv[0]) + einsum_f(
        "cfe,de->cfd", grad_values_cross, cross_kv[1]
    )
    memory_grad = lax.psum_scatter(
        memory_terms.astype(jnp.bfloat16), "mp", scatter_dimension=1, tiled=True
    )
    grad_cross_bias = jnp.stack([grad_query_bias, grad_value_bias])
    grad_second = lax.psum(
        einsum_f("tk,dk->td", grad_cross_queries, cross_q).astype(jnp.bfloat16), "mp"
    ).astype(jnp.float32)
    back_two, gain_two, shift_two = norm_back(normed_two, scale_two, ln_gain[1], grad_second)
    grad_one = grad_two + back_two
    up_one = grad_one.astype(jnp.bfloat16)
    grad_self_out = einsum_f("tk,td->kd", self_att, up_one)
    grad_self_out_bias = jnp.sum(up_one.astype(jnp.float32), axis=0)
    grad_self_att = einsum_f("td,kd->tk", up_one, self_out).astype(jnp.bfloat16)
    grad_self_att = jnp.where(valid_mask, grad_self_att, jnp.zeros_like(grad_self_att))
    grad_queries, grad_keys_self, grad_values_self = self_backward(
        queries, keys_self, values_self, allowed, log_self, grad_self_att
    )
    grad_self_in = jnp.stack(
        [
            einsum_f("td,tk->dk", first_in, grad_queries),
            einsum_f("td,tk->dk", first_in, grad_keys_self),
            einsum_f("td,tk->dk", first_in, grad_values_self),
        ]
    )
    grad_self_bias = jnp.stack(
        [
            jnp.sum(grad_queries.astype(jnp.float32), axis=0),
            jnp.sum(grad_values_self.astype(jnp.float32), axis=0),
        ]
    )
    first_terms = (
        einsum_f("tk,dk->td", grad_queries, self_in[0])
        + einsum_f("tk,dk->td", grad_keys_self, self_in[1])
        + einsum_f("tk,dk->td", grad_values_self, self_in[2])
    )
    grad_first = lax.psum(first_terms.astype(jnp.bfloat16), "mp").astype(jnp.float32)
    back_one, gain_one, shift_one = norm_back(normed_one, scale_one, ln_gain[0], grad_first)
    input_grad = (grad_one + back_one).astype(jnp.bfloat16)
    sum_self_in, sum_self_out, sum_cross_q, sum_cross_kv, sum_cross_out, sum_mlp_in, sum_mlp_out = (
        lax.psum_scatter(grad_self_in, "dp", scatter_dimension=1, tiled=True),
        lax.psum_scatter(grad_self_out, "dp", scatter_dimension=1, tiled=True),
        lax.psum_scatter(grad_cross_q, "dp", scatter_dimension=0, tiled=True),
        lax.psum_scatter(grad_cross_kv, "dp", scatter_dimension=1, tiled=True),
        lax.psum_scatter(grad_cross_out, "dp", scatter_dimension=1, tiled=True),
        lax.psum_scatter(grad_mlp_in, "dp", scatter_dimension=0, tiled=True),
        lax.psum_scatter(grad_mlp_out, "dp", scatter_dimension=1, tiled=True),
    )
    (
        sum_gain,
        sum_shift,
        sum_self_bias,
        sum_self_out_bias,
        sum_cross_bias,
        sum_cross_out_bias,
        sum_mlp_in_bias,
        sum_mlp_out_bias,
    ) = lax.psum(
        (
            jnp.stack([gain_one, gain_two, gain_three]),
            jnp.stack([shift_one, shift_two, shift_three]),
            grad_self_bias,
            grad_self_out_bias,
            grad_cross_bias,
            grad_cross_out_bias,
            grad_mlp_in_bias,
            grad_mlp_out_bias,
        ),
        "dp",
    )
    return (
        mixed,
        input_grad,
        memory_grad,
        sum_gain,
        sum_shift,
        sum_self_in,
        sum_self_bias,
        sum_self_out,
        sum_self_out_bias,
        sum_cross_q,
        sum_cross_kv,
        sum_cross_bias,
        sum_cross_out,
        sum_cross_out_bias,
        sum_mlp_in,
        sum_mlp_in_bias,
        sum_mlp_out,
        sum_mlp_out_bias,
    )


def solution(mesh):
    in_specs = (
        P("dp", None),
        P("dp", "mp", None),
        P("dp"),
        P("dp", None),
        P(),
        P(),
        P(None, None, "mp"),
        P(None, "mp"),
        P("mp", None),
        P(),
        P(None, "mp"),
        P(None, None, "mp"),
        P(None, "mp"),
        P("mp", None),
        P(),
        P(None, "mp"),
        P("mp"),
        P("mp", None),
        P(),
    )
    out_specs = (
        P("dp", None),
        P("dp", None),
        P("dp", "mp", None),
        P(),
        P(),
        P(None, "dp", "mp"),
        P(None, "mp"),
        P("mp", "dp"),
        P(),
        P("dp", "mp"),
        P(None, "dp", "mp"),
        P(None, "mp"),
        P("mp", "dp"),
        P(),
        P("dp", "mp"),
        P("mp"),
        P("mp", "dp"),
        P(),
    )
    shape = dict(mesh.shape)
    run = fused if (shape["dp"], shape["mp"]) == (8, 4) else body
    return jax.shard_map(run, mesh=mesh, in_specs=in_specs, out_specs=out_specs, check_vma=False)
```

```python
import math

import jax
import jax.numpy as jnp
from jax import lax
from jax.experimental import pallas as pl
from jax.experimental.pallas import tpu as pltpu
from jax.sharding import PartitionSpec as P

HD = 64
D, HW, T, TA, FQ, FP, AB, PB = 768, 192, 512, 448, 375, 384, 112, 32
NH = HW // HD
FT, TH = 4 * FP, T // 2
BF, F32 = jnp.bfloat16, jnp.float32
VMEM_LIMIT = 62 << 20


def nn(a, b):
    return lax.dot_general(a, b, (((1,), (0,)), ((), ())), preferred_element_type=F32)


def nt(a, b):
    return lax.dot_general(a, b, (((1,), (1,)), ((), ())), preferred_element_type=F32)


def tn(a, b):
    return lax.dot_general(a, b, (((0,), (0,)), ((), ())), preferred_element_type=F32)


def ds(start, size, step=16):
    return pl.ds(pl.multiple_of(start, step), size)


def colsum(values):
    return jnp.sum(values, axis=0, keepdims=True)


def normed(values):
    average = jnp.mean(values, axis=-1, keepdims=True)
    centred = values - average
    variance = jnp.mean(centred * centred, axis=-1, keepdims=True)
    inv = lax.rsqrt(variance + 1e-05)
    return centred * inv, inv


def layer_kernel(
    tok, mem, lens, cot, gains, shifts, w_si, self_bias, w_so, so_bias, w_cq, w_ck, cross_bias, w_co,
    co_bias, w_mi, mi_bias, w_mo, mo_bias,
    mixed_o, igrad_o, mgrad_o, grads_o, small_o,
    T_, G_, len_, qb_, si, so, cq, ck, co, mi, mo, slab,
    x1, q_, k_, v_, ps_, satt, m1, x2, cq_, K_, V_, pc_, catt, m2, x3, act, gh,
    ups, dO, dsb, gkv, gcq, upo, dOs, gqkv,
    pS, pR, zS, zR, fin,
    mtS, mtR, mtZ, mtZr, mtF,
    gb, gR, gFr, gO, sb, sR,
    lsem, ssem, rsem,
):
    d, z = lax.axis_index("dp"), lax.axis_index("mp")
    c = lax.rem(d, 2)
    p = z // 2
    chip = d // 2
    native = c == p
    foreign = jnp.logical_not(native)
    flip = lambda a, bit: a + bit * (1 - 2 * lax.rem(a // bit, 2))
    z1, z2 = flip(z, 1), flip(z, 2)
    z3 = flip(z2, 1)
    q = jnp.where(native, z, z2)
    dc, dx, dy = flip(d, 1), flip(d, 2), flip(d, 4)
    dd = flip(dx, 4)
    C, Zp, Fz, F3, CF, CF3 = (dc, z), (d, z1), (d, z2), (d, z3), (dc, z2), (dc, z3)
    X, Y, XY = (dx, z), (dy, z), (dd, z)
    plane = ((X, dx // 2), (Y, dy // 2), (XY, dd // 2))
    MESH = pl.DeviceIdType.MESH
    barrier = pltpu.get_barrier_semaphore()
    all_peers = (C, Zp, Fz, F3, CF, CF3, X, Y, XY)
    for peer in all_peers:
        pl.semaphore_signal(barrier, inc=1, device_id=peer, device_id_type=MESH)
    pl.semaphore_wait(barrier, len(all_peers))

    counter = [0, 0]
    drains = []

    def remote(src, dst, dev, when=None):
        i = counter[0]
        counter[0] += 1
        copy = pltpu.make_async_remote_copy(
            src_ref=src, dst_ref=dst, send_sem=ssem.at[i], recv_sem=rsem.at[i],
            device_id=dev, device_id_type=MESH,
        )
        drains.append((copy, when))
        return copy

    def local(src, dst):
        i = counter[1]
        counter[1] += 1
        return pltpu.make_async_copy(src, dst, lsem.at[i])

    def loop(count, fn):
        def step(i, carry):
            fn(i)
            return carry

        lax.fori_loop(0, count, step, 0)

    row = lambda ref: ref[...].astype(F32).reshape(1, D)
    gain = lambda i: gains[i : i + 1, :]
    shift = lambda i: shifts[i : i + 1, :]

    rc_tok = remote(tok, T_, C, "n")
    rc_len = remote(len_, len_, C, "n")
    rc_cot = remote(cot, G_, C, "n")
    rc_qb = remote(qb_, qb_, Fz, "n")
    weights = {}

    def weight(name, src, dst):
        size = dst.shape[0] // 4
        at = lambda ref: ref.at[ds(chip * size, size), :]
        first = remote(at(src), at(dst), Fz, "n")
        spread = [remote(at(dst), at(dst), dev, "f") for dev, _ in plane]
        weights[name] = (first, spread, local(src, dst))

    for name, src, dst in (
        ("si", w_si, si), ("ck", w_ck, ck), ("cq", w_cq, cq), ("so", w_so, so), ("co", w_co, co),
        ("mo", w_mo, mo), ("mi", w_mi, mi),
    ):
        weight(name, src, dst)
    lc_tok, lc_cot = local(tok, T_), local(cot, G_)
    rc_mem = remote(mem, slab.at[z], Fz, "f")
    lc_mem = local(mem, slab.at[z])
    rc_mz0 = remote(slab.at[z], slab.at[z], Zp, "n")
    rc_mz2 = remote(slab.at[z2], slab.at[z2], Zp, "n")
    rc_mc = [remote(slab.at[zz], slab.at[zz], C, "n") for zz in (z, z2, z1, z3)]

    def spread_weight(name):
        first, spread, loc = weights[name]
        first.wait_recv()
        for copy in spread:
            copy.start()

    def need_weight(name):
        first, spread, loc = weights[name]

        @pl.when(native)
        def _():
            loc.wait()

        @pl.when(foreign)
        def _():
            for copy in spread:
                copy.wait_recv()

    @pl.when(native)
    def _():
        weights["si"][0].start()
        rc_tok.start()
        lc_tok.start()
        weights["si"][2].start()
        len_[...] = jnp.broadcast_to(lens[...].astype(F32).reshape(1, 1), (8, 128))
        rc_len.start()
        qb_[0:2, 0:HW] = self_bias[...].astype(F32)
        qb_[2:4, 0:HW] = cross_bias[...].astype(F32)
        qb_[4:5, :] = row(mi_bias)
        rc_qb.start()
        for copy in (lc_mem, lc_cot) + tuple(weights[n][2] for n in ("ck", "so", "cq", "co", "mo", "mi")):
            copy.start()
        lc_tok.wait()

    @pl.when(foreign)
    def _():
        rc_tok.wait_recv()
        rc_len.wait_recv()

    def ln0(i):
        rows = ds(i * AB, AB)
        n, _ = normed(T_[rows, :].astype(F32))
        x1[rows, :] = (n * gain(0) + shift(0)).astype(BF)

    loop(TA // AB, ln0)

    @pl.when(foreign)
    def _():
        spread_weight("si")
        rc_mem.start()
        rc_qb.wait_recv()

    need_weight("si")

    def heads_to(ref, rows, values):
        for h in range(NH):
            ref[h, rows, :] = values[:, h * HD : (h + 1) * HD].astype(BF)

    def qkv(i):
        rows = ds(i * AB, AB)
        values = nt(x1[rows, :], si[...])
        heads_to(q_, rows, values[:, 0:HW] + qb_[0:1, 0:HW])
        heads_to(k_, rows, values[:, HW : 2 * HW])
        heads_to(v_, rows, values[:, 2 * HW :] + qb_[1:2, 0:HW])

    loop(TA // AB, qkv)

    @pl.when(native)
    def _():
        for name in ("so", "ck", "cq", "co"):
            weights[name][0].start()
        lc_mem.wait()
        rc_mz0.start()
        rc_mc[0].start()
        rc_cot.start()

    @pl.when(foreign)
    def _():
        for name in ("so", "ck", "cq", "co"):
            spread_weight(name)

    length = len_[0:1, 0:1]

    def valid_rows(start):
        return (start + lax.broadcasted_iota(jnp.int32, (AB, 1), 0)).astype(F32)

    size_of = (AB, AB, PB)
    lrows = lambda j: slice(j * AB, j * AB + size_of[j])
    gstart = lambda h, j: h * (TA // 2) + j * AB if j < 2 else TA + h * PB
    grows = lambda h, j: ds(gstart(h, j), size_of[j])
    mine, other = c, 1 - c
    half = lambda t: c + t * (1 - 2 * c)
    slots = {}

    def sum_open(slot, count):
        for copy in slots.get(slot, ()):
            copy.wait_send()
            drains[:] = [item for item in drains if item[0] is not copy]
        to_core = [remote(pS.at[slot, lrows(j), :], pR.at[slot, lrows(j), :], C) for j in range(count)]
        to_chip = [remote(zS.at[slot, lrows(j), :], zR.at[slot, lrows(j), :], Zp) for j in range(count)]
        slots[slot] = to_core + to_chip
        return slot, to_core, to_chip

    def emit(opened, j, product):
        slot, to_core, to_chip = opened
        pS[slot, lrows(j), :] = product(grows(other, j)).astype(BF)
        to_core[j].start()
        own = product(grows(mine, j))
        to_core[j].wait_recv()
        zS[slot, lrows(j), :] = (own + pR[slot, lrows(j), :].astype(F32)).astype(BF)
        to_chip[j].start()

    def take(opened, j):
        slot, to_core, to_chip = opened
        to_chip[j].wait_recv()
        return zS[slot, lrows(j), :].astype(F32) + zR[slot, lrows(j), :].astype(F32)

    def share(ref, j):
        copy = remote(ref.at[grows(mine, j), :], ref.at[grows(mine, j), :], C)
        copy.start()
        return copy

    def both(copy, fn):
        def part(t):
            @pl.when(t == 1)
            def _():
                copy.wait_recv()

            fn(half(t))

        loop(2, part)

    self_cols = lax.broadcasted_iota(jnp.int32, (1, TA), 1).astype(F32)

    def self_fwd(start):
        rows = ds(start, AB)
        ids = valid_rows(start)
        valid = ids < length
        allowed = (self_cols <= ids) & valid
        outs = []
        for h in range(NH):
            s = nt(q_[h, rows, :], k_[h]) * 0.125
            s = jnp.where(allowed, s, -1000000000.0)
            e = jnp.exp(s - jnp.max(s, axis=-1, keepdims=True))
            pb = (e * (1.0 / jnp.sum(e, axis=-1, keepdims=True))).astype(BF)
            ps_[h, rows, :] = pb
            outs.append(nn(pb, v_[h]))
        att = jnp.where(valid, jnp.concatenate(outs, axis=1), 0.0)
        satt[rows, :] = att.astype(BF)

    ar1 = sum_open(0, 2)
    loop(2, lambda t: self_fwd(gstart(half(1 - t), 0)))
    need_weight("so")
    emit(ar1, 0, lambda rows: nn(satt[rows, :], so[...]))
    loop(2, lambda t: self_fwd(gstart(half(1 - t), 1)))
    emit(ar1, 1, lambda rows: nn(satt[rows, :], so[...]))

    @pl.when(native)
    def _():
        weights["mo"][0].start()
        weights["mi"][0].start()

    need_weight("ck")

    for h in range(NH):
        for s in range(4):
            K_[h, (s + 1) * FP - 16 : (s + 1) * FP, :] = jnp.zeros((16, HD), BF)
            V_[h, (s + 1) * FP - 16 : (s + 1) * FP, :] = jnp.zeros((16, HD), BF)

    def project(zz):
        out = pl.ds(pl.multiple_of(zz * FP, FP), FQ)
        values = nt(slab[zz], ck[...])
        heads_to(K_, out, values[:, 0:HW])
        heads_to(V_, out, values[:, HW:] + qb_[3:4, 0:HW])

    for slot, zz in enumerate((z, z2, z1, z3)):
        @pl.when(native)
        def _():
            if slot == 1:
                rc_mem.wait_recv()
                rc_mz2.start()
                rc_mc[1].start()
            if slot == 2:
                rc_mz0.wait_recv()
                rc_mc[2].start()
            if slot == 3:
                rc_mz2.wait_recv()
                rc_mc[3].start()

        @pl.when(foreign)
        def _():
            rc_mc[slot].wait_recv()

        project(zz)

    @pl.when(foreign)
    def _():
        spread_weight("mo")
        spread_weight("mi")

    need_weight("cq")
    need_weight("co")
    frame = lax.broadcasted_iota(jnp.int32, (1, FT), 1)
    frame_ok = lax.rem(frame, FP) < FQ

    def cross_fwd(start):
        rows = ds(start, AB)
        valid = valid_rows(start) < length
        queries = nt(x2[rows, :], cq[...]) + qb_[2:3, 0:HW]
        heads_to(cq_, rows, queries)
        outs = []
        for h in range(NH):
            s = nt(cq_[h, rows, :], K_[h]) * 0.125
            s = jnp.where(frame_ok, s, -3e38)
            e = jnp.exp(s - jnp.max(s, axis=-1, keepdims=True))
            pb = (e * (1.0 / jnp.sum(e, axis=-1, keepdims=True))).astype(BF)
            pc_[h, rows, :] = pb
            outs.append(nn(pb, V_[h]))
        att = jnp.where(valid, jnp.concatenate(outs, axis=1), 0.0)
        catt[rows, :] = att.astype(BF)

    ar2 = sum_open(1, 2)
    for j in range(2):
        own = grows(mine, j)
        value = T_[own, :].astype(F32) + take(ar1, j) + row(so_bias)
        m1[lrows(j), :] = value
        n, _ = normed(value)
        x2[own, :] = (n * gain(1) + shift(1)).astype(BF)
        both(share(x2, j), lambda h: cross_fwd(gstart(h, j)))
        emit(ar2, j, lambda rows: nn(catt[rows, :], co[...]))

    @pl.when(native)
    def _():
        lc_cot.wait()

    @pl.when(foreign)
    def _():
        rc_cot.wait_recv()

    need_weight("mo")

    def grad_active(i):
        rows = ds(i * 128, 128)
        fin[rows, :] = nt(G_[rows, :], mo[...])

    loop(T // 128, grad_active)
    need_weight("mi")

    def mlp(rows):
        hidden = nn(x3[rows, :], mi[...]) + qb_[4:5, :]
        phi = 0.5 * (1.0 + lax.erf(hidden * (0.5**0.5)))
        density = jnp.exp(-0.5 * hidden * hidden) * (1.0 / math.sqrt(2.0 * math.pi))
        act[rows, :] = (hidden * phi).astype(BF)
        gh[rows, :] = (fin[rows, :] * (phi + hidden * density)).astype(BF)

    ar3 = sum_open(0, 3)
    for j in (2, 0, 1):
        own = grows(mine, j)
        if j == 2:
            value = T_[own, :].astype(F32) + row(so_bias) + row(co_bias)
        else:
            value = m1[lrows(j), :] + take(ar2, j) + row(co_bias)
        m2[lrows(j), :] = value
        n, _ = normed(value)
        x3[own, :] = (n * gain(2) + shift(2)).astype(BF)
        both(share(x3, j), lambda h: mlp(grows(h, j)))
        emit(ar3, j, lambda rows: nt(gh[rows, :], mi[...]))

    gsends = {}

    def plane_send(m):
        gsends[m] = [
            remote(gb.at[m, ds(kk * 192, 192), :], gR.at[m, s], dev)
            for s, (dev, kk) in enumerate(plane)
        ]
        for copy in gsends[m]:
            copy.start()

    thirds = [slice(i * 256, (i + 1) * 256) for i in range(3)]
    for cols in thirds:
        gb[0, cols, :] = tn(x3[:, cols], gh[...]).astype(BF)
    plane_send(0)
    arm = sum_open(2, 3)
    for j in range(3):
        emit(arm, j, lambda rows: nn(act[rows, :], mo[...]))
    for cols in thirds:
        gb[1, cols, :] = tn(G_[:, cols], act[...]).astype(BF)
    plane_send(1)
    mi_sums = colsum(gh[...].astype(F32))
    zero_row = jnp.zeros((1, D), F32)
    g_gain, g_shift = [zero_row] * 3, [zero_row] * 3
    b_out = [zero_row] * 3

    def norm_back(value, upstream, i):
        n, inv = normed(value)
        a = upstream * gain(i)
        g_gain[i] = g_gain[i] + colsum(upstream * n)
        g_shift[i] = g_shift[i] + colsum(upstream)
        return inv * (a - jnp.mean(a, axis=-1, keepdims=True) - n * jnp.mean(a * n, axis=-1, keepdims=True))

    def third_back(j):
        g = G_[grows(mine, j), :].astype(F32)
        b_out[2] = b_out[2] + colsum(g)
        value = g + norm_back(m2[lrows(j), :], take(ar3, j), 2)
        low = value.astype(BF)
        b_out[1] = b_out[1] + colsum(low.astype(F32))
        fin[lrows(j), :] = value
        return low

    def cross_bwd(start):
        rows = ds(start, AB)
        valid = valid_rows(start) < length
        heads_to(dO, rows, jnp.where(valid, nt(ups[rows, :], co[...]), 0.0))
        outs = []
        for h in range(NH):
            dp_ = nt(dO[h, rows, :], V_[h])
            pr = pc_[h, rows, :].astype(F32)
            dsv = (pr * (dp_ - jnp.sum(pr * dp_, axis=-1, keepdims=True))).astype(BF)
            dsb[h, rows, :] = dsv
            outs.append(nn(dsv, K_[h]) * 0.125)
        gcq[rows, :] = jnp.concatenate(outs, axis=1).astype(BF)

    ar4 = sum_open(1, 2)
    for j in range(2):
        ups[grows(mine, j), :] = third_back(j)
        both(share(ups, j), lambda h: cross_bwd(gstart(h, j)))
        emit(ar4, j, lambda rows: nn(gcq[rows, :], cq[...]))

    pad_low = third_back(2)
    b_out[0] = b_out[0] + colsum(pad_low.astype(F32))
    block = lax.rem(z, 2)
    outs = []

    def give(slot, out_ref):
        from_n, from_f, to_core = [], [], []
        for lo, hi, size, step in ((0, c * (TA // 2), AB, 16), (2 * AB, TA + c * PB, PB // 2, 16)):
            src = gO.at[slot, ds(lo + block * size, size), :]
            dst = out_ref.at[ds(hi + block * size, size), :]
            from_n += [remote(src, dst, dev, "n") for dev in (Fz, F3)]
            from_f += [remote(src, dst, dev, "f") for dev in (CF, CF3)]
            both_rows = out_ref.at[ds(hi, 2 * size), :]
            to_core.append(remote(gO.at[slot, lo : lo + 2 * size, :], both_rows, C, "f"))

        @pl.when(native)
        def _():
            for copy in from_n:
                copy.start()
            for j in range(3):
                out_ref[grows(mine, j), :] = gO[slot, lrows(j), :]

        @pl.when(foreign)
        def _():
            for copy in to_core + from_f:
                copy.start()

        outs.append((from_n, from_f, to_core))

    for j in range(3):
        value = m2[lrows(j), :] + take(arm, j) + row(mo_bias)
        gO[0, lrows(j), :] = value.astype(BF)
    give(0, mixed_o)

    def kv_grad(i):
        rows = ds(i * FP, FP)
        frames = ds(i * FP, FP, 128)
        parts = [tn(dsb[h, :, frames], cq_[h]) * 0.125 for h in range(NH)]
        parts += [tn(pc_[h, :, frames], dO[h]) for h in range(NH)]
        gkv[rows, :] = jnp.concatenate(parts, axis=1).astype(BF)

    loop(4, kv_grad)

    def mem_term(zz):
        return nn(gkv[ds(zz * FP, FP), :], ck[...])[0:FQ]

    q1, q2 = flip(q, 1), flip(q, 2)
    q3 = flip(q2, 1)
    mt_core = [remote(mtS.at[j], mtR.at[j], C) for j in range(2)]
    mt_chip = remote(mtZ, mtZr, Zp)
    mt_out = remote(mtF, mgrad_o, CF, "f")
    for j, zz in ((1, q3), (0, q2)):
        mtS[j] = mem_term(zz).astype(BF)
        mt_core[j].start()
    next_term = mem_term(q1)
    mt_core[1].wait_recv()
    mtZ[...] = (next_term + mtR[1].astype(F32)).astype(BF)
    mt_chip.start()
    own_term = mem_term(q)
    mt_core[0].wait_recv()
    mtF[...] = (own_term + mtR[0].astype(F32)).astype(BF)
    for cols in thirds:
        a = tn(x2[:, cols], gcq[...])
        b = sum(tn(slab[s, :, cols], gkv[s * FP : s * FP + FQ, :]) for s in range(4))
        e = tn(ups[:, cols], catt[...])
        gb[2, cols, :] = jnp.concatenate([a, b, e], axis=1).astype(BF)
    plane_send(2)

    finals = {}
    own_piece = ds(chip * 192, 192)
    for m in range(4):
        finals[m] = (
            remote(gb.at[m, own_piece, :], gFr.at[m], Fz, "f"),
            remote(fin.at[m * 96 : (m + 1) * 96, :], grads_o.at[m], C, "n"),
        )

    def piece_sum(m):
        piece = gb[m, own_piece, :].astype(F32)
        for s in range(3):
            gsends[m][s].wait_recv()
            piece = piece + gR[m, s].astype(F32)
        return piece

    def piece_out(m):
        @pl.when(foreign)
        def _():
            gb[m, own_piece, :] = piece_sum(m).astype(BF)
            finals[m][0].start()

    def piece_final(m):
        @pl.when(native)
        def _():
            piece = piece_sum(m)
            finals[m][0].wait_recv()
            whole = piece + gFr[m].astype(F32)
            fin[m * 96 : (m + 1) * 96, :] = jnp.where(c == 0, whole[96:192, :], whole[0:96, :])
            finals[m][1].start()
            grads_o[m] = jnp.where(c == 0, whole[0:96, :], whole[96:192, :])

    piece_out(0)

    def self_bwd(start):
        rows = ds(start, AB)
        valid = valid_rows(start) < length
        heads_to(dOs, rows, jnp.where(valid, nt(upo[rows, :], so[...]), 0.0))
        outs = []
        for h in range(NH):
            dp_ = nt(dOs[h, rows, :], v_[h])
            pr = ps_[h, rows, :].astype(F32)
            dsv = (pr * (dp_ - jnp.sum(pr * dp_, axis=-1, keepdims=True))).astype(BF)
            dsb[h, rows, 0:TA] = dsv
            outs.append(nn(dsv, k_[h]) * 0.125)
        gqkv[rows, 0:HW] = jnp.concatenate(outs, axis=1).astype(BF)

    for j in range(2):
        own = grows(mine, j)
        value = fin[lrows(j), :] + norm_back(m1[lrows(j), :], take(ar4, j), 1)
        low = value.astype(BF)
        b_out[0] = b_out[0] + colsum(low.astype(F32))
        upo[own, :] = low
        fin[TH + j * AB : TH + (j + 1) * AB, :] = value
        both(share(upo, j), lambda h: self_bwd(gstart(h, j)))
    gO[1, lrows(2), :] = pad_low
    kv = [tn(dsb[h, :, 0:TA], q_[h]) * 0.125 for h in range(NH)]
    kv += [tn(ps_[h], dOs[h]) for h in range(NH)]
    gqkv[:, HW:] = jnp.concatenate(kv, axis=1).astype(BF)

    ar5 = sum_open(0, 2)
    for j in range(2):
        emit(ar5, j, lambda rows: nn(gqkv[rows, :], si[...]))

    for cols in thirds:
        left = tn(x1[:, cols], gqkv[...])
        right = tn(upo[:, cols], satt[...])
        gb[3, cols, :] = jnp.concatenate([left, right], axis=1).astype(BF)
    plane_send(3)
    piece_out(1)
    mt_chip.wait_recv()
    mtF[...] = (mtF[...].astype(F32) + mtZr[...].astype(F32)).astype(BF)

    @pl.when(native)
    def _():
        mgrad_o[...] = mtF[...]

    @pl.when(foreign)
    def _():
        mt_out.start()

    gs = gqkv[...].astype(F32)
    quarter = jnp.concatenate(
        [
            colsum(gs[:, 0:HW]),
            colsum(gs[:, 2 * HW :]),
            colsum(gcq[...].astype(F32)),
            colsum(gkv[:, HW:].astype(F32)),
        ],
        axis=1,
    )

    for j in range(2):
        own = grows(mine, j)
        value = fin[TH + j * AB : TH + (j + 1) * AB, :] + norm_back(T_[own, :].astype(F32), take(ar5, j), 0)
        gO[1, lrows(j), :] = value.astype(BF)
    give(1, igrad_o)

    ids = lax.broadcasted_iota(jnp.int32, (24, 1), 0)
    packed = jnp.zeros((24, D), F32)
    for i, values in enumerate(g_gain + g_shift + b_out):
        packed = packed + jnp.where(ids == i, values * 0.5, 0.0)
    packed = packed + jnp.where(ids == 9 + q, quarter, 0.0) + jnp.where(ids == 13 + q, mi_sums, 0.0)
    sb[0] = packed
    fillers = [lambda: piece_out(2), lambda: piece_final(0), lambda: piece_final(1), lambda: piece_out(3), lambda: None]
    for i, dev in enumerate((C, Zp, Fz, X, Y)):
        copy = remote(sb.at[i], sR.at[i], dev)
        copy.start()
        fillers[i]()
        copy.wait_recv()
        sb[i + 1] = sb[i] + sR[i]
    total = sb[5]
    small_o[0:9, :] = total[0:9, :]
    small_o[9:10, :] = colsum(jnp.where(ids == 9 + z, total, 0.0))
    small_o[10:11, :] = colsum(jnp.where(ids == 13 + z, total, 0.0))
    small_o[11:16, :] = jnp.zeros((5, D), F32)

    piece_final(2)
    piece_final(3)

    @pl.when(foreign)
    def _():
        for m in range(4):
            finals[m][1].wait_recv()
        mt_out.wait_recv()
        for from_n, from_f, to_core in outs:
            for copy in from_n + from_f:
                copy.wait_recv()

    @pl.when(native)
    def _():
        for from_n, from_f, to_core in outs:
            for copy in to_core:
                copy.wait_recv()

    for copy, when in drains:
        if when is None:
            copy.wait_send()

    @pl.when(native)
    def _():
        for copy, when in drains:
            if when == "n":
                copy.wait_send()

    @pl.when(foreign)
    def _():
        for copy, when in drains:
            if when == "f":
                copy.wait_send()


def finish_kernel(
    mixed_i, igrad_i, mgrad_i, grads, small,
    mixed_o, igrad_o, mgrad_o, gain_o, shift_o, si_o, sb_o, so_o, sob_o, cq_o, ck_o, cb_o, co_o, cob_o,
    mi_o, mib_o, mo_o, mob_o,
):
    mixed_o[...] = mixed_i[...]
    igrad_o[...] = igrad_i[...]
    mgrad_o[...] = mgrad_i[...]
    gain_o[...] = small[0:3, :]
    shift_o[...] = small[3:6, :]
    for i in range(3):
        si_o[i] = grads[3, :, i * HW : (i + 1) * HW]
    for i in range(2):
        sb_o[i : i + 1, :] = small[9:10, i * HW : (i + 1) * HW]
        cb_o[i : i + 1, :] = small[9:10, (i + 2) * HW : (i + 3) * HW]
        ck_o[i] = grads[2, :, (i + 1) * HW : (i + 2) * HW]
    so_o[...] = grads[3, :, 3 * HW :].T
    cq_o[...] = grads[2, :, 0:HW]
    co_o[...] = grads[2, :, 3 * HW :].T
    sob_o[...] = small[6]
    cob_o[...] = small[7]
    mob_o[...] = small[8]
    mib_o[...] = small[10]
    mi_o[...] = grads[0]
    mo_o[...] = grads[1]


def fused(
    tokens, memory, lengths, cotangent, ln_gain, ln_bias, self_in, self_bias, self_out,
    self_out_bias, cross_q, cross_kv, cross_bias, cross_out, cross_out_bias, mlp_in,
    mlp_in_bias, mlp_out, mlp_out_bias,
):
    vmem = pltpu.VMEM
    heads, frames = vmem((NH, TA, HD), BF), vmem((NH, FT, HD), BF)
    rows, low_rows, own_rows = vmem((T, D), BF), vmem((TA, D), BF), vmem((TH, D), F32)
    att = vmem((TA, HW), BF)
    probs, sums, memo = vmem((NH, TA, FT), BF), vmem((3, TH, D), BF), vmem((FQ, D), BF)
    scratch = [
        rows, rows, vmem((8, 128), F32), vmem((8, D), F32),
        vmem((3 * HW, D), BF), vmem((HW, D), BF), vmem((HW, D), BF), vmem((2 * HW, D), BF), vmem((HW, D), BF),
        vmem((D, D), BF), vmem((D, D), BF), vmem((4, FQ, D), BF),
        low_rows, heads, heads, heads, vmem((NH, TA, TA), BF), att, own_rows, low_rows,
        heads, frames, frames, probs, att, own_rows, rows, rows, rows,
        low_rows, heads, probs, vmem((FT, 2 * HW), BF), att, low_rows, heads, vmem((TA, 3 * HW), BF),
        sums, sums, sums, sums, vmem((T, D), F32),
        vmem((2, FQ, D), BF), vmem((2, FQ, D), BF), memo, memo, memo,
        vmem((4, D, D), BF), vmem((4, 3, 192, D), BF), vmem((4, 192, D), BF),
        vmem((2, TH, D), BF), vmem((6, 24, D), F32), vmem((5, 24, D), F32),
        pltpu.SemaphoreType.DMA((16,)), pltpu.SemaphoreType.DMA((150,)), pltpu.SemaphoreType.DMA((150,)),
    ]
    hbm, on_chip = pl.BlockSpec(memory_space=pl.ANY), pl.BlockSpec(memory_space=pltpu.VMEM)
    shape = jax.ShapeDtypeStruct
    wide = [shape((T, D), BF), shape((T, D), BF), shape((FQ, D), BF)]
    h, v = hbm, on_chip
    parts = pl.pallas_call(
        layer_kernel,
        out_shape=wide + [shape((4, 96, D), F32), shape((16, D), F32)],
        in_specs=[h, h, v, h, v, v, h, v, h, v, h, h, v, h, v, h, v, h, v],
        out_specs=[on_chip] * 5,
        scratch_shapes=scratch,
        compiler_params=pltpu.CompilerParams(
            collective_id=0, has_side_effects=True, vmem_limit_bytes=VMEM_LIMIT
        ),
    )(
        tokens, memory[0], lengths, cotangent, ln_gain, ln_bias,
        jnp.swapaxes(self_in, 1, 2).reshape(3 * HW, D), self_bias, self_out, self_out_bias,
        cross_q.T, jnp.swapaxes(cross_kv, 1, 2).reshape(2 * HW, D), cross_bias, cross_out, cross_out_bias,
        mlp_in, mlp_in_bias, mlp_out, mlp_out_bias,
    )
    vec = shape((D,), F32)
    outs = list(pl.pallas_call(
        finish_kernel,
        out_shape=wide
        + [
            shape((3, D), F32), shape((3, D), F32), shape((3, 96, HW), F32), shape((2, HW), F32),
            shape((HW, 96), F32), vec, shape((96, HW), F32), shape((2, 96, HW), F32), shape((2, HW), F32),
            shape((HW, 96), F32), vec, shape((96, D), F32), vec, shape((96, D), F32), vec,
        ],
        in_specs=[on_chip] * 5,
        out_specs=[on_chip] * 18,
    )(*parts))
    outs[2] = outs[2][None]
    outs[16] = outs[16].T
    return tuple(outs)


def matmul(left, right):
    return jnp.dot(left, right, preferred_element_type=jnp.float32)


def einsum_f(form, left, right):
    return jnp.einsum(form, left, right, preferred_element_type=jnp.float32)


def norm_parts(values):
    average = jnp.mean(values, axis=-1, keepdims=True)
    centred = values - average
    variance = jnp.mean(centred * centred, axis=-1, keepdims=True)
    scale_inv = lax.rsqrt(variance + 1e-05)
    return (centred * scale_inv, scale_inv)


def norm_back(normed, scale_inv, gain, upstream):
    scaled = upstream * gain
    inner = (
        scaled
        - jnp.mean(scaled, axis=-1, keepdims=True)
        - normed * jnp.mean(scaled * normed, axis=-1, keepdims=True)
    )
    return (scale_inv * inner, jnp.sum(upstream * normed, axis=0), jnp.sum(upstream, axis=0))


def softmax_parts(scores):
    row_max = jnp.max(scores, axis=-1, keepdims=True)
    shifted = jnp.exp(scores - row_max)
    totals = jnp.sum(shifted, axis=-1, keepdims=True)
    return (shifted / totals, row_max[..., 0] + jnp.log(totals[..., 0]))


def gelu_exact(values):
    return jax.nn.gelu(values, approximate=False)


def self_forward(queries, keys_self, values_self, allowed, valid_mask):
    row_count, head_width = queries.shape
    head_count = head_width // HD
    query_heads = queries.reshape(row_count, head_count, HD)
    key_heads = keys_self.reshape(row_count, head_count, HD)
    value_heads = values_self.reshape(row_count, head_count, HD)
    scores = einsum_f("thd,shd->hts", query_heads, key_heads) * 0.125
    scores = jnp.where(allowed[None], scores, -1000000000.0)
    probs, log_total = softmax_parts(scores)
    attended = einsum_f("hts,shd->thd", probs.astype(jnp.bfloat16), value_heads).reshape(
        row_count, head_width
    )
    attended = jnp.where(valid_mask, attended, 0.0)
    return (attended.astype(jnp.bfloat16), log_total)


def self_backward(queries, keys_self, values_self, allowed, log_total, grad_out):
    row_count, head_width = queries.shape
    head_count = head_width // HD
    query_heads = queries.reshape(row_count, head_count, HD)
    key_heads = keys_self.reshape(row_count, head_count, HD)
    value_heads = values_self.reshape(row_count, head_count, HD)
    scores = einsum_f("thd,shd->hts", query_heads, key_heads) * 0.125
    scores = jnp.where(allowed[None], scores, -1000000000.0)
    probs = jnp.exp(scores - log_total[..., None])
    grad_heads = grad_out.reshape(row_count, head_count, HD)
    grad_values = einsum_f("hts,thd->shd", probs.astype(jnp.bfloat16), grad_heads)
    grad_probs = einsum_f("thd,shd->hts", grad_heads, value_heads)
    grad_scores = (
        probs * (grad_probs - jnp.sum(probs * grad_probs, axis=-1, keepdims=True))
    ).astype(jnp.bfloat16)
    grad_queries = einsum_f("hts,shd->thd", grad_scores, key_heads) * 0.125
    grad_keys = einsum_f("hts,thd->shd", grad_scores, query_heads) * 0.125
    return (
        grad_queries.reshape(row_count, head_width).astype(jnp.bfloat16),
        grad_keys.reshape(row_count, head_width).astype(jnp.bfloat16),
        grad_values.reshape(row_count, head_width).astype(jnp.bfloat16),
    )


def cross_forward(query_heads, memory_pairs, clip_of):
    row_count, head_count, _ = query_heads.shape
    head_width = head_count * HD
    clip_count = memory_pairs.shape[0]

    def per_clip(carry, clip_item):
        attended, log_rows = carry
        clip_index, clip_pairs = clip_item
        key_heads = clip_pairs[:, :head_width].reshape(-1, head_count, HD)
        value_heads = clip_pairs[:, head_width:].reshape(-1, head_count, HD)
        scores = einsum_f("thd,fhd->htf", query_heads, key_heads) * 0.125
        probs, log_total = softmax_parts(scores)
        result = einsum_f("htf,fhd->thd", probs.astype(jnp.bfloat16), value_heads).reshape(
            row_count, head_width
        )
        member = clip_of == clip_index
        return (
            (
                jnp.where(member[:, None], result, attended),
                jnp.where(member[None, :], log_total, log_rows),
            ),
            None,
        )

    start_carry = (
        jnp.zeros((row_count, head_width), jnp.float32),
        jnp.zeros((head_count, row_count), jnp.float32),
    )
    (attended, log_rows), _ = lax.scan(
        per_clip, start_carry, (jnp.arange(clip_count, dtype=jnp.int32), memory_pairs)
    )
    return (attended.astype(jnp.bfloat16), log_rows)


def cross_backward(query_heads, memory_pairs, clip_of, log_rows, grad_out):
    row_count, head_count, _ = query_heads.shape
    head_width = head_count * HD
    clip_count = memory_pairs.shape[0]

    def per_clip(grad_query, clip_item):
        clip_index, clip_pairs = clip_item
        frames = clip_pairs.shape[0]
        member = clip_of == clip_index
        key_heads = clip_pairs[:, :head_width].reshape(frames, head_count, HD)
        value_heads = clip_pairs[:, head_width:].reshape(frames, head_count, HD)
        scores = einsum_f("thd,fhd->htf", query_heads, key_heads) * 0.125
        probs = jnp.where(member[None, :, None], jnp.exp(scores - log_rows[:, :, None]), 0.0)
        grad_heads = jnp.where(member[:, None], grad_out, jnp.zeros_like(grad_out)).reshape(
            row_count, head_count, HD
        )
        grad_values = einsum_f("htf,thd->fhd", probs.astype(jnp.bfloat16), grad_heads)
        grad_probs = einsum_f("thd,fhd->htf", grad_heads, value_heads)
        grad_scores = (
            probs * (grad_probs - jnp.sum(probs * grad_probs, axis=-1, keepdims=True))
        ).astype(jnp.bfloat16)
        grad_query = grad_query + einsum_f("htf,fhd->thd", grad_scores, key_heads) * 0.125
        grad_keys = einsum_f("htf,thd->fhd", grad_scores, query_heads) * 0.125
        grad_pairs = jnp.concatenate(
            [grad_keys.reshape(frames, head_width), grad_values.reshape(frames, head_width)], axis=1
        )
        return (grad_query, grad_pairs.astype(jnp.bfloat16))

    grad_query, grad_pairs = lax.scan(
        per_clip,
        jnp.zeros((row_count, head_count, HD), jnp.float32),
        (jnp.arange(clip_count, dtype=jnp.int32), memory_pairs),
    )
    return (grad_query.reshape(row_count, head_width).astype(jnp.bfloat16), grad_pairs)


def body(
    tokens,
    memory,
    lengths,
    cotangent,
    ln_gain,
    ln_bias,
    self_in,
    self_bias,
    self_out,
    self_out_bias,
    cross_q,
    cross_kv,
    cross_bias,
    cross_out,
    cross_out_bias,
    mlp_in,
    mlp_in_bias,
    mlp_out,
    mlp_out_bias,
):
    row_count = tokens.shape[0]
    clip_count = lengths.shape[0]
    head_width = self_in.shape[2]
    head_count = head_width // HD
    clip_ends = jnp.cumsum(lengths)
    positions = jnp.arange(row_count, dtype=jnp.int32)
    clip_of = jnp.sum((positions[:, None] >= clip_ends[None, :]).astype(jnp.int32), axis=1)
    valid_mask = (clip_of < clip_count)[:, None]
    allowed = (
        (clip_of[:, None] == clip_of[None, :])
        & (positions[None, :] <= positions[:, None])
        & (clip_of[:, None] < clip_count)
    )
    inputs = tokens.astype(jnp.float32)
    normed_one, scale_one = norm_parts(inputs)
    first_in = (normed_one * ln_gain[0] + ln_bias[0]).astype(jnp.bfloat16)
    queries = (matmul(first_in, self_in[0]) + self_bias[0]).astype(jnp.bfloat16)
    keys_self = matmul(first_in, self_in[1]).astype(jnp.bfloat16)
    values_self = (matmul(first_in, self_in[2]) + self_bias[1]).astype(jnp.bfloat16)
    self_att, log_self = self_forward(queries, keys_self, values_self, allowed, valid_mask)
    mixed_one = inputs + lax.psum(matmul(self_att, self_out), "mp") + self_out_bias
    normed_two, scale_two = norm_parts(mixed_one)
    second_in = (normed_two * ln_gain[1] + ln_bias[1]).astype(jnp.bfloat16)
    cross_queries = (matmul(second_in, cross_q) + cross_bias[0]).astype(jnp.bfloat16)
    slab = lax.all_gather(memory, "mp", axis=1, tiled=True)
    slab_keys = einsum_f("cfd,de->cfe", slab, cross_kv[0]).astype(jnp.bfloat16)
    slab_values = (einsum_f("cfd,de->cfe", slab, cross_kv[1]) + cross_bias[1]).astype(jnp.bfloat16)
    memory_pairs = jnp.concatenate([slab_keys, slab_values], axis=2)
    query_heads = cross_queries.reshape(row_count, head_count, HD)
    cross_att, log_cross = cross_forward(query_heads, memory_pairs, clip_of)
    mixed_two = (
        mixed_one
        + lax.psum(matmul(cross_att, cross_out).astype(jnp.bfloat16), "mp").astype(jnp.float32)
        + cross_out_bias
    )
    normed_three, scale_three = norm_parts(mixed_two)
    third_in = (normed_three * ln_gain[2] + ln_bias[2]).astype(jnp.bfloat16)
    hidden = matmul(third_in, mlp_in) + mlp_in_bias
    active, gelu_back = jax.vjp(gelu_exact, hidden)
    active_low = active.astype(jnp.bfloat16)
    mixed = (
        mixed_two
        + lax.psum(matmul(active_low, mlp_out).astype(jnp.bfloat16), "mp").astype(jnp.float32)
        + mlp_out_bias
    ).astype(jnp.bfloat16)
    upstream = cotangent.astype(jnp.float32)
    grad_mlp_out = einsum_f("tf,td->fd", active_low, cotangent)
    grad_mlp_out_bias = jnp.sum(upstream, axis=0)
    grad_active = einsum_f("td,fd->tf", cotangent, mlp_out)
    grad_hidden = gelu_back(grad_active)[0].astype(jnp.bfloat16)
    grad_mlp_in = einsum_f("td,tf->df", third_in, grad_hidden)
    grad_mlp_in_bias = jnp.sum(grad_hidden.astype(jnp.float32), axis=0)
    grad_third = lax.psum(
        einsum_f("tf,df->td", grad_hidden, mlp_in).astype(jnp.bfloat16), "mp"
    ).astype(jnp.float32)
    back_three, gain_three, shift_three = norm_back(
        normed_three, scale_three, ln_gain[2], grad_third
    )
    grad_two = upstream + back_three
    up_two = grad_two.astype(jnp.bfloat16)
    grad_cross_out = einsum_f("tk,td->kd", cross_att, up_two)
    grad_cross_out_bias = jnp.sum(up_two.astype(jnp.float32), axis=0)
    grad_cross_att = einsum_f("td,kd->tk", up_two, cross_out).astype(jnp.bfloat16)
    grad_cross_att = jnp.where(valid_mask, grad_cross_att, jnp.zeros_like(grad_cross_att))
    grad_cross_queries, grad_pairs = cross_backward(
        query_heads, memory_pairs, clip_of, log_cross, grad_cross_att
    )
    grad_cross_q = einsum_f("td,tk->dk", second_in, grad_cross_queries)
    grad_query_bias = jnp.sum(grad_cross_queries.astype(jnp.float32), axis=0)
    grad_keys_cross = grad_pairs[:, :, :head_width]
    grad_values_cross = grad_pairs[:, :, head_width:]
    grad_cross_kv = jnp.stack(
        [
            einsum_f("cfd,cfe->de", slab, grad_keys_cross),
            einsum_f("cfd,cfe->de", slab, grad_values_cross),
        ]
    )
    grad_value_bias = jnp.sum(grad_values_cross.astype(jnp.float32), axis=(0, 1))
    memory_terms = einsum_f("cfe,de->cfd", grad_keys_cross, cross_kv[0]) + einsum_f(
        "cfe,de->cfd", grad_values_cross, cross_kv[1]
    )
    memory_grad = lax.psum_scatter(
        memory_terms.astype(jnp.bfloat16), "mp", scatter_dimension=1, tiled=True
    )
    grad_cross_bias = jnp.stack([grad_query_bias, grad_value_bias])
    grad_second = lax.psum(
        einsum_f("tk,dk->td", grad_cross_queries, cross_q).astype(jnp.bfloat16), "mp"
    ).astype(jnp.float32)
    back_two, gain_two, shift_two = norm_back(normed_two, scale_two, ln_gain[1], grad_second)
    grad_one = grad_two + back_two
    up_one = grad_one.astype(jnp.bfloat16)
    grad_self_out = einsum_f("tk,td->kd", self_att, up_one)
    grad_self_out_bias = jnp.sum(up_one.astype(jnp.float32), axis=0)
    grad_self_att = einsum_f("td,kd->tk", up_one, self_out).astype(jnp.bfloat16)
    grad_self_att = jnp.where(valid_mask, grad_self_att, jnp.zeros_like(grad_self_att))
    grad_queries, grad_keys_self, grad_values_self = self_backward(
        queries, keys_self, values_self, allowed, log_self, grad_self_att
    )
    grad_self_in = jnp.stack(
        [
            einsum_f("td,tk->dk", first_in, grad_queries),
            einsum_f("td,tk->dk", first_in, grad_keys_self),
            einsum_f("td,tk->dk", first_in, grad_values_self),
        ]
    )
    grad_self_bias = jnp.stack(
        [
            jnp.sum(grad_queries.astype(jnp.float32), axis=0),
            jnp.sum(grad_values_self.astype(jnp.float32), axis=0),
        ]
    )
    first_terms = (
        einsum_f("tk,dk->td", grad_queries, self_in[0])
        + einsum_f("tk,dk->td", grad_keys_self, self_in[1])
        + einsum_f("tk,dk->td", grad_values_self, self_in[2])
    )
    grad_first = lax.psum(first_terms.astype(jnp.bfloat16), "mp").astype(jnp.float32)
    back_one, gain_one, shift_one = norm_back(normed_one, scale_one, ln_gain[0], grad_first)
    input_grad = (grad_one + back_one).astype(jnp.bfloat16)
    sum_self_in, sum_self_out, sum_cross_q, sum_cross_kv, sum_cross_out, sum_mlp_in, sum_mlp_out = (
        lax.psum_scatter(grad_self_in, "dp", scatter_dimension=1, tiled=True),
        lax.psum_scatter(grad_self_out, "dp", scatter_dimension=1, tiled=True),
        lax.psum_scatter(grad_cross_q, "dp", scatter_dimension=0, tiled=True),
        lax.psum_scatter(grad_cross_kv, "dp", scatter_dimension=1, tiled=True),
        lax.psum_scatter(grad_cross_out, "dp", scatter_dimension=1, tiled=True),
        lax.psum_scatter(grad_mlp_in, "dp", scatter_dimension=0, tiled=True),
        lax.psum_scatter(grad_mlp_out, "dp", scatter_dimension=1, tiled=True),
    )
    (
        sum_gain,
        sum_shift,
        sum_self_bias,
        sum_self_out_bias,
        sum_cross_bias,
        sum_cross_out_bias,
        sum_mlp_in_bias,
        sum_mlp_out_bias,
    ) = lax.psum(
        (
            jnp.stack([gain_one, gain_two, gain_three]),
            jnp.stack([shift_one, shift_two, shift_three]),
            grad_self_bias,
            grad_self_out_bias,
            grad_cross_bias,
            grad_cross_out_bias,
            grad_mlp_in_bias,
            grad_mlp_out_bias,
        ),
        "dp",
    )
    return (
        mixed,
        input_grad,
        memory_grad,
        sum_gain,
        sum_shift,
        sum_self_in,
        sum_self_bias,
        sum_self_out,
        sum_self_out_bias,
        sum_cross_q,
        sum_cross_kv,
        sum_cross_bias,
        sum_cross_out,
        sum_cross_out_bias,
        sum_mlp_in,
        sum_mlp_in_bias,
        sum_mlp_out,
        sum_mlp_out_bias,
    )


def solution(mesh):
    in_specs = (
        P("dp", None),
        P("dp", "mp", None),
        P("dp"),
        P("dp", None),
        P(),
        P(),
        P(None, None, "mp"),
        P(None, "mp"),
        P("mp", None),
        P(),
        P(None, "mp"),
        P(None, None, "mp"),
        P(None, "mp"),
        P("mp", None),
        P(),
        P(None, "mp"),
        P("mp"),
        P("mp", None),
        P(),
    )
    out_specs = (
        P("dp", None),
        P("dp", None),
        P("dp", "mp", None),
        P(),
        P(),
        P(None, "dp", "mp"),
        P(None, "mp"),
        P("mp", "dp"),
        P(),
        P("dp", "mp"),
        P(None, "dp", "mp"),
        P(None, "mp"),
        P("mp", "dp"),
        P(),
        P("dp", "mp"),
        P("mp"),
        P("mp", "dp"),
        P(),
    )
    shape = dict(mesh.shape)
    run = fused if (shape["dp"], shape["mp"]) == (8, 4) else body
    return jax.shard_map(run, mesh=mesh, in_specs=in_specs, out_specs=out_specs, check_vma=False)
```

```python
import math

import jax
import jax.numpy as jnp
from jax import lax
from jax.experimental import pallas as pl
from jax.experimental.pallas import tpu as pltpu
from jax.sharding import PartitionSpec as P

HD = 64
D, HW, T, TA, FQ, FP, AB, PB = 768, 192, 512, 448, 375, 384, 112, 32
NH = HW // HD
FT, TH = 4 * FP, T // 2
BF, F32 = jnp.bfloat16, jnp.float32
VMEM_LIMIT = 62 << 20


def nn(a, b):
    return lax.dot_general(a, b, (((1,), (0,)), ((), ())), preferred_element_type=F32)


def nt(a, b):
    return lax.dot_general(a, b, (((1,), (1,)), ((), ())), preferred_element_type=F32)


def tn(a, b):
    return lax.dot_general(a, b, (((0,), (0,)), ((), ())), preferred_element_type=F32)


def ds(start, size, step=16):
    return pl.ds(pl.multiple_of(start, step), size)


def colsum(values):
    return jnp.sum(values, axis=0, keepdims=True)


def normed(values):
    average = jnp.mean(values, axis=-1, keepdims=True)
    centred = values - average
    variance = jnp.mean(centred * centred, axis=-1, keepdims=True)
    inv = lax.rsqrt(variance + 1e-05)
    return centred * inv, inv


def layer_kernel(
    tok, mem, lens, cot, gains, shifts, w_si, self_bias, w_so, so_bias, w_cq, w_ck, cross_bias, w_co,
    co_bias, w_mi, mi_bias, w_mo, mo_bias,
    mixed_o, igrad_o, mgrad_o, grads_o, small_o,
    T_, G_, len_, qb_, si, so, cq, ck, co, mi, mo, slab,
    x1, q_, k_, v_, ps_, satt, sat2, m1, x2, cq_, K_, V_, pc_, catt, m2, x3, act, gh,
    ups, dO, dsb, gkv, gcq, upo, dOs, gqkv,
    pS, pR, zS, zR, fin,
    mtS, mtR, mtZ, mtZr, mtF,
    gb, gR, gFr, gO, sb, sR, sX, sZ,
    lsem, ssem, rsem,
):
    d, z = lax.axis_index("dp"), lax.axis_index("mp")
    c = lax.rem(d, 2)
    p = z // 2
    chip = d // 2
    native = c == p
    foreign = jnp.logical_not(native)
    flip = lambda a, bit: a + bit * (1 - 2 * lax.rem(a // bit, 2))
    z1, z2 = flip(z, 1), flip(z, 2)
    z3 = flip(z2, 1)
    q = jnp.where(native, z, z2)
    dc, dx, dy = flip(d, 1), flip(d, 2), flip(d, 4)
    dd = flip(dx, 4)
    C, Zp, Fz, F3, CF = (dc, z), (d, z1), (d, z2), (d, z3), (dc, z2)
    X, Y, XY = (dx, z), (dy, z), (dd, z)
    CZ = (dc, z1)
    plane = ((X, dx // 2), (Y, dy // 2), (XY, dd // 2))
    MESH = pl.DeviceIdType.MESH
    barrier = pltpu.get_barrier_semaphore()
    all_peers = (C, Zp, Fz, F3, CF, CZ, X, Y, XY)
    for peer in all_peers:
        pl.semaphore_signal(barrier, inc=1, device_id=peer, device_id_type=MESH)

    counter = [0, 0]
    drains = []

    def remote(src, dst, dev, when=None):
        i = counter[0]
        counter[0] += 1
        copy = pltpu.make_async_remote_copy(
            src_ref=src, dst_ref=dst, send_sem=ssem.at[i], recv_sem=rsem.at[i],
            device_id=dev, device_id_type=MESH,
        )
        drains.append((copy, when))
        return copy

    def local(src, dst):
        i = counter[1]
        counter[1] += 1
        return pltpu.make_async_copy(src, dst, lsem.at[i])

    def loop(count, fn):
        def step(i, carry):
            fn(i)
            return carry

        lax.fori_loop(0, count, step, 0)

    row = lambda ref: ref[...].astype(F32).reshape(1, D)
    gain = lambda i: gains[i : i + 1, :]
    shift = lambda i: shifts[i : i + 1, :]

    rc_tok = remote(tok, T_, C, "n")
    rc_len = remote(len_, len_, C, "n")
    rc_cot = remote(cot, G_, C, "n")
    rc_qb = remote(qb_, qb_, Fz, "n")
    rc_sat = remote(sat2, satt, CF, "f")
    weights = {}

    def weight(name, src, dst):
        size = dst.shape[0] // 4
        at = lambda ref: ref.at[ds(chip * size, size), :]
        first = remote(at(src), at(dst), Fz, "n")
        spread = [remote(at(dst), at(dst), dev, "f") for dev, _ in plane]
        weights[name] = (first, spread, local(src, dst))

    for name, src, dst in (
        ("so", w_so, so), ("ck", w_ck, ck), ("cq", w_cq, cq), ("co", w_co, co), ("mo", w_mo, mo),
        ("mi", w_mi, mi), ("si", w_si, si),
    ):
        weight(name, src, dst)
    own_tok, own_si = act, gb.at[0, 0 : 3 * HW, :]
    lc_tok, lc_cot, lc_own, lc_own_si = local(tok, T_), local(cot, G_), local(tok, own_tok), local(w_si, own_si)
    rc_mem = remote(mem, slab.at[z], Fz, "f")
    lc_mem = local(mem, slab.at[z])
    rc_mz0 = remote(slab.at[z], slab.at[z], Zp, "n")
    rc_mz2 = remote(slab.at[z2], slab.at[z2], Zp, "n")
    rc_mc = [remote(slab.at[zz], slab.at[zz], C, "n") for zz in (z, z2, z1, z3)]

    def spread_weight(name):
        first, spread, loc = weights[name]
        first.wait_recv()
        for copy in spread:
            copy.start()

    def need_weight(name):
        first, spread, loc = weights[name]

        @pl.when(native)
        def _():
            loc.wait()

        @pl.when(foreign)
        def _():
            for copy in spread:
                copy.wait_recv()

    lc_own.start()
    lc_own_si.start()

    @pl.when(native)
    def _():
        lc_mem.start()
        for copy in [weights[n][2] for n in ("so", "ck")] + [lc_tok, lc_cot]:
            copy.start()
        for n in ("cq", "co", "mo", "mi", "si"):
            weights[n][2].start()
        len_[...] = jnp.broadcast_to(lens[...].astype(F32).reshape(1, 1), (8, 128))
        qb_[0:2, 0:HW] = self_bias[...].astype(F32)
        qb_[2:4, 0:HW] = cross_bias[...].astype(F32)
        qb_[4:5, :] = row(mi_bias)

    pl.semaphore_wait(barrier, len(all_peers))

    @pl.when(native)
    def _():
        weights["so"][0].start()
        weights["ck"][0].start()
        rc_qb.start()
        rc_len.start()
        lc_mem.wait()
        rc_mz0.start()
        rc_mc[0].start()
        rc_tok.start()
        rc_cot.start()

    @pl.when(foreign)
    def _():
        rc_mem.start()

    def ln0(src):
        def part(i):
            rows = ds(i * AB, AB)
            n, _ = normed(src[rows, :].astype(F32))
            x1[rows, :] = (n * gain(0) + shift(0)).astype(BF)

        loop(TA // AB, part)

    def heads_to(ref, rows, values):
        for h in range(NH):
            ref[h, rows, :] = values[:, h * HD : (h + 1) * HD].astype(BF)

    def qkv(proj, bias):
        def part(i):
            rows = ds(i * AB, AB)
            values = nt(x1[rows, :], proj[...])
            heads_to(q_, rows, values[:, 0:HW] + bias[0:1, 0:HW].astype(F32))
            heads_to(k_, rows, values[:, HW : 2 * HW])
            heads_to(v_, rows, values[:, 2 * HW :] + bias[1:2, 0:HW].astype(F32))

        loop(TA // AB, part)

    def row_ids(start):
        return (start + lax.broadcasted_iota(jnp.int32, (AB, 1), 0)).astype(F32)

    self_cols = lax.broadcasted_iota(jnp.int32, (1, TA), 1).astype(F32)

    def self_fwd(limit, dst):
        def part(i):
            start = i * AB
            rows = ds(start, AB)
            ids = row_ids(start)
            valid = ids < limit
            allowed = (self_cols <= ids) & valid
            outs = []
            for h in range(NH):
                s = nt(q_[h, rows, :], k_[h]) * 0.125
                s = jnp.where(allowed, s, -1000000000.0)
                e = jnp.exp(s - jnp.max(s, axis=-1, keepdims=True))
                pb = (e * (1.0 / jnp.sum(e, axis=-1, keepdims=True))).astype(BF)
                ps_[h, rows, :] = pb
                if dst is not None:
                    outs.append(nn(pb, v_[h]))
            if dst is not None:
                dst[rows, :] = jnp.where(valid, jnp.concatenate(outs, axis=1), 0.0).astype(BF)

        loop(TA // AB, part)

    lc_own.wait()
    ln0(own_tok)
    lc_own_si.wait()
    qkv(own_si, self_bias)

    @pl.when(foreign)
    def _():
        spread_weight("so")

    self_fwd(lens[...].astype(F32).reshape(1, 1), sat2)

    @pl.when(native)
    def _():
        for name in ("cq", "co"):
            weights[name][0].start()
        satt[...] = sat2[...]
        lc_tok.wait()

    @pl.when(foreign)
    def _():
        rc_sat.start()
        spread_weight("ck")
        rc_tok.wait_recv()
        rc_len.wait_recv()
        rc_qb.wait_recv()
        rc_sat.wait_recv()

    length = len_[0:1, 0:1]
    valid_rows = row_ids

    size_of = (AB, AB, PB)
    lrows = lambda j: slice(j * AB, j * AB + size_of[j])
    gstart = lambda h, j: h * (TA // 2) + j * AB if j < 2 else TA + h * PB
    grows = lambda h, j: ds(gstart(h, j), size_of[j])
    mine, other = c, 1 - c
    half = lambda t: c + t * (1 - 2 * c)
    slots = {}

    def sum_open(slot, count):
        for copy in slots.get(slot, ()):
            copy.wait_send()
            drains[:] = [item for item in drains if item[0] is not copy]
        to_core = [remote(pS.at[slot, lrows(j), :], pR.at[slot, lrows(j), :], C) for j in range(count)]
        to_chip = [remote(zS.at[slot, lrows(j), :], zR.at[slot, lrows(j), :], Zp) for j in range(count)]
        slots[slot] = to_core + to_chip
        return slot, to_core, to_chip

    def emit(opened, j, product, between=None):
        slot, to_core, to_chip = opened
        pS[slot, lrows(j), :] = product(grows(other, j)).astype(BF)
        to_core[j].start()
        own = product(grows(mine, j))
        if between is not None:
            between()
        to_core[j].wait_recv()
        zS[slot, lrows(j), :] = (own + pR[slot, lrows(j), :].astype(F32)).astype(BF)
        to_chip[j].start()

    def take(opened, j):
        slot, to_core, to_chip = opened
        to_chip[j].wait_recv()
        return zS[slot, lrows(j), :].astype(F32) + zR[slot, lrows(j), :].astype(F32)

    def share(ref, j):
        copy = remote(ref.at[grows(mine, j), :], ref.at[grows(mine, j), :], C)
        copy.start()
        return copy

    def both(copy, fn):
        def part(t):
            @pl.when(t == 1)
            def _():
                copy.wait_recv()

            fn(half(t))

        loop(2, part)

    def pass_memory():
        @pl.when(native)
        def _():
            rc_mem.wait_recv()
            rc_mz2.start()
            rc_mc[1].start()
            for name in ("mo", "mi", "si"):
                weights[name][0].start()

    ar1 = sum_open(0, 2)
    need_weight("so")
    emit(ar1, 0, lambda rows: nn(satt[rows, :], so[...]))
    emit(ar1, 1, lambda rows: nn(satt[rows, :], so[...]), pass_memory)

    @pl.when(foreign)
    def _():
        spread_weight("cq")
        spread_weight("co")

    need_weight("ck")

    for h in range(NH):
        for s in range(4):
            K_[h, (s + 1) * FP - 16 : (s + 1) * FP, :] = jnp.zeros((16, HD), BF)
            V_[h, (s + 1) * FP - 16 : (s + 1) * FP, :] = jnp.zeros((16, HD), BF)

    def project(zz):
        out = pl.ds(pl.multiple_of(zz * FP, FP), FQ)
        values = nt(slab[zz], ck[...])
        heads_to(K_, out, values[:, 0:HW])
        heads_to(V_, out, values[:, HW:] + qb_[3:4, 0:HW])

    for slot, zz in enumerate((z, z2, z1, z3)):
        @pl.when(native)
        def _():
            if slot == 2:
                rc_mz0.wait_recv()
                rc_mc[2].start()
            if slot == 3:
                rc_mz2.wait_recv()
                rc_mc[3].start()

        @pl.when(foreign)
        def _():
            rc_mc[slot].wait_recv()

        project(zz)

    need_weight("cq")
    need_weight("co")
    frame = lax.broadcasted_iota(jnp.int32, (1, FT), 1)
    frame_ok = lax.rem(frame, FP) < FQ

    def cross_fwd(start):
        rows = ds(start, AB)
        valid = valid_rows(start) < length
        queries = nt(x2[rows, :], cq[...]) + qb_[2:3, 0:HW]
        heads_to(cq_, rows, queries)
        outs = []
        for h in range(NH):
            s = nt(cq_[h, rows, :], K_[h]) * 0.125
            s = jnp.where(frame_ok, s, -3e38)
            e = jnp.exp(s - jnp.max(s, axis=-1, keepdims=True))
            pb = (e * (1.0 / jnp.sum(e, axis=-1, keepdims=True))).astype(BF)
            pc_[h, rows, :] = pb
            outs.append(nn(pb, V_[h]))
        att = jnp.where(valid, jnp.concatenate(outs, axis=1), 0.0)
        catt[rows, :] = att.astype(BF)

    @pl.when(foreign)
    def _():
        spread_weight("mo")

    ar2 = sum_open(1, 2)
    for j in range(2):
        own = grows(mine, j)
        value = T_[own, :].astype(F32) + take(ar1, j) + row(so_bias)
        m1[lrows(j), :] = value
        n, _ = normed(value)
        x2[own, :] = (n * gain(1) + shift(1)).astype(BF)
        both(share(x2, j), lambda h: cross_fwd(gstart(h, j)))
        emit(ar2, j, lambda rows: nn(catt[rows, :], co[...]))

        if j == 0:
            @pl.when(foreign)
            def _():
                spread_weight("mi")

    @pl.when(native)
    def _():
        lc_cot.wait()

    @pl.when(foreign)
    def _():
        rc_cot.wait_recv()

    need_weight("mo")

    def grad_active(i):
        rows = ds(i * 128, 128)
        fin[rows, :] = nt(G_[rows, :], mo[...])

    loop(T // 128, grad_active)
    need_weight("mi")

    def mlp(rows):
        hidden = nn(x3[rows, :], mi[...]) + qb_[4:5, :]
        phi = 0.5 * (1.0 + lax.erf(hidden * (0.5**0.5)))
        density = jnp.exp(-0.5 * hidden * hidden) * (1.0 / math.sqrt(2.0 * math.pi))
        act[rows, :] = (hidden * phi).astype(BF)
        gh[rows, :] = (fin[rows, :] * (phi + hidden * density)).astype(BF)

    ar3 = sum_open(0, 3)
    for j in (2, 0, 1):
        own = grows(mine, j)
        if j == 2:
            value = T_[own, :].astype(F32) + row(so_bias) + row(co_bias)
        else:
            value = m1[lrows(j), :] + take(ar2, j) + row(co_bias)
        m2[lrows(j), :] = value
        n, _ = normed(value)
        x3[own, :] = (n * gain(2) + shift(2)).astype(BF)
        both(share(x3, j), lambda h: mlp(grows(h, j)))
        emit(ar3, j, lambda rows: nt(gh[rows, :], mi[...]))
        if j == 2:
            @pl.when(foreign)
            def _():
                spread_weight("si")


    gsends = {}

    def plane_send(m):
        gsends[m] = [
            remote(gb.at[m, ds(kk * 192, 192), :], gR.at[m, s], dev)
            for s, (dev, kk) in enumerate(plane)
        ]
        for copy in gsends[m]:
            copy.start()

    thirds = [slice(i * 256, (i + 1) * 256) for i in range(3)]
    for cols in thirds:
        gb[0, cols, :] = tn(x3[:, cols], gh[...]).astype(BF)
    plane_send(0)
    arm = sum_open(2, 3)
    for j in range(3):
        emit(arm, j, lambda rows: nn(act[rows, :], mo[...]))
    for cols in thirds:
        gb[1, cols, :] = tn(G_[:, cols], act[...]).astype(BF)
    plane_send(1)
    mi_sums = colsum(gh[...].astype(F32))

    need_weight("si")

    @pl.when(foreign)
    def _():
        ln0(T_)
        qkv(si, qb_)
        self_fwd(length, None)

    zero_row = jnp.zeros((1, D), F32)
    g_gain, g_shift = [zero_row] * 3, [zero_row] * 3
    b_out = [zero_row] * 3

    def norm_back(value, upstream, i):
        n, inv = normed(value)
        a = upstream * gain(i)
        g_gain[i] = g_gain[i] + colsum(upstream * n)
        g_shift[i] = g_shift[i] + colsum(upstream)
        return inv * (a - jnp.mean(a, axis=-1, keepdims=True) - n * jnp.mean(a * n, axis=-1, keepdims=True))

    def third_back(j):
        g = G_[grows(mine, j), :].astype(F32)
        b_out[2] = b_out[2] + colsum(g)
        value = g + norm_back(m2[lrows(j), :], take(ar3, j), 2)
        low = value.astype(BF)
        b_out[1] = b_out[1] + colsum(low.astype(F32))
        fin[lrows(j), :] = value
        return low

    def cross_bwd(start):
        rows = ds(start, AB)
        valid = valid_rows(start) < length
        heads_to(dO, rows, jnp.where(valid, nt(ups[rows, :], co[...]), 0.0))
        outs = []
        for h in range(NH):
            dp_ = nt(dO[h, rows, :], V_[h])
            pr = pc_[h, rows, :].astype(F32)
            dsv = (pr * (dp_ - jnp.sum(pr * dp_, axis=-1, keepdims=True))).astype(BF)
            dsb[h, rows, :] = dsv
            outs.append(nn(dsv, K_[h]) * 0.125)
        gcq[rows, :] = jnp.concatenate(outs, axis=1).astype(BF)

    block = lax.rem(z, 2)
    outs = []

    def give(slot, out_ref):
        from_n, from_f, to_core, onward = [], [], [], []
        for lo, hi, step, size in ((0, 0, TA // 2, AB), (2 * AB, TA, PB, PB // 2)):
            src = gO.at[slot, ds(lo + block * size, size), :]
            dst = out_ref.at[ds(hi + c * step + block * size, size), :]
            from_n.append(remote(src, dst, Fz, "n"))
            from_f.append(remote(src, dst, CF, "f"))
            both_rows = out_ref.at[ds(hi + c * step, 2 * size), :]
            to_core.append(remote(gO.at[slot, lo : lo + 2 * size, :], both_rows, C, "f"))
            for h in range(2):
                rows = out_ref.at[ds(hi + h * step + block * size, size), :]
                onward.append(remote(rows, rows, Zp, "f"))

        @pl.when(native)
        def _():
            for copy in from_n:
                copy.start()
            for j in range(3):
                out_ref[grows(mine, j), :] = gO[slot, lrows(j), :]

        @pl.when(foreign)
        def _():
            for copy in from_f + to_core:
                copy.start()

        outs.append((from_n, from_f, to_core, onward))

    def pass_on(slot):
        from_n, from_f, to_core, onward = outs[slot]

        @pl.when(foreign)
        def _():
            for copy in from_n + from_f:
                copy.wait_recv()
            for copy in onward:
                copy.start()

    def give_mixed():
        for j in range(3):
            value = m2[lrows(j), :] + take(arm, j) + row(mo_bias)
            gO[0, lrows(j), :] = value.astype(BF)
        give(0, mixed_o)

    ar4 = sum_open(1, 2)
    for j in range(2):
        ups[grows(mine, j), :] = third_back(j)
        both(share(ups, j), lambda h: cross_bwd(gstart(h, j)))
        emit(ar4, j, lambda rows: nn(gcq[rows, :], cq[...]))
        if j == 0:
            give_mixed()

    finals = {}
    own_piece = ds(chip * 192, 192)
    for m in range(4):
        finals[m] = (
            remote(gb.at[m, own_piece, :], gFr.at[m], Fz, "f"),
            remote(fin.at[m * 96 : (m + 1) * 96, :], grads_o.at[m], C, "n"),
        )

    def piece_sum(m):
        piece = gb[m, own_piece, :].astype(F32)
        for s in range(3):
            gsends[m][s].wait_recv()
            piece = piece + gR[m, s].astype(F32)
        return piece

    def piece_out(m):
        @pl.when(foreign)
        def _():
            gb[m, own_piece, :] = piece_sum(m).astype(BF)
            finals[m][0].start()

    def piece_final(m):
        @pl.when(native)
        def _():
            piece = piece_sum(m)
            finals[m][0].wait_recv()
            whole = piece + gFr[m].astype(F32)
            fin[m * 96 : (m + 1) * 96, :] = jnp.where(c == 0, whole[96:192, :], whole[0:96, :])
            finals[m][1].start()
            grads_o[m] = jnp.where(c == 0, whole[0:96, :], whole[96:192, :])

    pad_low = third_back(2)
    b_out[0] = b_out[0] + colsum(pad_low.astype(F32))
    piece_out(0)

    def kv_grad(i):
        rows = ds(i * FP, FP)
        frames = ds(i * FP, FP, 128)
        parts = [tn(dsb[h, :, frames], cq_[h]) * 0.125 for h in range(NH)]
        parts += [tn(pc_[h, :, frames], dO[h]) for h in range(NH)]
        gkv[rows, :] = jnp.concatenate(parts, axis=1).astype(BF)

    loop(4, kv_grad)

    def mem_term(zz):
        return nn(gkv[ds(zz * FP, FP), :], ck[...])[0:FQ]

    q1, q2 = flip(q, 1), flip(q, 2)
    q3 = flip(q2, 1)
    mt_core = [remote(mtS.at[j], mtR.at[j], C) for j in range(2)]
    mt_chip = remote(mtZ, mtZr, Zp)
    mt_out = remote(mtF, mgrad_o, CF, "f")
    for j, zz in ((1, q3), (0, q2)):
        mtS[j] = mem_term(zz).astype(BF)
        mt_core[j].start()
    next_term = mem_term(q1)
    mt_core[1].wait_recv()
    mtZ[...] = (next_term + mtR[1].astype(F32)).astype(BF)
    mt_chip.start()
    own_term = mem_term(q)
    mt_core[0].wait_recv()
    mtF[...] = (own_term + mtR[0].astype(F32)).astype(BF)
    pass_on(0)
    for cols in thirds:
        a = tn(x2[:, cols], gcq[...])
        b = sum(tn(slab[s, :, cols], gkv[s * FP : s * FP + FQ, :]) for s in range(4))
        e = tn(ups[:, cols], catt[...])
        gb[2, cols, :] = jnp.concatenate([a, b, e], axis=1).astype(BF)
    plane_send(2)
    piece_out(1)

    def self_bwd(start):
        rows = ds(start, AB)
        valid = valid_rows(start) < length
        heads_to(dOs, rows, jnp.where(valid, nt(upo[rows, :], so[...]), 0.0))
        outs = []
        for h in range(NH):
            dp_ = nt(dOs[h, rows, :], v_[h])
            pr = ps_[h, rows, :].astype(F32)
            dsv = (pr * (dp_ - jnp.sum(pr * dp_, axis=-1, keepdims=True))).astype(BF)
            dsb[h, rows, 0:TA] = dsv
            outs.append(nn(dsv, k_[h]) * 0.125)
        gqkv[rows, 0:HW] = jnp.concatenate(outs, axis=1).astype(BF)

    for j in range(2):
        own = grows(mine, j)
        value = fin[lrows(j), :] + norm_back(m1[lrows(j), :], take(ar4, j), 1)
        low = value.astype(BF)
        b_out[0] = b_out[0] + colsum(low.astype(F32))
        upo[own, :] = low
        fin[TH + j * AB : TH + (j + 1) * AB, :] = value
        both(share(upo, j), lambda h: self_bwd(gstart(h, j)))
    gO[1, lrows(2), :] = pad_low
    kv = [tn(dsb[h, :, 0:TA], q_[h]) * 0.125 for h in range(NH)]
    kv += [tn(ps_[h], dOs[h]) for h in range(NH)]
    gqkv[:, HW:] = jnp.concatenate(kv, axis=1).astype(BF)

    for cols in thirds:
        left = tn(x1[:, cols], gqkv[...])
        right = tn(upo[:, cols], satt[...])
        gb[3, cols, :] = jnp.concatenate([left, right], axis=1).astype(BF)
    plane_send(3)
    last_core, last_chip = sum_open(0, 2)[1:]
    drains[:] = [item for item in drains if item[0] is not last_chip[1]]
    away, kept = 1 - block, block
    rows_of = lambda h, b: ds(h * (TA // 2) + b * AB, AB)
    last = None
    for step, b in enumerate((away, kept)):
        pS[0, lrows(step), :] = nn(gqkv[rows_of(other, b), :], si[...]).astype(BF)
        last_core[step].start()
        last = nn(gqkv[rows_of(mine, b), :], si[...])
        last_core[step].wait_recv()
        last = last + pR[0, lrows(step), :].astype(F32)
        if step == 0:
            zS[0, lrows(0), :] = last.astype(BF)
            last_chip[0].start()
    last_sum = last

    mt_chip.wait_recv()
    mtF[...] = (mtF[...].astype(F32) + mtZr[...].astype(F32)).astype(BF)

    @pl.when(native)
    def _():
        mgrad_o[...] = mtF[...]

    @pl.when(foreign)
    def _():
        mt_out.start()

    piece_out(2)
    piece_final(0)
    gs = gqkv[...].astype(F32)
    quarter = jnp.concatenate(
        [
            colsum(gs[:, 0:HW]),
            colsum(gs[:, 2 * HW :]),
            colsum(gcq[...].astype(F32)),
            colsum(gkv[:, HW:].astype(F32)),
        ],
        axis=1,
    )

    own = rows_of(mine, kept)
    last_chip[0].wait_recv()
    last_sum = last_sum + zR[0, lrows(0), :].astype(F32)
    value = fin[ds(TH + kept * AB, AB), :] + norm_back(T_[own, :].astype(F32), last_sum, 0)
    gO[1, 0:AB, :] = value.astype(BF)
    pads_at = lambda b: ds(TA + c * PB + b * (PB // 2), PB // 2)
    pad_src = gO.at[1, ds(2 * AB + block * (PB // 2), PB // 2), :]
    grad_src, grad_dst = gO.at[1, 0:AB, :], igrad_o.at[own, :]
    give_n = [remote(grad_src, grad_dst, dev, "n") for dev in (Fz, Zp)]
    give_f = [remote(grad_src, grad_dst, dev, "f") for dev in (CF, CZ, C)]
    pad_n = remote(pad_src, igrad_o.at[pads_at(block), :], Fz, "n")
    pad_f = remote(pad_src, igrad_o.at[pads_at(block), :], CF, "f")
    pad_c = remote(gO.at[1, 2 * AB : 2 * AB + PB, :], igrad_o.at[grows(mine, 2), :], C, "f")
    onward = []
    for h in range(2):
        for lo, size in ((h * (TA // 2) + block * AB, AB), (TA + h * PB + block * (PB // 2), PB // 2)):
            rows = igrad_o.at[ds(lo, size), :]
            onward.append(remote(rows, rows, Zp, "f"))

    @pl.when(native)
    def _():
        for copy in give_n + [pad_n]:
            copy.start()
        igrad_o[own, :] = gO[1, 0:AB, :]
        igrad_o[grows(mine, 2), :] = pad_low

    @pl.when(foreign)
    def _():
        for copy in give_f + [pad_f, pad_c]:
            copy.start()

    def pass_grad():
        @pl.when(foreign)
        def _():
            give_n[0].wait_recv()
            give_f[0].wait_recv()
            pad_n.wait_recv()
            pad_f.wait_recv()
            for copy in onward:
                copy.start()

    ids = lax.broadcasted_iota(jnp.int32, (24, 1), 0)
    packed = jnp.zeros((24, D), F32)
    for i, values in enumerate(g_gain + g_shift + b_out):
        share_of = 1.0 if i in (0, 3) else 0.5
        packed = packed + jnp.where(ids == i, values * share_of, 0.0)
    packed = packed + jnp.where(ids == 9 + q, quarter, 0.0) + jnp.where(ids == 13 + q, mi_sums, 0.0)
    sb[0] = packed
    small_c = remote(sb.at[0], sR, C)
    small_c.start()
    piece_final(1)
    small_c.wait_recv()
    sb[1] = sb[0] + sR[...]
    small_x = [remote(sb.at[1], sX.at[chip], dev) for dev, _ in plane]
    for copy in small_x:
        copy.start()
    sX[chip] = sb[1]
    piece_out(3)
    for copy in small_x:
        copy.wait_recv()
    sb[2] = sX[0] + sX[1] + sX[2] + sX[3]
    small_z = [remote(sb.at[2], sZ.at[z], dev) for dev in (Zp, Fz, F3)]
    for copy in small_z:
        copy.start()
    sZ[z] = sb[2]
    pass_grad()
    piece_final(2)
    for copy in small_z:
        copy.wait_recv()
    total = sZ[0] + sZ[1] + sZ[2] + sZ[3]
    small_o[0:9, :] = total[0:9, :]
    small_o[9:10, :] = colsum(jnp.where(ids == 9 + z, total, 0.0))
    small_o[10:11, :] = colsum(jnp.where(ids == 13 + z, total, 0.0))
    small_o[11:16, :] = jnp.zeros((5, D), F32)

    piece_final(3)

    @pl.when(foreign)
    def _():
        for m in range(4):
            finals[m][1].wait_recv()
        mt_out.wait_recv()
        for copy in outs[0][3] + onward:
            copy.wait_recv()

    @pl.when(native)
    def _():
        for copy in outs[0][2] + [give_n[1]] + give_f[1:] + [pad_c]:
            copy.wait_recv()

    for copy, when in drains:
        if when is None:
            copy.wait_send()

    @pl.when(native)
    def _():
        for copy, when in drains:
            if when == "n":
                copy.wait_send()

    @pl.when(foreign)
    def _():
        for copy, when in drains:
            if when == "f":
                copy.wait_send()


def finish_kernel(
    mixed_i, igrad_i, mgrad_i, grads, small,
    mixed_o, igrad_o, mgrad_o, gain_o, shift_o, si_o, sb_o, so_o, sob_o, cq_o, ck_o, cb_o, co_o, cob_o,
    mi_o, mib_o, mo_o, mob_o,
):
    mixed_o[...] = mixed_i[...]
    igrad_o[...] = igrad_i[...]
    mgrad_o[...] = mgrad_i[...]
    gain_o[...] = small[0:3, :]
    shift_o[...] = small[3:6, :]
    for i in range(3):
        si_o[i] = grads[3, :, i * HW : (i + 1) * HW]
    for i in range(2):
        sb_o[i : i + 1, :] = small[9:10, i * HW : (i + 1) * HW]
        cb_o[i : i + 1, :] = small[9:10, (i + 2) * HW : (i + 3) * HW]
        ck_o[i] = grads[2, :, (i + 1) * HW : (i + 2) * HW]
    so_o[...] = grads[3, :, 3 * HW :].T
    cq_o[...] = grads[2, :, 0:HW]
    co_o[...] = grads[2, :, 3 * HW :].T
    sob_o[...] = small[6]
    cob_o[...] = small[7]
    mob_o[...] = small[8]
    mib_o[...] = small[10]
    mi_o[...] = grads[0]
    mo_o[...] = grads[1]


def fused(
    tokens, memory, lengths, cotangent, ln_gain, ln_bias, self_in, self_bias, self_out,
    self_out_bias, cross_q, cross_kv, cross_bias, cross_out, cross_out_bias, mlp_in,
    mlp_in_bias, mlp_out, mlp_out_bias,
):
    vmem = pltpu.VMEM
    heads, frames = vmem((NH, TA, HD), BF), vmem((NH, FT, HD), BF)
    rows, low_rows, own_rows = vmem((T, D), BF), vmem((TA, D), BF), vmem((TH, D), F32)
    att = vmem((TA, HW), BF)
    probs, sums, memo = vmem((NH, TA, FT), BF), vmem((3, TH, D), BF), vmem((FQ, D), BF)
    scratch = [
        rows, rows, vmem((8, 128), F32), vmem((8, D), F32),
        vmem((3 * HW, D), BF), vmem((HW, D), BF), vmem((HW, D), BF), vmem((2 * HW, D), BF), vmem((HW, D), BF),
        vmem((D, D), BF), vmem((D, D), BF), vmem((4, FQ, D), BF),
        low_rows, heads, heads, heads, vmem((NH, TA, TA), BF), att, att, own_rows, low_rows,
        heads, frames, frames, probs, att, own_rows, rows, rows, rows,
        low_rows, heads, probs, vmem((FT, 2 * HW), BF), att, low_rows, heads, vmem((TA, 3 * HW), BF),
        sums, sums, sums, sums, vmem((T, D), F32),
        vmem((2, FQ, D), BF), vmem((2, FQ, D), BF), memo, memo, memo,
        vmem((4, D, D), BF), vmem((4, 3, 192, D), BF), vmem((4, 192, D), BF),
        vmem((2, TH, D), BF), vmem((3, 24, D), F32), vmem((24, D), F32),
        vmem((4, 24, D), F32), vmem((4, 24, D), F32),
        pltpu.SemaphoreType.DMA((16,)), pltpu.SemaphoreType.DMA((150,)), pltpu.SemaphoreType.DMA((150,)),
    ]
    hbm, on_chip = pl.BlockSpec(memory_space=pl.ANY), pl.BlockSpec(memory_space=pltpu.VMEM)
    shape = jax.ShapeDtypeStruct
    wide = [shape((T, D), BF), shape((T, D), BF), shape((FQ, D), BF)]
    h, v = hbm, on_chip
    parts = pl.pallas_call(
        layer_kernel,
        out_shape=wide + [shape((4, 96, D), F32), shape((16, D), F32)],
        in_specs=[h, h, v, h, v, v, h, v, h, v, h, h, v, h, v, h, v, h, v],
        out_specs=[on_chip] * 5,
        scratch_shapes=scratch,
        compiler_params=pltpu.CompilerParams(
            collective_id=0, has_side_effects=True, vmem_limit_bytes=VMEM_LIMIT
        ),
    )(
        tokens, memory[0], lengths, cotangent, ln_gain, ln_bias,
        jnp.swapaxes(self_in, 1, 2).reshape(3 * HW, D), self_bias, self_out, self_out_bias,
        cross_q.T, jnp.swapaxes(cross_kv, 1, 2).reshape(2 * HW, D), cross_bias, cross_out, cross_out_bias,
        mlp_in, mlp_in_bias, mlp_out, mlp_out_bias,
    )
    vec = shape((D,), F32)
    outs = list(pl.pallas_call(
        finish_kernel,
        out_shape=wide
        + [
            shape((3, D), F32), shape((3, D), F32), shape((3, 96, HW), F32), shape((2, HW), F32),
            shape((HW, 96), F32), vec, shape((96, HW), F32), shape((2, 96, HW), F32), shape((2, HW), F32),
            shape((HW, 96), F32), vec, shape((96, D), F32), vec, shape((96, D), F32), vec,
        ],
        in_specs=[on_chip] * 5,
        out_specs=[on_chip] * 18,
    )(*parts))
    outs[2] = outs[2][None]
    outs[16] = outs[16].T
    return tuple(outs)


def matmul(left, right):
    return jnp.dot(left, right, preferred_element_type=jnp.float32)


def einsum_f(form, left, right):
    return jnp.einsum(form, left, right, preferred_element_type=jnp.float32)


def norm_parts(values):
    average = jnp.mean(values, axis=-1, keepdims=True)
    centred = values - average
    variance = jnp.mean(centred * centred, axis=-1, keepdims=True)
    scale_inv = lax.rsqrt(variance + 1e-05)
    return (centred * scale_inv, scale_inv)


def norm_back(normed, scale_inv, gain, upstream):
    scaled = upstream * gain
    inner = (
        scaled
        - jnp.mean(scaled, axis=-1, keepdims=True)
        - normed * jnp.mean(scaled * normed, axis=-1, keepdims=True)
    )
    return (scale_inv * inner, jnp.sum(upstream * normed, axis=0), jnp.sum(upstream, axis=0))


def softmax_parts(scores):
    row_max = jnp.max(scores, axis=-1, keepdims=True)
    shifted = jnp.exp(scores - row_max)
    totals = jnp.sum(shifted, axis=-1, keepdims=True)
    return (shifted / totals, row_max[..., 0] + jnp.log(totals[..., 0]))


def gelu_exact(values):
    return jax.nn.gelu(values, approximate=False)


def self_forward(queries, keys_self, values_self, allowed, valid_mask):
    row_count, head_width = queries.shape
    head_count = head_width // HD
    query_heads = queries.reshape(row_count, head_count, HD)
    key_heads = keys_self.reshape(row_count, head_count, HD)
    value_heads = values_self.reshape(row_count, head_count, HD)
    scores = einsum_f("thd,shd->hts", query_heads, key_heads) * 0.125
    scores = jnp.where(allowed[None], scores, -1000000000.0)
    probs, log_total = softmax_parts(scores)
    attended = einsum_f("hts,shd->thd", probs.astype(jnp.bfloat16), value_heads).reshape(
        row_count, head_width
    )
    attended = jnp.where(valid_mask, attended, 0.0)
    return (attended.astype(jnp.bfloat16), log_total)


def self_backward(queries, keys_self, values_self, allowed, log_total, grad_out):
    row_count, head_width = queries.shape
    head_count = head_width // HD
    query_heads = queries.reshape(row_count, head_count, HD)
    key_heads = keys_self.reshape(row_count, head_count, HD)
    value_heads = values_self.reshape(row_count, head_count, HD)
    scores = einsum_f("thd,shd->hts", query_heads, key_heads) * 0.125
    scores = jnp.where(allowed[None], scores, -1000000000.0)
    probs = jnp.exp(scores - log_total[..., None])
    grad_heads = grad_out.reshape(row_count, head_count, HD)
    grad_values = einsum_f("hts,thd->shd", probs.astype(jnp.bfloat16), grad_heads)
    grad_probs = einsum_f("thd,shd->hts", grad_heads, value_heads)
    grad_scores = (
        probs * (grad_probs - jnp.sum(probs * grad_probs, axis=-1, keepdims=True))
    ).astype(jnp.bfloat16)
    grad_queries = einsum_f("hts,shd->thd", grad_scores, key_heads) * 0.125
    grad_keys = einsum_f("hts,thd->shd", grad_scores, query_heads) * 0.125
    return (
        grad_queries.reshape(row_count, head_width).astype(jnp.bfloat16),
        grad_keys.reshape(row_count, head_width).astype(jnp.bfloat16),
        grad_values.reshape(row_count, head_width).astype(jnp.bfloat16),
    )


def cross_forward(query_heads, memory_pairs, clip_of):
    row_count, head_count, _ = query_heads.shape
    head_width = head_count * HD
    clip_count = memory_pairs.shape[0]

    def per_clip(carry, clip_item):
        attended, log_rows = carry
        clip_index, clip_pairs = clip_item
        key_heads = clip_pairs[:, :head_width].reshape(-1, head_count, HD)
        value_heads = clip_pairs[:, head_width:].reshape(-1, head_count, HD)
        scores = einsum_f("thd,fhd->htf", query_heads, key_heads) * 0.125
        probs, log_total = softmax_parts(scores)
        result = einsum_f("htf,fhd->thd", probs.astype(jnp.bfloat16), value_heads).reshape(
            row_count, head_width
        )
        member = clip_of == clip_index
        return (
            (
                jnp.where(member[:, None], result, attended),
                jnp.where(member[None, :], log_total, log_rows),
            ),
            None,
        )

    start_carry = (
        jnp.zeros((row_count, head_width), jnp.float32),
        jnp.zeros((head_count, row_count), jnp.float32),
    )
    (attended, log_rows), _ = lax.scan(
        per_clip, start_carry, (jnp.arange(clip_count, dtype=jnp.int32), memory_pairs)
    )
    return (attended.astype(jnp.bfloat16), log_rows)


def cross_backward(query_heads, memory_pairs, clip_of, log_rows, grad_out):
    row_count, head_count, _ = query_heads.shape
    head_width = head_count * HD
    clip_count = memory_pairs.shape[0]

    def per_clip(grad_query, clip_item):
        clip_index, clip_pairs = clip_item
        frames = clip_pairs.shape[0]
        member = clip_of == clip_index
        key_heads = clip_pairs[:, :head_width].reshape(frames, head_count, HD)
        value_heads = clip_pairs[:, head_width:].reshape(frames, head_count, HD)
        scores = einsum_f("thd,fhd->htf", query_heads, key_heads) * 0.125
        probs = jnp.where(member[None, :, None], jnp.exp(scores - log_rows[:, :, None]), 0.0)
        grad_heads = jnp.where(member[:, None], grad_out, jnp.zeros_like(grad_out)).reshape(
            row_count, head_count, HD
        )
        grad_values = einsum_f("htf,thd->fhd", probs.astype(jnp.bfloat16), grad_heads)
        grad_probs = einsum_f("thd,fhd->htf", grad_heads, value_heads)
        grad_scores = (
            probs * (grad_probs - jnp.sum(probs * grad_probs, axis=-1, keepdims=True))
        ).astype(jnp.bfloat16)
        grad_query = grad_query + einsum_f("htf,fhd->thd", grad_scores, key_heads) * 0.125
        grad_keys = einsum_f("htf,thd->fhd", grad_scores, query_heads) * 0.125
        grad_pairs = jnp.concatenate(
            [grad_keys.reshape(frames, head_width), grad_values.reshape(frames, head_width)], axis=1
        )
        return (grad_query, grad_pairs.astype(jnp.bfloat16))

    grad_query, grad_pairs = lax.scan(
        per_clip,
        jnp.zeros((row_count, head_count, HD), jnp.float32),
        (jnp.arange(clip_count, dtype=jnp.int32), memory_pairs),
    )
    return (grad_query.reshape(row_count, head_width).astype(jnp.bfloat16), grad_pairs)


def body(
    tokens,
    memory,
    lengths,
    cotangent,
    ln_gain,
    ln_bias,
    self_in,
    self_bias,
    self_out,
    self_out_bias,
    cross_q,
    cross_kv,
    cross_bias,
    cross_out,
    cross_out_bias,
    mlp_in,
    mlp_in_bias,
    mlp_out,
    mlp_out_bias,
):
    row_count = tokens.shape[0]
    clip_count = lengths.shape[0]
    head_width = self_in.shape[2]
    head_count = head_width // HD
    clip_ends = jnp.cumsum(lengths)
    positions = jnp.arange(row_count, dtype=jnp.int32)
    clip_of = jnp.sum((positions[:, None] >= clip_ends[None, :]).astype(jnp.int32), axis=1)
    valid_mask = (clip_of < clip_count)[:, None]
    allowed = (
        (clip_of[:, None] == clip_of[None, :])
        & (positions[None, :] <= positions[:, None])
        & (clip_of[:, None] < clip_count)
    )
    inputs = tokens.astype(jnp.float32)
    normed_one, scale_one = norm_parts(inputs)
    first_in = (normed_one * ln_gain[0] + ln_bias[0]).astype(jnp.bfloat16)
    queries = (matmul(first_in, self_in[0]) + self_bias[0]).astype(jnp.bfloat16)
    keys_self = matmul(first_in, self_in[1]).astype(jnp.bfloat16)
    values_self = (matmul(first_in, self_in[2]) + self_bias[1]).astype(jnp.bfloat16)
    self_att, log_self = self_forward(queries, keys_self, values_self, allowed, valid_mask)
    mixed_one = inputs + lax.psum(matmul(self_att, self_out), "mp") + self_out_bias
    normed_two, scale_two = norm_parts(mixed_one)
    second_in = (normed_two * ln_gain[1] + ln_bias[1]).astype(jnp.bfloat16)
    cross_queries = (matmul(second_in, cross_q) + cross_bias[0]).astype(jnp.bfloat16)
    slab = lax.all_gather(memory, "mp", axis=1, tiled=True)
    slab_keys = einsum_f("cfd,de->cfe", slab, cross_kv[0]).astype(jnp.bfloat16)
    slab_values = (einsum_f("cfd,de->cfe", slab, cross_kv[1]) + cross_bias[1]).astype(jnp.bfloat16)
    memory_pairs = jnp.concatenate([slab_keys, slab_values], axis=2)
    query_heads = cross_queries.reshape(row_count, head_count, HD)
    cross_att, log_cross = cross_forward(query_heads, memory_pairs, clip_of)
    mixed_two = (
        mixed_one
        + lax.psum(matmul(cross_att, cross_out).astype(jnp.bfloat16), "mp").astype(jnp.float32)
        + cross_out_bias
    )
    normed_three, scale_three = norm_parts(mixed_two)
    third_in = (normed_three * ln_gain[2] + ln_bias[2]).astype(jnp.bfloat16)
    hidden = matmul(third_in, mlp_in) + mlp_in_bias
    active, gelu_back = jax.vjp(gelu_exact, hidden)
    active_low = active.astype(jnp.bfloat16)
    mixed = (
        mixed_two
        + lax.psum(matmul(active_low, mlp_out).astype(jnp.bfloat16), "mp").astype(jnp.float32)
        + mlp_out_bias
    ).astype(jnp.bfloat16)
    upstream = cotangent.astype(jnp.float32)
    grad_mlp_out = einsum_f("tf,td->fd", active_low, cotangent)
    grad_mlp_out_bias = jnp.sum(upstream, axis=0)
    grad_active = einsum_f("td,fd->tf", cotangent, mlp_out)
    grad_hidden = gelu_back(grad_active)[0].astype(jnp.bfloat16)
    grad_mlp_in = einsum_f("td,tf->df", third_in, grad_hidden)
    grad_mlp_in_bias = jnp.sum(grad_hidden.astype(jnp.float32), axis=0)
    grad_third = lax.psum(
        einsum_f("tf,df->td", grad_hidden, mlp_in).astype(jnp.bfloat16), "mp"
    ).astype(jnp.float32)
    back_three, gain_three, shift_three = norm_back(
        normed_three, scale_three, ln_gain[2], grad_third
    )
    grad_two = upstream + back_three
    up_two = grad_two.astype(jnp.bfloat16)
    grad_cross_out = einsum_f("tk,td->kd", cross_att, up_two)
    grad_cross_out_bias = jnp.sum(up_two.astype(jnp.float32), axis=0)
    grad_cross_att = einsum_f("td,kd->tk", up_two, cross_out).astype(jnp.bfloat16)
    grad_cross_att = jnp.where(valid_mask, grad_cross_att, jnp.zeros_like(grad_cross_att))
    grad_cross_queries, grad_pairs = cross_backward(
        query_heads, memory_pairs, clip_of, log_cross, grad_cross_att
    )
    grad_cross_q = einsum_f("td,tk->dk", second_in, grad_cross_queries)
    grad_query_bias = jnp.sum(grad_cross_queries.astype(jnp.float32), axis=0)
    grad_keys_cross = grad_pairs[:, :, :head_width]
    grad_values_cross = grad_pairs[:, :, head_width:]
    grad_cross_kv = jnp.stack(
        [
            einsum_f("cfd,cfe->de", slab, grad_keys_cross),
            einsum_f("cfd,cfe->de", slab, grad_values_cross),
        ]
    )
    grad_value_bias = jnp.sum(grad_values_cross.astype(jnp.float32), axis=(0, 1))
    memory_terms = einsum_f("cfe,de->cfd", grad_keys_cross, cross_kv[0]) + einsum_f(
        "cfe,de->cfd", grad_values_cross, cross_kv[1]
    )
    memory_grad = lax.psum_scatter(
        memory_terms.astype(jnp.bfloat16), "mp", scatter_dimension=1, tiled=True
    )
    grad_cross_bias = jnp.stack([grad_query_bias, grad_value_bias])
    grad_second = lax.psum(
        einsum_f("tk,dk->td", grad_cross_queries, cross_q).astype(jnp.bfloat16), "mp"
    ).astype(jnp.float32)
    back_two, gain_two, shift_two = norm_back(normed_two, scale_two, ln_gain[1], grad_second)
    grad_one = grad_two + back_two
    up_one = grad_one.astype(jnp.bfloat16)
    grad_self_out = einsum_f("tk,td->kd", self_att, up_one)
    grad_self_out_bias = jnp.sum(up_one.astype(jnp.float32), axis=0)
    grad_self_att = einsum_f("td,kd->tk", up_one, self_out).astype(jnp.bfloat16)
    grad_self_att = jnp.where(valid_mask, grad_self_att, jnp.zeros_like(grad_self_att))
    grad_queries, grad_keys_self, grad_values_self = self_backward(
        queries, keys_self, values_self, allowed, log_self, grad_self_att
    )
    grad_self_in = jnp.stack(
        [
            einsum_f("td,tk->dk", first_in, grad_queries),
            einsum_f("td,tk->dk", first_in, grad_keys_self),
            einsum_f("td,tk->dk", first_in, grad_values_self),
        ]
    )
    grad_self_bias = jnp.stack(
        [
            jnp.sum(grad_queries.astype(jnp.float32), axis=0),
            jnp.sum(grad_values_self.astype(jnp.float32), axis=0),
        ]
    )
    first_terms = (
        einsum_f("tk,dk->td", grad_queries, self_in[0])
        + einsum_f("tk,dk->td", grad_keys_self, self_in[1])
        + einsum_f("tk,dk->td", grad_values_self, self_in[2])
    )
    grad_first = lax.psum(first_terms.astype(jnp.bfloat16), "mp").astype(jnp.float32)
    back_one, gain_one, shift_one = norm_back(normed_one, scale_one, ln_gain[0], grad_first)
    input_grad = (grad_one + back_one).astype(jnp.bfloat16)
    sum_self_in, sum_self_out, sum_cross_q, sum_cross_kv, sum_cross_out, sum_mlp_in, sum_mlp_out = (
        lax.psum_scatter(grad_self_in, "dp", scatter_dimension=1, tiled=True),
        lax.psum_scatter(grad_self_out, "dp", scatter_dimension=1, tiled=True),
        lax.psum_scatter(grad_cross_q, "dp", scatter_dimension=0, tiled=True),
        lax.psum_scatter(grad_cross_kv, "dp", scatter_dimension=1, tiled=True),
        lax.psum_scatter(grad_cross_out, "dp", scatter_dimension=1, tiled=True),
        lax.psum_scatter(grad_mlp_in, "dp", scatter_dimension=0, tiled=True),
        lax.psum_scatter(grad_mlp_out, "dp", scatter_dimension=1, tiled=True),
    )
    (
        sum_gain,
        sum_shift,
        sum_self_bias,
        sum_self_out_bias,
        sum_cross_bias,
        sum_cross_out_bias,
        sum_mlp_in_bias,
        sum_mlp_out_bias,
    ) = lax.psum(
        (
            jnp.stack([gain_one, gain_two, gain_three]),
            jnp.stack([shift_one, shift_two, shift_three]),
            grad_self_bias,
            grad_self_out_bias,
            grad_cross_bias,
            grad_cross_out_bias,
            grad_mlp_in_bias,
            grad_mlp_out_bias,
        ),
        "dp",
    )
    return (
        mixed,
        input_grad,
        memory_grad,
        sum_gain,
        sum_shift,
        sum_self_in,
        sum_self_bias,
        sum_self_out,
        sum_self_out_bias,
        sum_cross_q,
        sum_cross_kv,
        sum_cross_bias,
        sum_cross_out,
        sum_cross_out_bias,
        sum_mlp_in,
        sum_mlp_in_bias,
        sum_mlp_out,
        sum_mlp_out_bias,
    )


def solution(mesh):
    in_specs = (
        P("dp", None),
        P("dp", "mp", None),
        P("dp"),
        P("dp", None),
        P(),
        P(),
        P(None, None, "mp"),
        P(None, "mp"),
        P("mp", None),
        P(),
        P(None, "mp"),
        P(None, None, "mp"),
        P(None, "mp"),
        P("mp", None),
        P(),
        P(None, "mp"),
        P("mp"),
        P("mp", None),
        P(),
    )
    out_specs = (
        P("dp", None),
        P("dp", None),
        P("dp", "mp", None),
        P(),
        P(),
        P(None, "dp", "mp"),
        P(None, "mp"),
        P("mp", "dp"),
        P(),
        P("dp", "mp"),
        P(None, "dp", "mp"),
        P(None, "mp"),
        P("mp", "dp"),
        P(),
        P("dp", "mp"),
        P("mp"),
        P("mp", "dp"),
        P(),
    )
    shape = dict(mesh.shape)
    run = fused if (shape["dp"], shape["mp"]) == (8, 4) else body
    return jax.shard_map(run, mesh=mesh, in_specs=in_specs, out_specs=out_specs, check_vma=False)
```

```python
import math

import jax
import jax.numpy as jnp
from jax import lax
from jax.experimental import pallas as pl
from jax.experimental.pallas import tpu as pltpu
from jax.sharding import PartitionSpec as P

HD = 64
D, HW, T, TA, FQ, FP, AB, PB = 768, 192, 512, 448, 375, 384, 112, 32
NH = HW // HD
FT, TH = 2 * FP, T // 2
CH, CW = 2 * NH, 2 * HW
BF, F32 = jnp.bfloat16, jnp.float32
VMEM_LIMIT = 62 << 20


def nn(a, b):
    return lax.dot_general(a, b, (((1,), (0,)), ((), ())), preferred_element_type=F32)


def nt(a, b):
    return lax.dot_general(a, b, (((1,), (1,)), ((), ())), preferred_element_type=F32)


def tn(a, b):
    return lax.dot_general(a, b, (((0,), (0,)), ((), ())), preferred_element_type=F32)


def ds(start, size, step=16):
    return pl.ds(pl.multiple_of(start, step), size)


def colsum(values):
    return jnp.sum(values, axis=0, keepdims=True)


def normed(values):
    average = jnp.mean(values, axis=-1, keepdims=True)
    centred = values - average
    variance = jnp.mean(centred * centred, axis=-1, keepdims=True)
    inv = lax.rsqrt(variance + 1e-05)
    return centred * inv, inv


def layer_kernel(
    tok, mem, lens, cot, gains, shifts, w_si, self_bias, w_so, so_bias, w_cq, w_ck, cross_bias, w_co,
    co_bias, w_mi, mi_bias, w_mo, mo_bias,
    mixed_o, igrad_o, mgrad_o, grads_o, small_o,
    T_, G_, len_, qb_, qn_, si, so, cq, ck, co, mi, mo, slab,
    x1, q_, k_, v_, ps_, satt, sat2, m1, x2, cq_, K_, V_, pc_, catt, m2, x3, act, gh,
    ups, dO, dOf, dsb, gkv, gcq, upo, dOs, gqkv,
    oS, oR, stS, stR, ff, gqS, gqR,
    pS, pR, zS, zR, fin,
    mtS, mtR, mtF,
    gb, gR, gFr, gkb, gRb, gkS, gkR, gO, sb, sR, sX, sZ,
    lsem, ssem, rsem,
):
    d, z = lax.axis_index("dp"), lax.axis_index("mp")
    c = lax.rem(d, 2)
    p = z // 2
    chip = d // 2
    native = c == p
    foreign = jnp.logical_not(native)
    flip = lambda a, bit: a + bit * (1 - 2 * lax.rem(a // bit, 2))
    z1, z2 = flip(z, 1), flip(z, 2)
    z3 = flip(z2, 1)
    q = jnp.where(native, z, z2)
    q1 = flip(q, 1)
    block = lax.rem(z, 2)
    low_chip = block == 0
    dc, dx, dy = flip(d, 1), flip(d, 2), flip(d, 4)
    dd = flip(dx, 4)
    C, Zp, Fz, F3, CF = (dc, z), (d, z1), (d, z2), (d, z3), (dc, z2)
    X, Y, XY = (dx, z), (dy, z), (dd, z)
    CZ = (dc, z1)
    plane = ((X, dx // 2), (Y, dy // 2), (XY, dd // 2))
    MESH = pl.DeviceIdType.MESH
    barrier = pltpu.get_barrier_semaphore()
    all_peers = (C, Zp, Fz, F3, CF, CZ, X, Y, XY)
    for peer in all_peers:
        pl.semaphore_signal(barrier, inc=1, device_id=peer, device_id_type=MESH)

    counter = [0, 0]
    drains = []

    def remote(src, dst, dev, when=None):
        i = counter[0]
        counter[0] += 1
        copy = pltpu.make_async_remote_copy(
            src_ref=src, dst_ref=dst, send_sem=ssem.at[i], recv_sem=rsem.at[i],
            device_id=dev, device_id_type=MESH,
        )
        drains.append((copy, when))
        return copy

    def local(src, dst):
        i = counter[1]
        counter[1] += 1
        return pltpu.make_async_copy(src, dst, lsem.at[i])

    def loop(count, fn):
        def step(i, carry):
            fn(i)
            return carry

        lax.fori_loop(0, count, step, 0)

    row = lambda ref: ref[...].astype(F32).reshape(1, D)
    gain = lambda i: gains[i : i + 1, :]
    shift = lambda i: shifts[i : i + 1, :]

    rc_tok = remote(tok, T_, C, "n")
    rc_len = remote(len_, len_, C, "n")
    rc_cot = remote(cot, G_, C, "n")
    rc_qb = remote(qb_, qb_, Fz, "n")
    rc_sat = remote(sat2, satt, CF, "f")
    rc_qn = remote(qb_, qn_, Zp, "n")
    rc_qf = remote(qb_, qn_, Zp, "f")
    weights = {}
    nears = {}

    def weight(name, src, dst, both_quarters):
        size = src.shape[0] // 4
        base = block * src.shape[0] if both_quarters else 0
        at = lambda ref, start: ref.at[ds(start + chip * size, size), :]
        first = remote(at(src, 0), at(dst, base), Fz, "n")
        spread = [remote(at(dst, base), at(dst, base), dev, "f") for dev, _ in plane]
        whole = dst.at[ds(base, src.shape[0]), :] if both_quarters else dst
        weights[name] = (first, spread, local(src, whole))
        if both_quarters:
            near = (1 - block) * src.shape[0]
            nears[name] = (
                remote(at(src, 0), at(dst, base), Zp, "n"),
                remote(at(dst, base), at(dst, base), Zp, "f"),
                [remote(at(dst, near), at(dst, near), dev) for dev, _ in plane],
            )

    for name, src, dst, both_quarters in (
        ("so", w_so, so, False), ("ck", w_ck, ck, True), ("cq", w_cq, cq, True), ("co", w_co, co, True),
        ("mo", w_mo, mo, False), ("mi", w_mi, mi, False), ("si", w_si, si, False),
    ):
        weight(name, src, dst, both_quarters)
    own_tok, own_si = act, gb.at[0, 0 : 3 * HW, :]
    lc_tok, lc_cot, lc_own, lc_own_si = local(tok, T_), local(cot, G_), local(tok, own_tok), local(w_si, own_si)
    rc_mem = remote(mem, slab.at[1], Fz, "f")
    lc_mem = local(mem, slab.at[0])
    rc_mc = [remote(slab.at[s], slab.at[s], C, "n") for s in range(2)]

    def spread_weight(name):
        first, spread, loc = weights[name]
        first.wait_recv()
        for copy in spread:
            copy.start()
        if name in nears:
            nears[name][1].start()

    def spread_near(role):
        for name in ("ck", "cq", "co"):
            nears[name][role].wait_recv()
            for copy in nears[name][2]:
                copy.start()

    def need_weight(name):
        first, spread, loc = weights[name]

        @pl.when(native)
        def _():
            loc.wait()

        @pl.when(foreign)
        def _():
            for copy in spread:
                copy.wait_recv()

        if name in nears:
            for copy in nears[name][2]:
                copy.wait_recv()

    lc_own.start()
    lc_own_si.start()

    @pl.when(native)
    def _():
        lc_mem.start()
        for copy in [weights[n][2] for n in ("so", "ck")] + [lc_tok, lc_cot]:
            copy.start()
        for n in ("cq", "co", "mo", "mi", "si"):
            weights[n][2].start()
        len_[...] = jnp.broadcast_to(lens[...].astype(F32).reshape(1, 1), (8, 128))
        qb_[0:2, 0:HW] = self_bias[...].astype(F32)
        qb_[2:4, 0:HW] = cross_bias[...].astype(F32)
        qb_[4:5, :] = row(mi_bias)

    pl.semaphore_wait(barrier, len(all_peers))

    @pl.when(native)
    def _():
        for name in ("so", "ck", "cq", "co"):
            weights[name][0].start()
            if name != "so":
                nears[name][0].start()
        rc_qb.start()
        rc_qn.start()
        rc_len.start()
        lc_mem.wait()
        rc_mc[0].start()
        rc_tok.start()
        rc_cot.start()

    @pl.when(foreign)
    def _():
        rc_mem.start()

    def ln0(src):
        def part(i):
            rows = ds(i * AB, AB)
            n, _ = normed(src[rows, :].astype(F32))
            x1[rows, :] = (n * gain(0) + shift(0)).astype(BF)

        loop(TA // AB, part)

    def heads_to(ref, rows, values, first=0):
        for h in range(values.shape[1] // HD):
            ref[first + h, rows, :] = values[:, h * HD : (h + 1) * HD].astype(BF)

    def qkv(proj, bias):
        def part(i):
            rows = ds(i * AB, AB)
            values = nt(x1[rows, :], proj[...])
            heads_to(q_, rows, values[:, 0:HW] + bias[0:1, 0:HW].astype(F32))
            heads_to(k_, rows, values[:, HW : 2 * HW])
            heads_to(v_, rows, values[:, 2 * HW :] + bias[1:2, 0:HW].astype(F32))

        loop(TA // AB, part)

    def row_ids(start):
        return (start + lax.broadcasted_iota(jnp.int32, (AB, 1), 0)).astype(F32)

    self_cols = lax.broadcasted_iota(jnp.int32, (1, TA), 1).astype(F32)

    def self_fwd(limit, dst):
        def part(i):
            start = i * AB
            rows = ds(start, AB)
            ids = row_ids(start)
            valid = ids < limit
            allowed = (self_cols <= ids) & valid
            outs = []
            for h in range(NH):
                s = nt(q_[h, rows, :], k_[h]) * 0.125
                s = jnp.where(allowed, s, -1000000000.0)
                e = jnp.exp(s - jnp.max(s, axis=-1, keepdims=True))
                pb = (e * (1.0 / jnp.sum(e, axis=-1, keepdims=True))).astype(BF)
                ps_[h, rows, :] = pb
                if dst is not None:
                    outs.append(nn(pb, v_[h]))
            if dst is not None:
                dst[rows, :] = jnp.where(valid, jnp.concatenate(outs, axis=1), 0.0).astype(BF)

        loop(TA // AB, part)

    lc_own.wait()
    ln0(own_tok)
    lc_own_si.wait()
    qkv(own_si, self_bias)

    @pl.when(foreign)
    def _():
        spread_weight("so")
        spread_weight("ck")

    @pl.when(native)
    def _():
        spread_near(0)

    self_fwd(lens[...].astype(F32).reshape(1, 1), sat2)

    @pl.when(native)
    def _():
        satt[...] = sat2[...]
        lc_tok.wait()

    @pl.when(foreign)
    def _():
        rc_sat.start()
        spread_weight("cq")
        spread_weight("co")
        rc_tok.wait_recv()
        rc_len.wait_recv()
        rc_qb.wait_recv()
        rc_qf.start()
        rc_sat.wait_recv()

    length = len_[0:1, 0:1]
    valid_rows = row_ids

    size_of = (AB, AB, PB)
    lrows = lambda j: slice(j * AB, j * AB + size_of[j])
    gstart = lambda h, j: h * (TA // 2) + j * AB if j < 2 else TA + h * PB
    grows = lambda h, j: ds(gstart(h, j), size_of[j])
    mine, other = c, 1 - c
    half = lambda t: c + t * (1 - 2 * c)
    slots = {}

    def sum_open(slot, count, chips=True):
        for copy in slots.get(slot, ()):
            copy.wait_send()
            drains[:] = [item for item in drains if item[0] is not copy]
        to_core = [remote(pS.at[slot, lrows(j), :], pR.at[slot, lrows(j), :], C) for j in range(count)]
        if not chips:
            slots[slot] = to_core
            return slot, to_core
        zslot = slot // 2
        to_chip = [remote(zS.at[zslot, lrows(j), :], zR.at[zslot, lrows(j), :], Zp) for j in range(count)]
        slots[slot] = to_core + to_chip
        return slot, to_core, to_chip

    def emit(opened, j, product, between=None):
        slot, to_core, to_chip = opened
        pS[slot, lrows(j), :] = product(grows(other, j)).astype(BF)
        to_core[j].start()
        own = product(grows(mine, j))
        if between is not None:
            between()
        to_core[j].wait_recv()
        zS[slot // 2, lrows(j), :] = (own + pR[slot, lrows(j), :].astype(F32)).astype(BF)
        to_chip[j].start()

    def take(opened, j):
        slot, to_core, to_chip = opened
        to_chip[j].wait_recv()
        return zS[slot // 2, lrows(j), :].astype(F32) + zR[slot // 2, lrows(j), :].astype(F32)

    def share(ref, j):
        copy = remote(ref.at[grows(mine, j), :], ref.at[grows(mine, j), :], C)
        copy.start()
        return copy

    def both(copy, fn):
        def part(t):
            @pl.when(t == 1)
            def _():
                copy.wait_recv()

            fn(half(t))

        loop(2, part)

    def pass_memory():
        @pl.when(native)
        def _():
            rc_mem.wait_recv()
            rc_mc[1].start()
            for name in ("mo", "mi", "si"):
                weights[name][0].start()

    ar1 = sum_open(0, 2)
    need_weight("so")
    emit(ar1, 0, lambda rows: nn(satt[rows, :], so[...]))
    emit(ar1, 1, lambda rows: nn(satt[rows, :], so[...]), pass_memory)

    @pl.when(foreign)
    def _():
        spread_near(1)
        rc_qf.wait_recv()

    @pl.when(native)
    def _():
        rc_qn.wait_recv()

    for h in range(CH):
        for s in range(2):
            K_[h, (s + 1) * FP - 16 : (s + 1) * FP, :] = jnp.zeros((16, HD), BF)
            V_[h, (s + 1) * FP - 16 : (s + 1) * FP, :] = jnp.zeros((16, HD), BF)

    def pair_bias(i):
        mine_, near_ = qb_[i : i + 1, 0:HW], qn_[i : i + 1, 0:HW]
        return jnp.where(low_chip, mine_, near_), jnp.where(low_chip, near_, mine_)

    q_bias = jnp.concatenate(pair_bias(2), axis=1)
    v_bias = pair_bias(3)
    need_weight("ck")
    for s in range(2):
        @pl.when(foreign)
        def _():
            rc_mc[s].wait_recv()

        out = slice(s * FP, s * FP + FQ)
        values = nt(slab[s], ck[...])
        for i in range(2):
            heads_to(K_, out, values[:, 2 * i * HW : (2 * i + 1) * HW], i * NH)
            heads_to(V_, out, values[:, (2 * i + 1) * HW : (2 * i + 2) * HW] + v_bias[i], i * NH)

    need_weight("cq")
    frame = lax.broadcasted_iota(jnp.int32, (1, FT), 1)
    frame_ok = lax.rem(frame, FP) < FQ

    def cross_fwd(h_, j):
        rows = ds(gstart(h_, j), AB)
        heads_to(cq_, rows, nt(x2[rows, :], cq[...]) + q_bias)
        outs, tops, totals = [], [], []
        for h in range(CH):
            s = nt(cq_[h, rows, :], K_[h]) * 0.125
            s = jnp.where(frame_ok, s, -3e38)
            top = jnp.max(s, axis=-1, keepdims=True)
            e = jnp.exp(s - top)
            total = jnp.sum(e, axis=-1, keepdims=True)
            pb = (e * (1.0 / total)).astype(BF)
            pc_[h, rows, :] = pb
            outs.append(nn(pb, V_[h]))
            tops.append(top)
            totals.append(total)
        oS[2 * j + h_] = jnp.concatenate(outs, axis=1).astype(BF)
        filler = [jnp.ones((AB, 8 - CH), F32)]
        stats = jnp.concatenate(tops + filler + totals + filler + [jnp.ones((AB, 112), F32)], axis=1)
        stS[2 * j + h_] = jnp.concatenate([stats, jnp.ones((16, 128), F32)], axis=0).T[0:16, :]

    def merge(h_, j):
        i = 2 * j + h_
        start = gstart(h_, j)
        rows = ds(start, AB)
        a, b = stS[i], stR[i]
        low, high = jnp.where(low_chip, a, b), jnp.where(low_chip, b, a)
        top = jnp.maximum(low[0:8], high[0:8])
        w_low, w_high = low[8:16] * jnp.exp(low[0:8] - top), high[8:16] * jnp.exp(high[0:8] - top)
        part = w_low / (w_low + w_high)
        spread_part = jnp.concatenate([part, jnp.ones((120, 128), F32)], axis=0).T[0:AB, :]
        ff[rows, :] = jnp.where(low_chip, spread_part, 1.0 - spread_part)
        wide = jnp.concatenate(
            [jnp.broadcast_to(spread_part[:, h : h + 1], (AB, HD)) for h in range(CH)], axis=1
        )
        me, near = oS[i].astype(F32), oR[i].astype(F32)
        att = jnp.where(low_chip, me, near) * wide + jnp.where(low_chip, near, me) * (1.0 - wide)
        catt[rows, :] = jnp.where(valid_rows(start) < length, att, 0.0).astype(BF)

    def to_near(j, src, dst):
        copy = remote(src.at[2 * j : 2 * j + 2], dst.at[2 * j : 2 * j + 2], Zp)
        copy.start()
        return copy

    def core_sum(opened, j, product):
        slot, to_core = opened
        pS[slot, lrows(j), :] = product(grows(other, j)).astype(BF)
        to_core[j].start()
        own = product(grows(mine, j))
        to_core[j].wait_recv()
        return own + pR[slot, lrows(j), :].astype(F32)

    near_att = []

    @pl.when(foreign)
    def _():
        spread_weight("mo")

    ar2 = sum_open(1, 2, chips=False)
    for j in range(2):
        own = grows(mine, j)
        value = T_[own, :].astype(F32) + take(ar1, j) + row(so_bias)
        m1[lrows(j), :] = value
        n, _ = normed(value)
        x2[own, :] = (n * gain(1) + shift(1)).astype(BF)
        both(share(x2, j), lambda h: cross_fwd(h, j))
        near_att.append((to_near(j, oS, oR), to_near(j, stS, stR)))

        if j == 0:
            @pl.when(foreign)
            def _():
                spread_weight("mi")

    @pl.when(native)
    def _():
        lc_cot.wait()

    @pl.when(foreign)
    def _():
        rc_cot.wait_recv()

    need_weight("mo")

    def grad_active(i):
        rows = ds(i * 128, 128)
        fin[rows, :] = nt(G_[rows, :], mo[...])

    loop(T // 128, grad_active)
    need_weight("mi")
    need_weight("co")

    def mlp(rows):
        hidden = nn(x3[rows, :], mi[...]) + qb_[4:5, :]
        phi = 0.5 * (1.0 + lax.erf(hidden * (0.5**0.5)))
        density = jnp.exp(-0.5 * hidden * hidden) * (1.0 / math.sqrt(2.0 * math.pi))
        act[rows, :] = (hidden * phi).astype(BF)
        gh[rows, :] = (fin[rows, :] * (phi + hidden * density)).astype(BF)

    ar3 = sum_open(0, 3)
    for j in (2, 0, 1):
        own = grows(mine, j)
        if j == 2:
            value = T_[own, :].astype(F32) + row(so_bias) + row(co_bias)
        else:
            for copy in near_att[j]:
                copy.wait_recv()
            loop(2, lambda h: merge(h, j))
            value = core_sum(ar2, j, lambda rows: nn(catt[rows, :], co[...])) + m1[lrows(j), :] + row(co_bias)
        m2[lrows(j), :] = value
        n, _ = normed(value)
        x3[own, :] = (n * gain(2) + shift(2)).astype(BF)
        both(share(x3, j), lambda h: mlp(grows(h, j)))
        emit(ar3, j, lambda rows: nt(gh[rows, :], mi[...]))
        if j == 2:
            @pl.when(foreign)
            def _():
                spread_weight("si")


    gsends = {}

    def plane_send(m):
        gsends[m] = [
            remote(gb.at[m, ds(kk * 192, 192), :], gR.at[m, s], dev)
            for s, (dev, kk) in enumerate(plane)
        ]
        for copy in gsends[m]:
            copy.start()

    thirds = [slice(i * 256, (i + 1) * 256) for i in range(3)]
    for cols in thirds:
        gb[0, cols, :] = tn(x3[:, cols], gh[...]).astype(BF)
    plane_send(0)
    arm = sum_open(2, 3)
    for j in range(3):
        emit(arm, j, lambda rows: nn(act[rows, :], mo[...]))
    for cols in thirds:
        gb[1, cols, :] = tn(G_[:, cols], act[...]).astype(BF)
    plane_send(1)
    mi_sums = colsum(gh[...].astype(F32))

    need_weight("si")

    @pl.when(foreign)
    def _():
        ln0(T_)
        qkv(si, qb_)
        self_fwd(length, None)

    zero_row = jnp.zeros((1, D), F32)
    g_gain, g_shift = [zero_row] * 3, [zero_row] * 3
    b_out = [zero_row] * 3

    def norm_back(value, upstream, i):
        n, inv = normed(value)
        a = upstream * gain(i)
        g_gain[i] = g_gain[i] + colsum(upstream * n)
        g_shift[i] = g_shift[i] + colsum(upstream)
        return inv * (a - jnp.mean(a, axis=-1, keepdims=True) - n * jnp.mean(a * n, axis=-1, keepdims=True))

    def third_back(j):
        g = G_[grows(mine, j), :].astype(F32)
        b_out[2] = b_out[2] + colsum(g)
        value = g + norm_back(m2[lrows(j), :], take(ar3, j), 2)
        low = value.astype(BF)
        b_out[1] = b_out[1] + colsum(low.astype(F32))
        fin[lrows(j), :] = value
        return low

    def cross_bwd(h_, j):
        start = gstart(h_, j)
        rows = ds(start, AB)
        valid = valid_rows(start) < length
        grads = jnp.where(valid, nt(ups[rows, :], co[...]), 0.0).astype(BF)
        heads_to(dO, rows, grads)
        weighted = grads.astype(F32) * catt[rows, :].astype(F32)
        outs = []
        for h in range(CH):
            cols = slice(h * HD, (h + 1) * HD)
            factor = ff[rows, h : h + 1]
            dOf[h, rows, :] = (grads[:, cols].astype(F32) * factor).astype(BF)
            delta = jnp.sum(weighted[:, cols], axis=-1, keepdims=True)
            dp_ = nt(dO[h, rows, :], V_[h])
            dsv = (pc_[h, rows, :].astype(F32) * ((dp_ - delta) * factor)).astype(BF)
            dsb[h, rows, :] = dsv
            outs.append(nn(dsv, K_[h]) * 0.125)
        gqS[2 * j + h_] = jnp.concatenate(outs, axis=1).astype(BF)

    outs = []

    def give(slot, out_ref):
        from_n, from_f, to_core, onward = [], [], [], []
        for lo, hi, step, size in ((0, 0, TA // 2, AB), (2 * AB, TA, PB, PB // 2)):
            src = gO.at[slot, ds(lo + block * size, size), :]
            dst = out_ref.at[ds(hi + c * step + block * size, size), :]
            from_n.append(remote(src, dst, Fz, "n"))
            from_f.append(remote(src, dst, CF, "f"))
            both_rows = out_ref.at[ds(hi + c * step, 2 * size), :]
            to_core.append(remote(gO.at[slot, lo : lo + 2 * size, :], both_rows, C, "f"))
            for h in range(2):
                rows = out_ref.at[ds(hi + h * step + block * size, size), :]
                onward.append(remote(rows, rows, Zp, "f"))

        @pl.when(native)
        def _():
            for copy in from_n:
                copy.start()
            for j in range(3):
                out_ref[grows(mine, j), :] = gO[slot, lrows(j), :]

        @pl.when(foreign)
        def _():
            for copy in from_f + to_core:
                copy.start()

        outs.append((from_n, from_f, to_core, onward))

    def pass_on(slot):
        from_n, from_f, to_core, onward = outs[slot]

        @pl.when(foreign)
        def _():
            for copy in from_n + from_f:
                copy.wait_recv()
            for copy in onward:
                copy.start()

    def give_mixed():
        for j in range(3):
            value = m2[lrows(j), :] + take(arm, j) + row(mo_bias)
            gO[0, lrows(j), :] = value.astype(BF)
        give(0, mixed_o)

    ar4 = sum_open(1, 2, chips=False)
    near_queries = []
    for j in range(2):
        ups[grows(mine, j), :] = third_back(j)
        both(share(ups, j), lambda h: cross_bwd(h, j))
        near_queries.append(to_near(j, gqS, gqR))
        if j == 0:
            give_mixed()

    finals = {}
    own_piece = ds(chip * 192, 192)
    for m in range(4):
        finals[m] = (
            remote(gb.at[m, own_piece, :], gFr.at[m], Fz, "f"),
            remote(fin.at[m * 96 : (m + 1) * 96, :], grads_o.at[m], C, "n"),
        )

    def piece_sum(m):
        piece = gb[m, own_piece, :].astype(F32)
        for s in range(3):
            gsends[m][s].wait_recv()
            piece = piece + gR[m, s].astype(F32)
        if m == 2:
            rc_gk.wait_recv()
            piece = piece + jnp.concatenate(
                [jnp.zeros((192, HW), F32), gkR[...].astype(F32), jnp.zeros((192, HW), F32)], axis=1
            )
        return piece

    def piece_out(m):
        @pl.when(foreign)
        def _():
            gb[m, own_piece, :] = piece_sum(m).astype(BF)
            finals[m][0].start()

    def piece_final(m):
        @pl.when(native)
        def _():
            piece = piece_sum(m)
            finals[m][0].wait_recv()
            whole = piece + gFr[m].astype(F32)
            fin[m * 96 : (m + 1) * 96, :] = jnp.where(c == 0, whole[96:192, :], whole[0:96, :])
            finals[m][1].start()
            grads_o[m] = jnp.where(c == 0, whole[0:96, :], whole[96:192, :])

    pad_low = third_back(2)
    b_out[0] = b_out[0] + colsum(pad_low.astype(F32))
    piece_out(0)

    def kv_grad(i):
        rows = ds(i * FP, FP)
        frames = ds(i * FP, FP, 128)
        parts = []
        for first in (0, NH):
            heads = range(first, first + NH)
            parts += [tn(dsb[h, :, frames], cq_[h]) * 0.125 for h in heads]
            parts += [tn(pc_[h, :, frames], dOf[h]) for h in heads]
        gkv[rows, :] = jnp.concatenate(parts, axis=1).astype(BF)

    loop(2, kv_grad)

    def mem_term(s):
        return nn(gkv[ds(s * FP, FP), :], ck[...])[0:FQ]

    my_frames = jnp.where(native, 0, 1)
    mt_core = remote(mtS, mtR, C)
    mt_out = remote(mtF, mgrad_o, CF, "f")
    mtS[...] = mem_term(1 - my_frames).astype(BF)
    mt_core.start()
    own_term = mem_term(my_frames)
    mt_core.wait_recv()
    mtF[...] = (own_term + mtR[...].astype(F32)).astype(BF)

    @pl.when(native)
    def _():
        mgrad_o[...] = mtF[...]

    @pl.when(foreign)
    def _():
        mt_out.start()

    pick = lambda a, w: (jnp.where(low_chip, a[:, 0:w], a[:, w:]), jnp.where(low_chip, a[:, w:], a[:, 0:w]))
    catt_mine = pick(catt[...], HW)[0]
    for cols in thirds:
        kv_part = tn(slab[0, :, cols], gkv[0:FQ, :]) + tn(slab[1, :, cols], gkv[FP : FP + FQ, :])
        kv_mine, kv_near = pick(kv_part, CW)
        gb[2, cols, HW : 3 * HW] = kv_mine.astype(BF)
        gb[2, cols, 3 * HW :] = tn(ups[:, cols], catt_mine).astype(BF)
        gkb[cols, :] = kv_near.astype(BF)
    near_sends = [
        remote(gkb.at[ds(kk * 192, 192), :], gRb.at[s], dev) for s, (dev, kk) in enumerate(plane)
    ]
    for copy in near_sends:
        copy.start()
    rc_gk = remote(gkS, gkR, Zp)
    pass_on(0)
    piece_out(1)

    def self_bwd(start):
        rows = ds(start, AB)
        valid = valid_rows(start) < length
        heads_to(dOs, rows, jnp.where(valid, nt(upo[rows, :], so[...]), 0.0))
        outs = []
        for h in range(NH):
            dp_ = nt(dOs[h, rows, :], v_[h])
            pr = ps_[h, rows, :].astype(F32)
            dsv = (pr * (dp_ - jnp.sum(pr * dp_, axis=-1, keepdims=True))).astype(BF)
            dsb[h, rows, 0:TA] = dsv
            outs.append(nn(dsv, k_[h]) * 0.125)
        gqkv[rows, 0:HW] = jnp.concatenate(outs, axis=1).astype(BF)

    for j in range(2):
        own = grows(mine, j)
        near_queries[j].wait_recv()
        for h in range(2):
            both_rows = ds(gstart(h, j), AB)
            gcq[both_rows, :] = (gqS[2 * j + h].astype(F32) + gqR[2 * j + h].astype(F32)).astype(BF)
        upstream = core_sum(ar4, j, lambda rows: nn(gcq[rows, :], cq[...]))
        value = fin[lrows(j), :] + norm_back(m1[lrows(j), :], upstream, 1)
        low = value.astype(BF)
        b_out[0] = b_out[0] + colsum(low.astype(F32))
        upo[own, :] = low
        fin[TH + j * AB : TH + (j + 1) * AB, :] = value
        both(share(upo, j), lambda h: self_bwd(gstart(h, j)))
    gO[1, lrows(2), :] = pad_low
    kv = [tn(dsb[h, :, 0:TA], q_[h]) * 0.125 for h in range(NH)]
    kv += [tn(ps_[h], dOs[h]) for h in range(NH)]
    gqkv[:, HW:] = jnp.concatenate(kv, axis=1).astype(BF)

    gcq_mine = pick(gcq[...], HW)[0]
    for cols in thirds:
        gb[2, cols, 0:HW] = tn(x2[:, cols], gcq_mine).astype(BF)
    plane_send(2)
    for cols in thirds:
        left = tn(x1[:, cols], gqkv[...])
        right = tn(upo[:, cols], satt[...])
        gb[3, cols, :] = jnp.concatenate([left, right], axis=1).astype(BF)
    plane_send(3)
    last_core, last_chip = sum_open(0, 2)[1:]
    drains[:] = [item for item in drains if item[0] is not last_chip[1]]
    away, kept = 1 - block, block
    rows_of = lambda h, b: ds(h * (TA // 2) + b * AB, AB)
    last = None
    for step, b in enumerate((away, kept)):
        pS[0, lrows(step), :] = nn(gqkv[rows_of(other, b), :], si[...]).astype(BF)
        last_core[step].start()
        last = nn(gqkv[rows_of(mine, b), :], si[...])
        last_core[step].wait_recv()
        last = last + pR[0, lrows(step), :].astype(F32)
        if step == 0:
            zS[0, lrows(0), :] = last.astype(BF)
            last_chip[0].start()
    last_sum = last

    near_piece = gkb[own_piece, :].astype(F32)
    for s in range(3):
        near_sends[s].wait_recv()
        near_piece = near_piece + gRb[s].astype(F32)
    gkS[...] = near_piece.astype(BF)
    rc_gk.start()
    piece_out(2)
    piece_final(0)
    gs = gqkv[...].astype(F32)
    quarter = jnp.concatenate(
        [
            colsum(gs[:, 0:HW]),
            colsum(gs[:, 2 * HW :]),
            colsum(gcq_mine.astype(F32)),
            jnp.zeros((1, HW), F32),
        ],
        axis=1,
    )
    values_sum = pick(colsum(gkv[...].astype(F32)), CW)
    quarters = [jnp.concatenate([jnp.zeros((1, 3 * HW), F32), v[:, HW:]], axis=1) for v in values_sum]

    own = rows_of(mine, kept)
    last_chip[0].wait_recv()
    last_sum = last_sum + zR[0, lrows(0), :].astype(F32)
    value = fin[ds(TH + kept * AB, AB), :] + norm_back(T_[own, :].astype(F32), last_sum, 0)
    gO[1, 0:AB, :] = value.astype(BF)
    pads_at = lambda b: ds(TA + c * PB + b * (PB // 2), PB // 2)
    pad_src = gO.at[1, ds(2 * AB + block * (PB // 2), PB // 2), :]
    grad_src, grad_dst = gO.at[1, 0:AB, :], igrad_o.at[own, :]
    give_n = [remote(grad_src, grad_dst, dev, "n") for dev in (Fz, Zp)]
    give_f = [remote(grad_src, grad_dst, dev, "f") for dev in (CF, CZ, C)]
    pad_n = remote(pad_src, igrad_o.at[pads_at(block), :], Fz, "n")
    pad_f = remote(pad_src, igrad_o.at[pads_at(block), :], CF, "f")
    pad_c = remote(gO.at[1, 2 * AB : 2 * AB + PB, :], igrad_o.at[grows(mine, 2), :], C, "f")
    onward = []
    for h in range(2):
        for lo, size in ((h * (TA // 2) + block * AB, AB), (TA + h * PB + block * (PB // 2), PB // 2)):
            rows = igrad_o.at[ds(lo, size), :]
            onward.append(remote(rows, rows, Zp, "f"))

    @pl.when(native)
    def _():
        for copy in give_n + [pad_n]:
            copy.start()
        igrad_o[own, :] = gO[1, 0:AB, :]
        igrad_o[grows(mine, 2), :] = pad_low

    @pl.when(foreign)
    def _():
        for copy in give_f + [pad_f, pad_c]:
            copy.start()

    def pass_grad():
        @pl.when(foreign)
        def _():
            give_n[0].wait_recv()
            give_f[0].wait_recv()
            pad_n.wait_recv()
            pad_f.wait_recv()
            for copy in onward:
                copy.start()

    ids = lax.broadcasted_iota(jnp.int32, (24, 1), 0)
    packed = jnp.zeros((24, D), F32)
    for i, values in enumerate(g_gain + g_shift + b_out):
        share_of = 1.0 if i in (0, 3) else 0.5
        packed = packed + jnp.where(ids == i, values * share_of, 0.0)
    packed = packed + jnp.where(ids == 9 + q, quarter + quarters[0], 0.0)
    packed = packed + jnp.where(ids == 9 + q1, quarters[1], 0.0) + jnp.where(ids == 13 + q, mi_sums, 0.0)
    sb[0] = packed
    small_c = remote(sb.at[0], sR, C)
    small_c.start()
    piece_final(1)
    small_c.wait_recv()
    sb[1] = sb[0] + sR[...]
    small_x = [remote(sb.at[1], sX.at[chip], dev) for dev, _ in plane]
    for copy in small_x:
        copy.start()
    sX[chip] = sb[1]
    piece_out(3)
    for copy in small_x:
        copy.wait_recv()
    sb[2] = sX[0] + sX[1] + sX[2] + sX[3]
    small_z = [remote(sb.at[2], sZ.at[z], dev) for dev in (Zp, Fz, F3)]
    for copy in small_z:
        copy.start()
    sZ[z] = sb[2]
    pass_grad()
    piece_final(2)
    for copy in small_z:
        copy.wait_recv()
    total = sZ[0] + sZ[1] + sZ[2] + sZ[3]
    small_o[0:9, :] = total[0:9, :]
    small_o[9:10, :] = colsum(jnp.where(ids == 9 + z, total, 0.0))
    small_o[10:11, :] = colsum(jnp.where(ids == 13 + z, total, 0.0))
    small_o[11:16, :] = jnp.zeros((5, D), F32)

    piece_final(3)

    @pl.when(foreign)
    def _():
        for m in range(4):
            finals[m][1].wait_recv()
        mt_out.wait_recv()
        for copy in outs[0][3] + onward:
            copy.wait_recv()

    @pl.when(native)
    def _():
        for copy in outs[0][2] + [give_n[1]] + give_f[1:] + [pad_c]:
            copy.wait_recv()

    for copy, when in drains:
        if when is None:
            copy.wait_send()

    @pl.when(native)
    def _():
        for copy, when in drains:
            if when == "n":
                copy.wait_send()

    @pl.when(foreign)
    def _():
        for copy, when in drains:
            if when == "f":
                copy.wait_send()


def finish_kernel(
    mixed_i, igrad_i, mgrad_i, grads, small,
    mixed_o, igrad_o, mgrad_o, gain_o, shift_o, si_o, sb_o, so_o, sob_o, cq_o, ck_o, cb_o, co_o, cob_o,
    mi_o, mib_o, mo_o, mob_o,
):
    mixed_o[...] = mixed_i[...]
    igrad_o[...] = igrad_i[...]
    mgrad_o[...] = mgrad_i[...]
    gain_o[...] = small[0:3, :]
    shift_o[...] = small[3:6, :]
    for i in range(3):
        si_o[i] = grads[3, :, i * HW : (i + 1) * HW]
    for i in range(2):
        sb_o[i : i + 1, :] = small[9:10, i * HW : (i + 1) * HW]
        cb_o[i : i + 1, :] = small[9:10, (i + 2) * HW : (i + 3) * HW]
        ck_o[i] = grads[2, :, (i + 1) * HW : (i + 2) * HW]
    so_o[...] = grads[3, :, 3 * HW :].T
    cq_o[...] = grads[2, :, 0:HW]
    co_o[...] = grads[2, :, 3 * HW :].T
    sob_o[...] = small[6]
    cob_o[...] = small[7]
    mob_o[...] = small[8]
    mib_o[...] = small[10]
    mi_o[...] = grads[0]
    mo_o[...] = grads[1]


def fused(
    tokens, memory, lengths, cotangent, ln_gain, ln_bias, self_in, self_bias, self_out,
    self_out_bias, cross_q, cross_kv, cross_bias, cross_out, cross_out_bias, mlp_in,
    mlp_in_bias, mlp_out, mlp_out_bias,
):
    vmem = pltpu.VMEM
    heads, frames = vmem((NH, TA, HD), BF), vmem((CH, FT, HD), BF)
    rows, low_rows, own_rows = vmem((T, D), BF), vmem((TA, D), BF), vmem((TH, D), F32)
    att = vmem((TA, HW), BF)
    probs, sums, memo = vmem((CH, TA, FT), BF), vmem((3, TH, D), BF), vmem((FQ, D), BF)
    chip_sums = vmem((2, TH, D), BF)
    heads6, two = vmem((CH, TA, HD), BF), vmem((4, AB, CW), BF)
    wide_w, att6 = vmem((CW, D), BF), vmem((TA, CW), BF)
    scratch = [
        rows, rows, vmem((8, 128), F32), vmem((8, D), F32), vmem((8, D), F32),
        vmem((3 * HW, D), BF), vmem((HW, D), BF), wide_w, vmem((2 * CW, D), BF), wide_w,
        vmem((D, D), BF), vmem((D, D), BF), vmem((2, FQ, D), BF),
        low_rows, heads, heads, heads, vmem((NH, TA, TA), BF), att, att, own_rows, low_rows,
        heads6, frames, frames, probs, att6, own_rows, rows, rows, rows,
        low_rows, heads6, heads6, probs, vmem((FT, 2 * CW), BF), att6, low_rows, heads, vmem((TA, 3 * HW), BF),
        two, two, vmem((4, 16, 128), F32), vmem((4, 16, 128), F32), vmem((TA, 128), F32), two, two,
        sums, sums, chip_sums, chip_sums, vmem((T, D), F32),
        memo, memo, memo,
        vmem((4, D, D), BF), vmem((4, 3, 192, D), BF), vmem((4, 192, D), BF),
        vmem((D, CW), BF), vmem((3, 192, CW), BF), vmem((192, CW), BF), vmem((192, CW), BF),
        vmem((2, TH, D), BF), vmem((3, 24, D), F32), vmem((24, D), F32),
        vmem((4, 24, D), F32), vmem((4, 24, D), F32),
        pltpu.SemaphoreType.DMA((16,)), pltpu.SemaphoreType.DMA((200,)), pltpu.SemaphoreType.DMA((200,)),
    ]
    hbm, on_chip = pl.BlockSpec(memory_space=pl.ANY), pl.BlockSpec(memory_space=pltpu.VMEM)
    shape = jax.ShapeDtypeStruct
    wide = [shape((T, D), BF), shape((T, D), BF), shape((FQ, D), BF)]
    h, v = hbm, on_chip
    parts = pl.pallas_call(
        layer_kernel,
        out_shape=wide + [shape((4, 96, D), F32), shape((16, D), F32)],
        in_specs=[h, h, v, h, v, v, h, v, h, v, h, h, v, h, v, h, v, h, v],
        out_specs=[on_chip] * 5,
        scratch_shapes=scratch,
        compiler_params=pltpu.CompilerParams(
            collective_id=0, has_side_effects=True, vmem_limit_bytes=VMEM_LIMIT
        ),
    )(
        tokens, memory[0], lengths, cotangent, ln_gain, ln_bias,
        jnp.swapaxes(self_in, 1, 2).reshape(3 * HW, D), self_bias, self_out, self_out_bias,
        cross_q.T, jnp.swapaxes(cross_kv, 1, 2).reshape(2 * HW, D), cross_bias, cross_out, cross_out_bias,
        mlp_in, mlp_in_bias, mlp_out, mlp_out_bias,
    )
    vec = shape((D,), F32)
    outs = list(pl.pallas_call(
        finish_kernel,
        out_shape=wide
        + [
            shape((3, D), F32), shape((3, D), F32), shape((3, 96, HW), F32), shape((2, HW), F32),
            shape((HW, 96), F32), vec, shape((96, HW), F32), shape((2, 96, HW), F32), shape((2, HW), F32),
            shape((HW, 96), F32), vec, shape((96, D), F32), vec, shape((96, D), F32), vec,
        ],
        in_specs=[on_chip] * 5,
        out_specs=[on_chip] * 18,
    )(*parts))
    outs[2] = outs[2][None]
    outs[16] = outs[16].T
    return tuple(outs)


def matmul(left, right):
    return jnp.dot(left, right, preferred_element_type=jnp.float32)


def einsum_f(form, left, right):
    return jnp.einsum(form, left, right, preferred_element_type=jnp.float32)


def norm_parts(values):
    average = jnp.mean(values, axis=-1, keepdims=True)
    centred = values - average
    variance = jnp.mean(centred * centred, axis=-1, keepdims=True)
    scale_inv = lax.rsqrt(variance + 1e-05)
    return (centred * scale_inv, scale_inv)


def norm_back(normed, scale_inv, gain, upstream):
    scaled = upstream * gain
    inner = (
        scaled
        - jnp.mean(scaled, axis=-1, keepdims=True)
        - normed * jnp.mean(scaled * normed, axis=-1, keepdims=True)
    )
    return (scale_inv * inner, jnp.sum(upstream * normed, axis=0), jnp.sum(upstream, axis=0))


def softmax_parts(scores):
    row_max = jnp.max(scores, axis=-1, keepdims=True)
    shifted = jnp.exp(scores - row_max)
    totals = jnp.sum(shifted, axis=-1, keepdims=True)
    return (shifted / totals, row_max[..., 0] + jnp.log(totals[..., 0]))


def gelu_exact(values):
    return jax.nn.gelu(values, approximate=False)


def self_forward(queries, keys_self, values_self, allowed, valid_mask):
    row_count, head_width = queries.shape
    head_count = head_width // HD
    query_heads = queries.reshape(row_count, head_count, HD)
    key_heads = keys_self.reshape(row_count, head_count, HD)
    value_heads = values_self.reshape(row_count, head_count, HD)
    scores = einsum_f("thd,shd->hts", query_heads, key_heads) * 0.125
    scores = jnp.where(allowed[None], scores, -1000000000.0)
    probs, log_total = softmax_parts(scores)
    attended = einsum_f("hts,shd->thd", probs.astype(jnp.bfloat16), value_heads).reshape(
        row_count, head_width
    )
    attended = jnp.where(valid_mask, attended, 0.0)
    return (attended.astype(jnp.bfloat16), log_total)


def self_backward(queries, keys_self, values_self, allowed, log_total, grad_out):
    row_count, head_width = queries.shape
    head_count = head_width // HD
    query_heads = queries.reshape(row_count, head_count, HD)
    key_heads = keys_self.reshape(row_count, head_count, HD)
    value_heads = values_self.reshape(row_count, head_count, HD)
    scores = einsum_f("thd,shd->hts", query_heads, key_heads) * 0.125
    scores = jnp.where(allowed[None], scores, -1000000000.0)
    probs = jnp.exp(scores - log_total[..., None])
    grad_heads = grad_out.reshape(row_count, head_count, HD)
    grad_values = einsum_f("hts,thd->shd", probs.astype(jnp.bfloat16), grad_heads)
    grad_probs = einsum_f("thd,shd->hts", grad_heads, value_heads)
    grad_scores = (
        probs * (grad_probs - jnp.sum(probs * grad_probs, axis=-1, keepdims=True))
    ).astype(jnp.bfloat16)
    grad_queries = einsum_f("hts,shd->thd", grad_scores, key_heads) * 0.125
    grad_keys = einsum_f("hts,thd->shd", grad_scores, query_heads) * 0.125
    return (
        grad_queries.reshape(row_count, head_width).astype(jnp.bfloat16),
        grad_keys.reshape(row_count, head_width).astype(jnp.bfloat16),
        grad_values.reshape(row_count, head_width).astype(jnp.bfloat16),
    )


def cross_forward(query_heads, memory_pairs, clip_of):
    row_count, head_count, _ = query_heads.shape
    head_width = head_count * HD
    clip_count = memory_pairs.shape[0]

    def per_clip(carry, clip_item):
        attended, log_rows = carry
        clip_index, clip_pairs = clip_item
        key_heads = clip_pairs[:, :head_width].reshape(-1, head_count, HD)
        value_heads = clip_pairs[:, head_width:].reshape(-1, head_count, HD)
        scores = einsum_f("thd,fhd->htf", query_heads, key_heads) * 0.125
        probs, log_total = softmax_parts(scores)
        result = einsum_f("htf,fhd->thd", probs.astype(jnp.bfloat16), value_heads).reshape(
            row_count, head_width
        )
        member = clip_of == clip_index
        return (
            (
                jnp.where(member[:, None], result, attended),
                jnp.where(member[None, :], log_total, log_rows),
            ),
            None,
        )

    start_carry = (
        jnp.zeros((row_count, head_width), jnp.float32),
        jnp.zeros((head_count, row_count), jnp.float32),
    )
    (attended, log_rows), _ = lax.scan(
        per_clip, start_carry, (jnp.arange(clip_count, dtype=jnp.int32), memory_pairs)
    )
    return (attended.astype(jnp.bfloat16), log_rows)


def cross_backward(query_heads, memory_pairs, clip_of, log_rows, grad_out):
    row_count, head_count, _ = query_heads.shape
    head_width = head_count * HD
    clip_count = memory_pairs.shape[0]

    def per_clip(grad_query, clip_item):
        clip_index, clip_pairs = clip_item
        frames = clip_pairs.shape[0]
        member = clip_of == clip_index
        key_heads = clip_pairs[:, :head_width].reshape(frames, head_count, HD)
        value_heads = clip_pairs[:, head_width:].reshape(frames, head_count, HD)
        scores = einsum_f("thd,fhd->htf", query_heads, key_heads) * 0.125
        probs = jnp.where(member[None, :, None], jnp.exp(scores - log_rows[:, :, None]), 0.0)
        grad_heads = jnp.where(member[:, None], grad_out, jnp.zeros_like(grad_out)).reshape(
            row_count, head_count, HD
        )
        grad_values = einsum_f("htf,thd->fhd", probs.astype(jnp.bfloat16), grad_heads)
        grad_probs = einsum_f("thd,fhd->htf", grad_heads, value_heads)
        grad_scores = (
            probs * (grad_probs - jnp.sum(probs * grad_probs, axis=-1, keepdims=True))
        ).astype(jnp.bfloat16)
        grad_query = grad_query + einsum_f("htf,fhd->thd", grad_scores, key_heads) * 0.125
        grad_keys = einsum_f("htf,thd->fhd", grad_scores, query_heads) * 0.125
        grad_pairs = jnp.concatenate(
            [grad_keys.reshape(frames, head_width), grad_values.reshape(frames, head_width)], axis=1
        )
        return (grad_query, grad_pairs.astype(jnp.bfloat16))

    grad_query, grad_pairs = lax.scan(
        per_clip,
        jnp.zeros((row_count, head_count, HD), jnp.float32),
        (jnp.arange(clip_count, dtype=jnp.int32), memory_pairs),
    )
    return (grad_query.reshape(row_count, head_width).astype(jnp.bfloat16), grad_pairs)


def body(
    tokens,
    memory,
    lengths,
    cotangent,
    ln_gain,
    ln_bias,
    self_in,
    self_bias,
    self_out,
    self_out_bias,
    cross_q,
    cross_kv,
    cross_bias,
    cross_out,
    cross_out_bias,
    mlp_in,
    mlp_in_bias,
    mlp_out,
    mlp_out_bias,
):
    row_count = tokens.shape[0]
    clip_count = lengths.shape[0]
    head_width = self_in.shape[2]
    head_count = head_width // HD
    clip_ends = jnp.cumsum(lengths)
    positions = jnp.arange(row_count, dtype=jnp.int32)
    clip_of = jnp.sum((positions[:, None] >= clip_ends[None, :]).astype(jnp.int32), axis=1)
    valid_mask = (clip_of < clip_count)[:, None]
    allowed = (
        (clip_of[:, None] == clip_of[None, :])
        & (positions[None, :] <= positions[:, None])
        & (clip_of[:, None] < clip_count)
    )
    inputs = tokens.astype(jnp.float32)
    normed_one, scale_one = norm_parts(inputs)
    first_in = (normed_one * ln_gain[0] + ln_bias[0]).astype(jnp.bfloat16)
    queries = (matmul(first_in, self_in[0]) + self_bias[0]).astype(jnp.bfloat16)
    keys_self = matmul(first_in, self_in[1]).astype(jnp.bfloat16)
    values_self = (matmul(first_in, self_in[2]) + self_bias[1]).astype(jnp.bfloat16)
    self_att, log_self = self_forward(queries, keys_self, values_self, allowed, valid_mask)
    mixed_one = inputs + lax.psum(matmul(self_att, self_out), "mp") + self_out_bias
    normed_two, scale_two = norm_parts(mixed_one)
    second_in = (normed_two * ln_gain[1] + ln_bias[1]).astype(jnp.bfloat16)
    cross_queries = (matmul(second_in, cross_q) + cross_bias[0]).astype(jnp.bfloat16)
    slab = lax.all_gather(memory, "mp", axis=1, tiled=True)
    slab_keys = einsum_f("cfd,de->cfe", slab, cross_kv[0]).astype(jnp.bfloat16)
    slab_values = (einsum_f("cfd,de->cfe", slab, cross_kv[1]) + cross_bias[1]).astype(jnp.bfloat16)
    memory_pairs = jnp.concatenate([slab_keys, slab_values], axis=2)
    query_heads = cross_queries.reshape(row_count, head_count, HD)
    cross_att, log_cross = cross_forward(query_heads, memory_pairs, clip_of)
    mixed_two = (
        mixed_one
        + lax.psum(matmul(cross_att, cross_out).astype(jnp.bfloat16), "mp").astype(jnp.float32)
        + cross_out_bias
    )
    normed_three, scale_three = norm_parts(mixed_two)
    third_in = (normed_three * ln_gain[2] + ln_bias[2]).astype(jnp.bfloat16)
    hidden = matmul(third_in, mlp_in) + mlp_in_bias
    active, gelu_back = jax.vjp(gelu_exact, hidden)
    active_low = active.astype(jnp.bfloat16)
    mixed = (
        mixed_two
        + lax.psum(matmul(active_low, mlp_out).astype(jnp.bfloat16), "mp").astype(jnp.float32)
        + mlp_out_bias
    ).astype(jnp.bfloat16)
    upstream = cotangent.astype(jnp.float32)
    grad_mlp_out = einsum_f("tf,td->fd", active_low, cotangent)
    grad_mlp_out_bias = jnp.sum(upstream, axis=0)
    grad_active = einsum_f("td,fd->tf", cotangent, mlp_out)
    grad_hidden = gelu_back(grad_active)[0].astype(jnp.bfloat16)
    grad_mlp_in = einsum_f("td,tf->df", third_in, grad_hidden)
    grad_mlp_in_bias = jnp.sum(grad_hidden.astype(jnp.float32), axis=0)
    grad_third = lax.psum(
        einsum_f("tf,df->td", grad_hidden, mlp_in).astype(jnp.bfloat16), "mp"
    ).astype(jnp.float32)
    back_three, gain_three, shift_three = norm_back(
        normed_three, scale_three, ln_gain[2], grad_third
    )
    grad_two = upstream + back_three
    up_two = grad_two.astype(jnp.bfloat16)
    grad_cross_out = einsum_f("tk,td->kd", cross_att, up_two)
    grad_cross_out_bias = jnp.sum(up_two.astype(jnp.float32), axis=0)
    grad_cross_att = einsum_f("td,kd->tk", up_two, cross_out).astype(jnp.bfloat16)
    grad_cross_att = jnp.where(valid_mask, grad_cross_att, jnp.zeros_like(grad_cross_att))
    grad_cross_queries, grad_pairs = cross_backward(
        query_heads, memory_pairs, clip_of, log_cross, grad_cross_att
    )
    grad_cross_q = einsum_f("td,tk->dk", second_in, grad_cross_queries)
    grad_query_bias = jnp.sum(grad_cross_queries.astype(jnp.float32), axis=0)
    grad_keys_cross = grad_pairs[:, :, :head_width]
    grad_values_cross = grad_pairs[:, :, head_width:]
    grad_cross_kv = jnp.stack(
        [
            einsum_f("cfd,cfe->de", slab, grad_keys_cross),
            einsum_f("cfd,cfe->de", slab, grad_values_cross),
        ]
    )
    grad_value_bias = jnp.sum(grad_values_cross.astype(jnp.float32), axis=(0, 1))
    memory_terms = einsum_f("cfe,de->cfd", grad_keys_cross, cross_kv[0]) + einsum_f(
        "cfe,de->cfd", grad_values_cross, cross_kv[1]
    )
    memory_grad = lax.psum_scatter(
        memory_terms.astype(jnp.bfloat16), "mp", scatter_dimension=1, tiled=True
    )
    grad_cross_bias = jnp.stack([grad_query_bias, grad_value_bias])
    grad_second = lax.psum(
        einsum_f("tk,dk->td", grad_cross_queries, cross_q).astype(jnp.bfloat16), "mp"
    ).astype(jnp.float32)
    back_two, gain_two, shift_two = norm_back(normed_two, scale_two, ln_gain[1], grad_second)
    grad_one = grad_two + back_two
    up_one = grad_one.astype(jnp.bfloat16)
    grad_self_out = einsum_f("tk,td->kd", self_att, up_one)
    grad_self_out_bias = jnp.sum(up_one.astype(jnp.float32), axis=0)
    grad_self_att = einsum_f("td,kd->tk", up_one, self_out).astype(jnp.bfloat16)
    grad_self_att = jnp.where(valid_mask, grad_self_att, jnp.zeros_like(grad_self_att))
    grad_queries, grad_keys_self, grad_values_self = self_backward(
        queries, keys_self, values_self, allowed, log_self, grad_self_att
    )
    grad_self_in = jnp.stack(
        [
            einsum_f("td,tk->dk", first_in, grad_queries),
            einsum_f("td,tk->dk", first_in, grad_keys_self),
            einsum_f("td,tk->dk", first_in, grad_values_self),
        ]
    )
    grad_self_bias = jnp.stack(
        [
            jnp.sum(grad_queries.astype(jnp.float32), axis=0),
            jnp.sum(grad_values_self.astype(jnp.float32), axis=0),
        ]
    )
    first_terms = (
        einsum_f("tk,dk->td", grad_queries, self_in[0])
        + einsum_f("tk,dk->td", grad_keys_self, self_in[1])
        + einsum_f("tk,dk->td", grad_values_self, self_in[2])
    )
    grad_first = lax.psum(first_terms.astype(jnp.bfloat16), "mp").astype(jnp.float32)
    back_one, gain_one, shift_one = norm_back(normed_one, scale_one, ln_gain[0], grad_first)
    input_grad = (grad_one + back_one).astype(jnp.bfloat16)
    sum_self_in, sum_self_out, sum_cross_q, sum_cross_kv, sum_cross_out, sum_mlp_in, sum_mlp_out = (
        lax.psum_scatter(grad_self_in, "dp", scatter_dimension=1, tiled=True),
        lax.psum_scatter(grad_self_out, "dp", scatter_dimension=1, tiled=True),
        lax.psum_scatter(grad_cross_q, "dp", scatter_dimension=0, tiled=True),
        lax.psum_scatter(grad_cross_kv, "dp", scatter_dimension=1, tiled=True),
        lax.psum_scatter(grad_cross_out, "dp", scatter_dimension=1, tiled=True),
        lax.psum_scatter(grad_mlp_in, "dp", scatter_dimension=0, tiled=True),
        lax.psum_scatter(grad_mlp_out, "dp", scatter_dimension=1, tiled=True),
    )
    (
        sum_gain,
        sum_shift,
        sum_self_bias,
        sum_self_out_bias,
        sum_cross_bias,
        sum_cross_out_bias,
        sum_mlp_in_bias,
        sum_mlp_out_bias,
    ) = lax.psum(
        (
            jnp.stack([gain_one, gain_two, gain_three]),
            jnp.stack([shift_one, shift_two, shift_three]),
            grad_self_bias,
            grad_self_out_bias,
            grad_cross_bias,
            grad_cross_out_bias,
            grad_mlp_in_bias,
            grad_mlp_out_bias,
        ),
        "dp",
    )
    return (
        mixed,
        input_grad,
        memory_grad,
        sum_gain,
        sum_shift,
        sum_self_in,
        sum_self_bias,
        sum_self_out,
        sum_self_out_bias,
        sum_cross_q,
        sum_cross_kv,
        sum_cross_bias,
        sum_cross_out,
        sum_cross_out_bias,
        sum_mlp_in,
        sum_mlp_in_bias,
        sum_mlp_out,
        sum_mlp_out_bias,
    )


def solution(mesh):
    in_specs = (
        P("dp", None),
        P("dp", "mp", None),
        P("dp"),
        P("dp", None),
        P(),
        P(),
        P(None, None, "mp"),
        P(None, "mp"),
        P("mp", None),
        P(),
        P(None, "mp"),
        P(None, None, "mp"),
        P(None, "mp"),
        P("mp", None),
        P(),
        P(None, "mp"),
        P("mp"),
        P("mp", None),
        P(),
    )
    out_specs = (
        P("dp", None),
        P("dp", None),
        P("dp", "mp", None),
        P(),
        P(),
        P(None, "dp", "mp"),
        P(None, "mp"),
        P("mp", "dp"),
        P(),
        P("dp", "mp"),
        P(None, "dp", "mp"),
        P(None, "mp"),
        P("mp", "dp"),
        P(),
        P("dp", "mp"),
        P("mp"),
        P("mp", "dp"),
        P(),
    )
    shape = dict(mesh.shape)
    run = fused if (shape["dp"], shape["mp"]) == (8, 4) else body
    return jax.shard_map(run, mesh=mesh, in_specs=in_specs, out_specs=out_specs, check_vma=False)
```

```python
import math

import jax
import jax.numpy as jnp
from jax import lax
from jax.experimental import pallas as pl
from jax.experimental.pallas import tpu as pltpu
from jax.sharding import PartitionSpec as P

HD = 64
D, HW, T, TA, FQ, FP, AB, PB = 768, 192, 512, 448, 375, 384, 112, 32
NH = HW // HD
FT, TH = 2 * FP, T // 2
CH, CW = 2 * NH, 2 * HW
BF, F32 = jnp.bfloat16, jnp.float32
VMEM_LIMIT = 62 << 20


def nn(a, b):
    return lax.dot_general(a, b, (((1,), (0,)), ((), ())), preferred_element_type=F32)


def nt(a, b):
    return lax.dot_general(a, b, (((1,), (1,)), ((), ())), preferred_element_type=F32)


def tn(a, b):
    return lax.dot_general(a, b, (((0,), (0,)), ((), ())), preferred_element_type=F32)


def ds(start, size, step=16):
    return pl.ds(pl.multiple_of(start, step), size)


def colsum(values):
    return jnp.sum(values, axis=0, keepdims=True)


def normed(values):
    average = jnp.mean(values, axis=-1, keepdims=True)
    centred = values - average
    variance = jnp.mean(centred * centred, axis=-1, keepdims=True)
    inv = lax.rsqrt(variance + 1e-05)
    return centred * inv, inv


def layer_kernel(
    tok, mem, lens, cot, gains, shifts, w_si, self_bias, w_so, so_bias, w_cq, w_ck, cross_bias, w_co,
    co_bias, w_mi, mi_bias, w_mo, mo_bias,
    mixed_o, igrad_o, mgrad_o, grads_o, small_o,
    T_, G_, len_, qb_, qn_, si, so, cq, ck, co, mi, mo, slab,
    x1, q_, k_, v_, ps_, satt, sat2, m1, x2, cq_, K_, V_, pc_, catt, m2, x3, act, gh,
    ups, dO, dOf, dsb, gkv, gcq, upo, dOs, gqkv,
    oS, oR, stS, stR, ff, gqS, gqR,
    pS, pR, zS, zR, fin,
    mtS, mtR, mtF,
    gb, gR, gFr, gkb, gRb, gkS, gkR, gO, sb, sR, sX, sZ,
    lsem, ssem, rsem,
):
    d, z = lax.axis_index("dp"), lax.axis_index("mp")
    c = lax.rem(d, 2)
    p = z // 2
    chip = d // 2
    native = c == p
    foreign = jnp.logical_not(native)
    flip = lambda a, bit: a + bit * (1 - 2 * lax.rem(a // bit, 2))
    z1, z2 = flip(z, 1), flip(z, 2)
    z3 = flip(z2, 1)
    q = jnp.where(native, z, z2)
    q1 = flip(q, 1)
    block = lax.rem(z, 2)
    low_chip = block == 0
    dc, dx, dy = flip(d, 1), flip(d, 2), flip(d, 4)
    dd = flip(dx, 4)
    C, Zp, Fz, F3, CF = (dc, z), (d, z1), (d, z2), (d, z3), (dc, z2)
    X, Y, XY = (dx, z), (dy, z), (dd, z)
    CZ = (dc, z1)
    plane = ((X, dx // 2), (Y, dy // 2), (XY, dd // 2))
    MESH = pl.DeviceIdType.MESH
    barrier = pltpu.get_barrier_semaphore()
    all_peers = (C, Zp, Fz, F3, CF, CZ, X, Y, XY)
    for peer in all_peers:
        pl.semaphore_signal(barrier, inc=1, device_id=peer, device_id_type=MESH)

    counter = [0, 0]
    drains = []

    def remote(src, dst, dev, when=None):
        i = counter[0]
        counter[0] += 1
        copy = pltpu.make_async_remote_copy(
            src_ref=src, dst_ref=dst, send_sem=ssem.at[i], recv_sem=rsem.at[i],
            device_id=dev, device_id_type=MESH,
        )
        drains.append((copy, when))
        return copy

    def local(src, dst):
        i = counter[1]
        counter[1] += 1
        return pltpu.make_async_copy(src, dst, lsem.at[i])

    def loop(count, fn):
        def step(i, carry):
            fn(i)
            return carry

        lax.fori_loop(0, count, step, 0)

    row = lambda ref: ref[...].astype(F32).reshape(1, D)
    gain = lambda i: gains[i : i + 1, :]
    shift = lambda i: shifts[i : i + 1, :]

    rc_tok = remote(tok, T_, C, "n")
    rc_len = remote(len_, len_, C, "n")
    rc_cot = remote(cot, G_, C, "n")
    rc_qb = remote(qb_, qb_, Fz, "n")
    rc_sat = remote(sat2, satt, CF, "f")
    rc_qn = remote(qb_, qn_, Zp, "n")
    rc_qf = remote(qb_, qn_, Zp, "f")
    weights = {}
    nears = {}

    def weight(name, src, dst, both_quarters):
        size = src.shape[0] // 4
        base = block * src.shape[0] if both_quarters else 0
        at = lambda ref, start: ref.at[ds(start + chip * size, size), :]
        first = remote(at(src, 0), at(dst, base), Fz, "n")
        spread = [remote(at(dst, base), at(dst, base), dev, "f") for dev, _ in plane]
        whole = dst.at[ds(base, src.shape[0]), :] if both_quarters else dst
        weights[name] = (first, spread, local(src, whole))
        if both_quarters:
            near = (1 - block) * src.shape[0]
            nears[name] = (
                remote(at(src, 0), at(dst, base), Zp, "n"),
                remote(at(dst, base), at(dst, base), Zp, "f"),
                [remote(at(dst, near), at(dst, near), dev) for dev, _ in plane],
            )

    for name, src, dst, both_quarters in (
        ("so", w_so, so, False), ("ck", w_ck, ck, True), ("cq", w_cq, cq, True), ("co", w_co, co, True),
        ("mo", w_mo, mo, False), ("mi", w_mi, mi, False), ("si", w_si, si, False),
    ):
        weight(name, src, dst, both_quarters)
    own_tok, own_si = act, gb.at[0, 0 : 3 * HW, :]
    lc_tok, lc_cot, lc_own, lc_own_si = local(tok, T_), local(cot, G_), local(tok, own_tok), local(w_si, own_si)
    rc_mem = remote(mem, slab.at[1], Fz, "f")
    lc_mem = local(mem, slab.at[0])
    rc_mc = [remote(slab.at[s], slab.at[s], C, "n") for s in range(2)]

    def spread_weight(name):
        first, spread, loc = weights[name]
        first.wait_recv()
        for copy in spread:
            copy.start()
        if name in nears:
            nears[name][1].start()

    def spread_near(role):
        for name in ("ck", "cq", "co"):
            nears[name][role].wait_recv()
            for copy in nears[name][2]:
                copy.start()

    def need_weight(name):
        first, spread, loc = weights[name]

        @pl.when(native)
        def _():
            loc.wait()

        @pl.when(foreign)
        def _():
            for copy in spread:
                copy.wait_recv()

        if name in nears:
            for copy in nears[name][2]:
                copy.wait_recv()

    lc_own.start()
    lc_own_si.start()

    @pl.when(native)
    def _():
        lc_mem.start()
        for copy in [weights[n][2] for n in ("so", "ck")] + [lc_tok, lc_cot]:
            copy.start()
        for n in ("cq", "co", "mo", "mi", "si"):
            weights[n][2].start()
        len_[...] = jnp.broadcast_to(lens[...].astype(F32).reshape(1, 1), (8, 128))
        qb_[0:2, 0:HW] = self_bias[...].astype(F32)
        qb_[2:4, 0:HW] = cross_bias[...].astype(F32)
        qb_[4:5, :] = row(mi_bias)

    pl.semaphore_wait(barrier, len(all_peers))

    @pl.when(native)
    def _():
        for name in ("so", "ck"):
            weights[name][0].start()
        for name in ("ck", "cq", "co"):
            nears[name][0].start()
        rc_qb.start()
        rc_qn.start()
        rc_len.start()
        lc_mem.wait()
        rc_mc[0].start()
        rc_tok.start()
        rc_cot.start()

    @pl.when(foreign)
    def _():
        rc_mem.start()

    def ln0(src):
        def part(i):
            rows = ds(i * AB, AB)
            n, _ = normed(src[rows, :].astype(F32))
            x1[rows, :] = (n * gain(0) + shift(0)).astype(BF)

        loop(TA // AB, part)

    def heads_to(ref, rows, values, first=0):
        for h in range(values.shape[1] // HD):
            ref[first + h, rows, :] = values[:, h * HD : (h + 1) * HD].astype(BF)

    def qkv(proj, bias):
        def part(i):
            rows = ds(i * AB, AB)
            values = nt(x1[rows, :], proj[...])
            heads_to(q_, rows, values[:, 0:HW] + bias[0:1, 0:HW].astype(F32))
            heads_to(k_, rows, values[:, HW : 2 * HW])
            heads_to(v_, rows, values[:, 2 * HW :] + bias[1:2, 0:HW].astype(F32))

        loop(TA // AB, part)

    def row_ids(start):
        return (start + lax.broadcasted_iota(jnp.int32, (AB, 1), 0)).astype(F32)

    self_cols = lax.broadcasted_iota(jnp.int32, (1, TA), 1).astype(F32)

    def self_fwd(limit, dst):
        def part(i):
            start = i * AB
            rows = ds(start, AB)
            ids = row_ids(start)
            valid = ids < limit
            allowed = (self_cols <= ids) & valid
            outs = []
            for h in range(NH):
                s = nt(q_[h, rows, :], k_[h]) * 0.125
                s = jnp.where(allowed, s, -1000000000.0)
                e = jnp.exp(s - jnp.max(s, axis=-1, keepdims=True))
                pb = (e * (1.0 / jnp.sum(e, axis=-1, keepdims=True))).astype(BF)
                ps_[h, rows, :] = pb
                if dst is not None:
                    outs.append(nn(pb, v_[h]))
            if dst is not None:
                dst[rows, :] = jnp.where(valid, jnp.concatenate(outs, axis=1), 0.0).astype(BF)

        loop(TA // AB, part)

    lc_own.wait()
    ln0(own_tok)
    lc_own_si.wait()
    qkv(own_si, self_bias)

    @pl.when(foreign)
    def _():
        spread_weight("so")
        spread_weight("ck")

    @pl.when(native)
    def _():
        spread_near(0)

    self_fwd(lens[...].astype(F32).reshape(1, 1), sat2)

    @pl.when(native)
    def _():
        for name in ("cq", "co"):
            weights[name][0].start()
        satt[...] = sat2[...]
        lc_tok.wait()

    @pl.when(foreign)
    def _():
        rc_sat.start()
        spread_weight("cq")
        spread_weight("co")
        rc_tok.wait_recv()
        rc_len.wait_recv()
        rc_qb.wait_recv()
        rc_qf.start()
        rc_sat.wait_recv()

    length = len_[0:1, 0:1]
    valid_rows = row_ids

    size_of = (AB, AB, PB)
    lrows = lambda j: slice(j * AB, j * AB + size_of[j])
    gstart = lambda h, j: h * (TA // 2) + j * AB if j < 2 else TA + h * PB
    grows = lambda h, j: ds(gstart(h, j), size_of[j])
    mine, other = c, 1 - c
    half = lambda t: c + t * (1 - 2 * c)
    slots = {}

    def sum_open(slot, count, chips=True):
        for copy in slots.get(slot, ()):
            copy.wait_send()
            drains[:] = [item for item in drains if item[0] is not copy]
        to_core = [remote(pS.at[slot, lrows(j), :], pR.at[slot, lrows(j), :], C) for j in range(count)]
        if not chips:
            slots[slot] = to_core
            return slot, to_core
        zslot = slot // 2
        to_chip = [remote(zS.at[zslot, lrows(j), :], zR.at[zslot, lrows(j), :], Zp) for j in range(count)]
        slots[slot] = to_core + to_chip
        return slot, to_core, to_chip

    def emit(opened, j, product, between=None):
        slot, to_core, to_chip = opened
        pS[slot, lrows(j), :] = product(grows(other, j)).astype(BF)
        to_core[j].start()
        own = product(grows(mine, j))
        if between is not None:
            between()
        to_core[j].wait_recv()
        zS[slot // 2, lrows(j), :] = (own + pR[slot, lrows(j), :].astype(F32)).astype(BF)
        to_chip[j].start()

    def take(opened, j):
        slot, to_core, to_chip = opened
        to_chip[j].wait_recv()
        return zS[slot // 2, lrows(j), :].astype(F32) + zR[slot // 2, lrows(j), :].astype(F32)

    def share(ref, j):
        copy = remote(ref.at[grows(mine, j), :], ref.at[grows(mine, j), :], C)
        copy.start()
        return copy

    def both(copy, fn):
        def part(t):
            @pl.when(t == 1)
            def _():
                copy.wait_recv()

            fn(half(t))

        loop(2, part)

    def pass_memory():
        @pl.when(native)
        def _():
            rc_mem.wait_recv()
            rc_mc[1].start()
            for name in ("mo", "mi", "si"):
                weights[name][0].start()

    ar1 = sum_open(0, 2)
    need_weight("so")
    emit(ar1, 0, lambda rows: nn(satt[rows, :], so[...]))
    emit(ar1, 1, lambda rows: nn(satt[rows, :], so[...]))
    pass_memory()

    @pl.when(foreign)
    def _():
        spread_near(1)
        rc_qf.wait_recv()

    @pl.when(native)
    def _():
        rc_qn.wait_recv()

    for h in range(CH):
        for s in range(2):
            K_[h, (s + 1) * FP - 16 : (s + 1) * FP, :] = jnp.zeros((16, HD), BF)
            V_[h, (s + 1) * FP - 16 : (s + 1) * FP, :] = jnp.zeros((16, HD), BF)

    def pair_bias(i):
        mine_, near_ = qb_[i : i + 1, 0:HW], qn_[i : i + 1, 0:HW]
        return jnp.where(low_chip, mine_, near_), jnp.where(low_chip, near_, mine_)

    q_bias = jnp.concatenate(pair_bias(2), axis=1)
    v_bias = pair_bias(3)
    need_weight("ck")
    for s in range(2):
        @pl.when(foreign)
        def _():
            rc_mc[s].wait_recv()

        out = slice(s * FP, s * FP + FQ)
        values = nt(slab[s], ck[...])
        for i in range(2):
            heads_to(K_, out, values[:, 2 * i * HW : (2 * i + 1) * HW], i * NH)
            heads_to(V_, out, values[:, (2 * i + 1) * HW : (2 * i + 2) * HW] + v_bias[i], i * NH)

    need_weight("cq")
    frame = lax.broadcasted_iota(jnp.int32, (1, FT), 1)
    frame_ok = lax.rem(frame, FP) < FQ

    def cross_fwd(h_, j):
        rows = ds(gstart(h_, j), AB)
        heads_to(cq_, rows, nt(x2[rows, :], cq[...]) + q_bias)
        outs, tops, totals = [], [], []
        for h in range(CH):
            s = nt(cq_[h, rows, :], K_[h]) * 0.125
            s = jnp.where(frame_ok, s, -3e38)
            top = jnp.max(s, axis=-1, keepdims=True)
            e = jnp.exp(s - top)
            total = jnp.sum(e, axis=-1, keepdims=True)
            pb = (e * (1.0 / total)).astype(BF)
            pc_[h, rows, :] = pb
            outs.append(nn(pb, V_[h]))
            tops.append(top)
            totals.append(total)
        oS[2 * j + h_] = jnp.concatenate(outs, axis=1).astype(BF)
        filler = [jnp.ones((AB, 8 - CH), F32)]
        stats = jnp.concatenate(tops + filler + totals + filler + [jnp.ones((AB, 112), F32)], axis=1)
        stS[2 * j + h_] = jnp.concatenate([stats, jnp.ones((16, 128), F32)], axis=0).T[0:16, :]

    def merge(h_, j):
        i = 2 * j + h_
        start = gstart(h_, j)
        rows = ds(start, AB)
        a, b = stS[i], stR[i]
        low, high = jnp.where(low_chip, a, b), jnp.where(low_chip, b, a)
        top = jnp.maximum(low[0:8], high[0:8])
        w_low, w_high = low[8:16] * jnp.exp(low[0:8] - top), high[8:16] * jnp.exp(high[0:8] - top)
        part = w_low / (w_low + w_high)
        spread_part = jnp.concatenate([part, jnp.ones((120, 128), F32)], axis=0).T[0:AB, :]
        ff[rows, :] = jnp.where(low_chip, spread_part, 1.0 - spread_part)
        wide = jnp.concatenate(
            [jnp.broadcast_to(spread_part[:, h : h + 1], (AB, HD)) for h in range(CH)], axis=1
        )
        me, near = oS[i].astype(F32), oR[i].astype(F32)
        att = jnp.where(low_chip, me, near) * wide + jnp.where(low_chip, near, me) * (1.0 - wide)
        catt[rows, :] = jnp.where(valid_rows(start) < length, att, 0.0).astype(BF)

    def to_near(j, src, dst):
        copy = remote(src.at[2 * j : 2 * j + 2], dst.at[2 * j : 2 * j + 2], Zp)
        copy.start()
        return copy

    def core_sum(opened, j, product):
        slot, to_core = opened
        pS[slot, lrows(j), :] = product(grows(other, j)).astype(BF)
        to_core[j].start()
        own = product(grows(mine, j))
        to_core[j].wait_recv()
        return own + pR[slot, lrows(j), :].astype(F32)

    near_att = []

    @pl.when(foreign)
    def _():
        spread_weight("mo")

    ar2 = sum_open(1, 2, chips=False)
    for j in range(2):
        own = grows(mine, j)
        value = T_[own, :].astype(F32) + take(ar1, j) + row(so_bias)
        m1[lrows(j), :] = value
        n, _ = normed(value)
        x2[own, :] = (n * gain(1) + shift(1)).astype(BF)
        both(share(x2, j), lambda h: cross_fwd(h, j))
        near_att.append((to_near(j, oS, oR), to_near(j, stS, stR)))

        if j == 0:
            @pl.when(foreign)
            def _():
                spread_weight("mi")

    @pl.when(native)
    def _():
        lc_cot.wait()

    @pl.when(foreign)
    def _():
        rc_cot.wait_recv()

    need_weight("mo")

    def grad_active(i):
        rows = ds(i * 128, 128)
        fin[rows, :] = nt(G_[rows, :], mo[...])

    loop(T // 128, grad_active)
    need_weight("mi")
    need_weight("co")

    def mlp(rows):
        hidden = nn(x3[rows, :], mi[...]) + qb_[4:5, :]
        phi = 0.5 * (1.0 + lax.erf(hidden * (0.5**0.5)))
        density = jnp.exp(-0.5 * hidden * hidden) * (1.0 / math.sqrt(2.0 * math.pi))
        act[rows, :] = (hidden * phi).astype(BF)
        gh[rows, :] = (fin[rows, :] * (phi + hidden * density)).astype(BF)

    ar3 = sum_open(0, 3)
    for j in (2, 0, 1):
        own = grows(mine, j)
        if j == 2:
            value = T_[own, :].astype(F32) + row(so_bias) + row(co_bias)
        else:
            for copy in near_att[j]:
                copy.wait_recv()
            loop(2, lambda h: merge(h, j))
            value = core_sum(ar2, j, lambda rows: nn(catt[rows, :], co[...])) + m1[lrows(j), :] + row(co_bias)
        m2[lrows(j), :] = value
        n, _ = normed(value)
        x3[own, :] = (n * gain(2) + shift(2)).astype(BF)
        both(share(x3, j), lambda h: mlp(grows(h, j)))
        emit(ar3, j, lambda rows: nt(gh[rows, :], mi[...]))
        if j == 2:
            @pl.when(foreign)
            def _():
                spread_weight("si")


    gsends = {}

    def plane_send(m):
        gsends[m] = [
            remote(gb.at[m, ds(kk * 192, 192), :], gR.at[m, s], dev)
            for s, (dev, kk) in enumerate(plane)
        ]
        for copy in gsends[m]:
            copy.start()

    thirds = [slice(i * 256, (i + 1) * 256) for i in range(3)]
    for cols in thirds:
        gb[0, cols, :] = tn(x3[:, cols], gh[...]).astype(BF)
    plane_send(0)
    arm = sum_open(2, 3)
    for j in range(3):
        emit(arm, j, lambda rows: nn(act[rows, :], mo[...]))
    for cols in thirds:
        gb[1, cols, :] = tn(G_[:, cols], act[...]).astype(BF)
    plane_send(1)
    mi_sums = colsum(gh[...].astype(F32))

    need_weight("si")

    @pl.when(foreign)
    def _():
        ln0(T_)
        qkv(si, qb_)
        self_fwd(length, None)

    zero_row = jnp.zeros((1, D), F32)
    g_gain, g_shift = [zero_row] * 3, [zero_row] * 3
    b_out = [zero_row] * 3

    def norm_back(value, upstream, i):
        n, inv = normed(value)
        a = upstream * gain(i)
        g_gain[i] = g_gain[i] + colsum(upstream * n)
        g_shift[i] = g_shift[i] + colsum(upstream)
        return inv * (a - jnp.mean(a, axis=-1, keepdims=True) - n * jnp.mean(a * n, axis=-1, keepdims=True))

    def third_back(j):
        g = G_[grows(mine, j), :].astype(F32)
        b_out[2] = b_out[2] + colsum(g)
        value = g + norm_back(m2[lrows(j), :], take(ar3, j), 2)
        low = value.astype(BF)
        b_out[1] = b_out[1] + colsum(low.astype(F32))
        fin[lrows(j), :] = value
        return low

    def cross_bwd(h_, j):
        start = gstart(h_, j)
        rows = ds(start, AB)
        valid = valid_rows(start) < length
        grads = jnp.where(valid, nt(ups[rows, :], co[...]), 0.0).astype(BF)
        heads_to(dO, rows, grads)
        weighted = grads.astype(F32) * catt[rows, :].astype(F32)
        outs = []
        for h in range(CH):
            cols = slice(h * HD, (h + 1) * HD)
            factor = ff[rows, h : h + 1]
            dOf[h, rows, :] = (grads[:, cols].astype(F32) * factor).astype(BF)
            delta = jnp.sum(weighted[:, cols], axis=-1, keepdims=True)
            dp_ = nt(dO[h, rows, :], V_[h])
            dsv = (pc_[h, rows, :].astype(F32) * ((dp_ - delta) * factor)).astype(BF)
            dsb[h, rows, :] = dsv
            outs.append(nn(dsv, K_[h]) * 0.125)
        gqS[2 * j + h_] = jnp.concatenate(outs, axis=1).astype(BF)

    outs = []

    def give(slot, out_ref):
        from_n, from_f, to_core, onward = [], [], [], []
        for lo, hi, step, size in ((0, 0, TA // 2, AB), (2 * AB, TA, PB, PB // 2)):
            src = gO.at[slot, ds(lo + block * size, size), :]
            dst = out_ref.at[ds(hi + c * step + block * size, size), :]
            from_n.append(remote(src, dst, Fz, "n"))
            from_f.append(remote(src, dst, CF, "f"))
            both_rows = out_ref.at[ds(hi + c * step, 2 * size), :]
            to_core.append(remote(gO.at[slot, lo : lo + 2 * size, :], both_rows, C, "f"))
            for h in range(2):
                rows = out_ref.at[ds(hi + h * step + block * size, size), :]
                onward.append(remote(rows, rows, Zp, "f"))

        @pl.when(native)
        def _():
            for copy in from_n:
                copy.start()
            for j in range(3):
                out_ref[grows(mine, j), :] = gO[slot, lrows(j), :]

        @pl.when(foreign)
        def _():
            for copy in from_f + to_core:
                copy.start()

        outs.append((from_n, from_f, to_core, onward))

    def pass_on(slot):
        from_n, from_f, to_core, onward = outs[slot]

        @pl.when(foreign)
        def _():
            for copy in from_n + from_f:
                copy.wait_recv()
            for copy in onward:
                copy.start()

    def give_mixed():
        for j in range(3):
            value = m2[lrows(j), :] + take(arm, j) + row(mo_bias)
            gO[0, lrows(j), :] = value.astype(BF)
        give(0, mixed_o)

    ar4 = sum_open(1, 2, chips=False)
    near_queries = []
    for j in range(2):
        ups[grows(mine, j), :] = third_back(j)
        both(share(ups, j), lambda h: cross_bwd(h, j))
        near_queries.append(to_near(j, gqS, gqR))
        if j == 0:
            give_mixed()

    finals = {}
    own_piece = ds(chip * 192, 192)
    for m in range(4):
        finals[m] = (
            remote(gb.at[m, own_piece, :], gFr.at[m], Fz, "f"),
            remote(fin.at[m * 96 : (m + 1) * 96, :], grads_o.at[m], C, "n"),
        )

    def piece_sum(m):
        piece = gb[m, own_piece, :].astype(F32)
        for s in range(3):
            gsends[m][s].wait_recv()
            piece = piece + gR[m, s].astype(F32)
        if m == 2:
            rc_gk.wait_recv()
            piece = piece + jnp.concatenate(
                [jnp.zeros((192, HW), F32), gkR[...].astype(F32), jnp.zeros((192, HW), F32)], axis=1
            )
        return piece

    def piece_out(m):
        @pl.when(foreign)
        def _():
            gb[m, own_piece, :] = piece_sum(m).astype(BF)
            finals[m][0].start()

    def piece_final(m):
        @pl.when(native)
        def _():
            piece = piece_sum(m)
            finals[m][0].wait_recv()
            whole = piece + gFr[m].astype(F32)
            fin[m * 96 : (m + 1) * 96, :] = jnp.where(c == 0, whole[96:192, :], whole[0:96, :])
            finals[m][1].start()
            grads_o[m] = jnp.where(c == 0, whole[0:96, :], whole[96:192, :])

    pad_low = third_back(2)
    b_out[0] = b_out[0] + colsum(pad_low.astype(F32))
    piece_out(0)

    def kv_grad(i):
        rows = ds(i * FP, FP)
        frames = ds(i * FP, FP, 128)
        parts = []
        for first in (0, NH):
            heads = range(first, first + NH)
            parts += [tn(dsb[h, :, frames], cq_[h]) * 0.125 for h in heads]
            parts += [tn(pc_[h, :, frames], dOf[h]) for h in heads]
        gkv[rows, :] = jnp.concatenate(parts, axis=1).astype(BF)

    loop(2, kv_grad)

    def mem_term(s):
        return nn(gkv[ds(s * FP, FP), :], ck[...])[0:FQ]

    my_frames = jnp.where(native, 0, 1)
    mt_core = remote(mtS, mtR, C)
    mt_out = remote(mtF, mgrad_o, CF, "f")
    pick = lambda a, w: (jnp.where(low_chip, a[:, 0:w], a[:, w:]), jnp.where(low_chip, a[:, w:], a[:, 0:w]))
    catt_mine = pick(catt[...], HW)[0]
    for cols in thirds:
        kv_part = tn(slab[0, :, cols], gkv[0:FQ, :]) + tn(slab[1, :, cols], gkv[FP : FP + FQ, :])
        kv_mine, kv_near = pick(kv_part, CW)
        gb[2, cols, HW : 3 * HW] = kv_mine.astype(BF)
        gb[2, cols, 3 * HW :] = tn(ups[:, cols], catt_mine).astype(BF)
        gkb[cols, :] = kv_near.astype(BF)
    near_sends = [
        remote(gkb.at[ds(kk * 192, 192), :], gRb.at[s], dev) for s, (dev, kk) in enumerate(plane)
    ]
    for copy in near_sends:
        copy.start()
    mtS[...] = mem_term(1 - my_frames).astype(BF)
    mt_core.start()
    own_term = mem_term(my_frames)
    mt_core.wait_recv()
    mtF[...] = (own_term + mtR[...].astype(F32)).astype(BF)

    @pl.when(native)
    def _():
        mgrad_o[...] = mtF[...]

    @pl.when(foreign)
    def _():
        mt_out.start()

    rc_gk = remote(gkS, gkR, Zp)
    pass_on(0)
    piece_out(1)

    def self_bwd(start):
        rows = ds(start, AB)
        valid = valid_rows(start) < length
        heads_to(dOs, rows, jnp.where(valid, nt(upo[rows, :], so[...]), 0.0))
        outs = []
        for h in range(NH):
            dp_ = nt(dOs[h, rows, :], v_[h])
            pr = ps_[h, rows, :].astype(F32)
            dsv = (pr * (dp_ - jnp.sum(pr * dp_, axis=-1, keepdims=True))).astype(BF)
            dsb[h, rows, 0:TA] = dsv
            outs.append(nn(dsv, k_[h]) * 0.125)
        gqkv[rows, 0:HW] = jnp.concatenate(outs, axis=1).astype(BF)

    for j in range(2):
        own = grows(mine, j)
        near_queries[j].wait_recv()
        for h in range(2):
            both_rows = ds(gstart(h, j), AB)
            gcq[both_rows, :] = (gqS[2 * j + h].astype(F32) + gqR[2 * j + h].astype(F32)).astype(BF)
        upstream = core_sum(ar4, j, lambda rows: nn(gcq[rows, :], cq[...]))
        value = fin[lrows(j), :] + norm_back(m1[lrows(j), :], upstream, 1)
        low = value.astype(BF)
        b_out[0] = b_out[0] + colsum(low.astype(F32))
        upo[own, :] = low
        fin[TH + j * AB : TH + (j + 1) * AB, :] = value
        both(share(upo, j), lambda h: self_bwd(gstart(h, j)))
    gO[1, lrows(2), :] = pad_low
    kv = [tn(dsb[h, :, 0:TA], q_[h]) * 0.125 for h in range(NH)]
    kv += [tn(ps_[h], dOs[h]) for h in range(NH)]
    gqkv[:, HW:] = jnp.concatenate(kv, axis=1).astype(BF)

    gcq_mine = pick(gcq[...], HW)[0]
    gs = gqkv[...].astype(F32)
    quarter = jnp.concatenate(
        [
            colsum(gs[:, 0:HW]),
            colsum(gs[:, 2 * HW :]),
            colsum(gcq_mine.astype(F32)),
            jnp.zeros((1, HW), F32),
        ],
        axis=1,
    )
    values_sum = pick(colsum(gkv[...].astype(F32)), CW)
    quarters = [jnp.concatenate([jnp.zeros((1, 3 * HW), F32), v[:, HW:]], axis=1) for v in values_sum]

    ids = lax.broadcasted_iota(jnp.int32, (16, 1), 0)
    early, late = slice(0, 16), slice(16, 24)

    def pack(count, values):
        lines = lax.broadcasted_iota(jnp.int32, (count, 1), 0)
        packed = jnp.zeros((count, D), F32)
        for i, line in enumerate(values):
            packed = packed + jnp.where(lines == i, line, 0.0)
        return packed

    def over_cores(part, packed):
        sb[0, part, :] = packed
        copy = remote(sb.at[0, part, :], sR.at[part, :], C)
        copy.start()
        return copy

    def over_plane(part, copy):
        copy.wait_recv()
        sb[1, part, :] = sb[0, part, :] + sR[part, :]
        copies = [remote(sb.at[1, part, :], sX.at[chip, part, :], dev) for dev, _ in plane]
        for copy in copies:
            copy.start()
        sX[chip, part, :] = sb[1, part, :]
        return copies

    def over_chips(part, copies):
        for copy in copies:
            copy.wait_recv()
        sb[2, part, :] = sX[0, part, :] + sX[1, part, :] + sX[2, part, :] + sX[3, part, :]
        copies = [remote(sb.at[2, part, :], sZ.at[z, part, :], dev) for dev in (Zp, Fz, F3)]
        for copy in copies:
            copy.start()
        sZ[z, part, :] = sb[2, part, :]
        return copies

    def whole_sum(part, copies):
        for copy in copies:
            copy.wait_recv()
        return sZ[0, part, :] + sZ[1, part, :] + sZ[2, part, :] + sZ[3, part, :]

    packed = pack(16, [0.5 * v for v in g_gain[1:] + g_shift[1:] + b_out])
    packed = packed + jnp.where(ids == 7 + q, quarter + quarters[0], 0.0)
    packed = packed + jnp.where(ids == 7 + q1, quarters[1], 0.0) + jnp.where(ids == 11 + q, mi_sums, 0.0)
    early_copy = over_cores(early, packed)
    for cols in thirds:
        gb[2, cols, 0:HW] = tn(x2[:, cols], gcq_mine).astype(BF)
    early_copies = over_plane(early, early_copy)
    plane_send(2)
    for cols in thirds:
        left = tn(x1[:, cols], gqkv[...])
        right = tn(upo[:, cols], satt[...])
        gb[3, cols, :] = jnp.concatenate([left, right], axis=1).astype(BF)
    plane_send(3)
    last_core, last_chip = sum_open(0, 2)[1:]
    drains[:] = [item for item in drains if item[0] is not last_chip[1]]
    away, kept = 1 - block, block
    rows_of = lambda h, b: ds(h * (TA // 2) + b * AB, AB)
    last = None
    for step, b in enumerate((away, kept)):
        pS[0, lrows(step), :] = nn(gqkv[rows_of(other, b), :], si[...]).astype(BF)
        last_core[step].start()
        last = nn(gqkv[rows_of(mine, b), :], si[...])
        last_core[step].wait_recv()
        last = last + pR[0, lrows(step), :].astype(F32)
        if step == 0:
            zS[0, lrows(0), :] = last.astype(BF)
            last_chip[0].start()
    last_sum = last

    near_piece = gkb[own_piece, :].astype(F32)
    for s in range(3):
        near_sends[s].wait_recv()
        near_piece = near_piece + gRb[s].astype(F32)
    gkS[...] = near_piece.astype(BF)
    rc_gk.start()
    early_copies = over_chips(early, early_copies)
    piece_out(2)
    piece_final(0)
    own = rows_of(mine, kept)
    last_chip[0].wait_recv()
    last_sum = last_sum + zR[0, lrows(0), :].astype(F32)
    value = fin[ds(TH + kept * AB, AB), :] + norm_back(T_[own, :].astype(F32), last_sum, 0)
    gO[1, 0:AB, :] = value.astype(BF)
    pads_at = lambda b: ds(TA + c * PB + b * (PB // 2), PB // 2)
    pad_src = gO.at[1, ds(2 * AB + block * (PB // 2), PB // 2), :]
    grad_src, grad_dst = gO.at[1, 0:AB, :], igrad_o.at[own, :]
    give_n = [remote(grad_src, grad_dst, dev, "n") for dev in (Fz, Zp)]
    give_f = [remote(grad_src, grad_dst, dev, "f") for dev in (CF, CZ, C)]
    pad_n = remote(pad_src, igrad_o.at[pads_at(block), :], Fz, "n")
    pad_f = remote(pad_src, igrad_o.at[pads_at(block), :], CF, "f")
    pad_c = remote(gO.at[1, 2 * AB : 2 * AB + PB, :], igrad_o.at[grows(mine, 2), :], C, "f")
    onward = []
    for h in range(2):
        for lo, size in ((h * (TA // 2) + block * AB, AB), (TA + h * PB + block * (PB // 2), PB // 2)):
            rows = igrad_o.at[ds(lo, size), :]
            onward.append(remote(rows, rows, Zp, "f"))

    @pl.when(native)
    def _():
        for copy in give_n + [pad_n]:
            copy.start()
        igrad_o[own, :] = gO[1, 0:AB, :]
        igrad_o[grows(mine, 2), :] = pad_low

    @pl.when(foreign)
    def _():
        for copy in give_f + [pad_f, pad_c]:
            copy.start()

    def pass_grad():
        @pl.when(foreign)
        def _():
            give_n[0].wait_recv()
            give_f[0].wait_recv()
            pad_n.wait_recv()
            pad_f.wait_recv()
            for copy in onward:
                copy.start()

    late_copy = over_cores(late, pack(8, [g_gain[0], g_shift[0]]))
    piece_final(1)
    late_copies = over_plane(late, late_copy)
    piece_out(3)
    late_copies = over_chips(late, late_copies)
    pass_grad()
    piece_final(2)
    total = whole_sum(early, early_copies)
    first = whole_sum(late, late_copies)
    small_o[0:1, :] = first[0:1, :]
    small_o[1:3, :] = total[0:2, :]
    small_o[3:4, :] = first[1:2, :]
    small_o[4:9, :] = total[2:7, :]
    small_o[9:10, :] = colsum(jnp.where(ids == 7 + z, total, 0.0))
    small_o[10:11, :] = colsum(jnp.where(ids == 11 + z, total, 0.0))
    small_o[11:16, :] = jnp.zeros((5, D), F32)

    piece_final(3)

    @pl.when(foreign)
    def _():
        for m in range(4):
            finals[m][1].wait_recv()
        mt_out.wait_recv()
        for copy in outs[0][3] + onward:
            copy.wait_recv()

    @pl.when(native)
    def _():
        for copy in outs[0][2] + [give_n[1]] + give_f[1:] + [pad_c]:
            copy.wait_recv()

    for copy, when in drains:
        if when is None:
            copy.wait_send()

    @pl.when(native)
    def _():
        for copy, when in drains:
            if when == "n":
                copy.wait_send()

    @pl.when(foreign)
    def _():
        for copy, when in drains:
            if when == "f":
                copy.wait_send()


def finish_kernel(
    mixed_i, igrad_i, mgrad_i, grads, small,
    mixed_o, igrad_o, mgrad_o, gain_o, shift_o, si_o, sb_o, so_o, sob_o, cq_o, ck_o, cb_o, co_o, cob_o,
    mi_o, mib_o, mo_o, mob_o,
):
    mixed_o[...] = mixed_i[...]
    igrad_o[...] = igrad_i[...]
    mgrad_o[...] = mgrad_i[...]
    gain_o[...] = small[0:3, :]
    shift_o[...] = small[3:6, :]
    for i in range(3):
        si_o[i] = grads[3, :, i * HW : (i + 1) * HW]
    for i in range(2):
        sb_o[i : i + 1, :] = small[9:10, i * HW : (i + 1) * HW]
        cb_o[i : i + 1, :] = small[9:10, (i + 2) * HW : (i + 3) * HW]
        ck_o[i] = grads[2, :, (i + 1) * HW : (i + 2) * HW]
    so_o[...] = grads[3, :, 3 * HW :].T
    cq_o[...] = grads[2, :, 0:HW]
    co_o[...] = grads[2, :, 3 * HW :].T
    sob_o[...] = small[6]
    cob_o[...] = small[7]
    mob_o[...] = small[8]
    mib_o[...] = small[10]
    mi_o[...] = grads[0]
    mo_o[...] = grads[1]


def fused(
    tokens, memory, lengths, cotangent, ln_gain, ln_bias, self_in, self_bias, self_out,
    self_out_bias, cross_q, cross_kv, cross_bias, cross_out, cross_out_bias, mlp_in,
    mlp_in_bias, mlp_out, mlp_out_bias,
):
    vmem = pltpu.VMEM
    heads, frames = vmem((NH, TA, HD), BF), vmem((CH, FT, HD), BF)
    rows, low_rows, own_rows = vmem((T, D), BF), vmem((TA, D), BF), vmem((TH, D), F32)
    att = vmem((TA, HW), BF)
    probs, sums, memo = vmem((CH, TA, FT), BF), vmem((3, TH, D), BF), vmem((FQ, D), BF)
    chip_sums = vmem((2, TH, D), BF)
    heads6, two = vmem((CH, TA, HD), BF), vmem((4, AB, CW), BF)
    wide_w, att6 = vmem((CW, D), BF), vmem((TA, CW), BF)
    scratch = [
        rows, rows, vmem((8, 128), F32), vmem((8, D), F32), vmem((8, D), F32),
        vmem((3 * HW, D), BF), vmem((HW, D), BF), wide_w, vmem((2 * CW, D), BF), wide_w,
        vmem((D, D), BF), vmem((D, D), BF), vmem((2, FQ, D), BF),
        low_rows, heads, heads, heads, vmem((NH, TA, TA), BF), att, att, own_rows, low_rows,
        heads6, frames, frames, probs, att6, own_rows, rows, rows, rows,
        low_rows, heads6, heads6, probs, vmem((FT, 2 * CW), BF), att6, low_rows, heads, vmem((TA, 3 * HW), BF),
        two, two, vmem((4, 16, 128), F32), vmem((4, 16, 128), F32), vmem((TA, 128), F32), two, two,
        sums, sums, chip_sums, chip_sums, vmem((T, D), F32),
        memo, memo, memo,
        vmem((4, D, D), BF), vmem((4, 3, 192, D), BF), vmem((4, 192, D), BF),
        vmem((D, CW), BF), vmem((3, 192, CW), BF), vmem((192, CW), BF), vmem((192, CW), BF),
        vmem((2, TH, D), BF), vmem((3, 24, D), F32), vmem((24, D), F32),
        vmem((4, 24, D), F32), vmem((4, 24, D), F32),
        pltpu.SemaphoreType.DMA((16,)), pltpu.SemaphoreType.DMA((200,)), pltpu.SemaphoreType.DMA((200,)),
    ]
    hbm, on_chip = pl.BlockSpec(memory_space=pl.ANY), pl.BlockSpec(memory_space=pltpu.VMEM)
    shape = jax.ShapeDtypeStruct
    wide = [shape((T, D), BF), shape((T, D), BF), shape((FQ, D), BF)]
    h, v = hbm, on_chip
    parts = pl.pallas_call(
        layer_kernel,
        out_shape=wide + [shape((4, 96, D), F32), shape((16, D), F32)],
        in_specs=[h, h, v, h, v, v, h, v, h, v, h, h, v, h, v, h, v, h, v],
        out_specs=[on_chip] * 5,
        scratch_shapes=scratch,
        compiler_params=pltpu.CompilerParams(
            collective_id=0, has_side_effects=True, vmem_limit_bytes=VMEM_LIMIT
        ),
    )(
        tokens, memory[0], lengths, cotangent, ln_gain, ln_bias,
        jnp.swapaxes(self_in, 1, 2).reshape(3 * HW, D), self_bias, self_out, self_out_bias,
        cross_q.T, jnp.swapaxes(cross_kv, 1, 2).reshape(2 * HW, D), cross_bias, cross_out, cross_out_bias,
        mlp_in, mlp_in_bias, mlp_out, mlp_out_bias,
    )
    vec = shape((D,), F32)
    outs = list(pl.pallas_call(
        finish_kernel,
        out_shape=wide
        + [
            shape((3, D), F32), shape((3, D), F32), shape((3, 96, HW), F32), shape((2, HW), F32),
            shape((HW, 96), F32), vec, shape((96, HW), F32), shape((2, 96, HW), F32), shape((2, HW), F32),
            shape((HW, 96), F32), vec, shape((96, D), F32), vec, shape((96, D), F32), vec,
        ],
        in_specs=[on_chip] * 5,
        out_specs=[on_chip] * 18,
    )(*parts))
    outs[2] = outs[2][None]
    outs[16] = outs[16].T
    return tuple(outs)


def matmul(left, right):
    return jnp.dot(left, right, preferred_element_type=jnp.float32)


def einsum_f(form, left, right):
    return jnp.einsum(form, left, right, preferred_element_type=jnp.float32)


def norm_parts(values):
    average = jnp.mean(values, axis=-1, keepdims=True)
    centred = values - average
    variance = jnp.mean(centred * centred, axis=-1, keepdims=True)
    scale_inv = lax.rsqrt(variance + 1e-05)
    return (centred * scale_inv, scale_inv)


def norm_back(normed, scale_inv, gain, upstream):
    scaled = upstream * gain
    inner = (
        scaled
        - jnp.mean(scaled, axis=-1, keepdims=True)
        - normed * jnp.mean(scaled * normed, axis=-1, keepdims=True)
    )
    return (scale_inv * inner, jnp.sum(upstream * normed, axis=0), jnp.sum(upstream, axis=0))


def softmax_parts(scores):
    row_max = jnp.max(scores, axis=-1, keepdims=True)
    shifted = jnp.exp(scores - row_max)
    totals = jnp.sum(shifted, axis=-1, keepdims=True)
    return (shifted / totals, row_max[..., 0] + jnp.log(totals[..., 0]))


def gelu_exact(values):
    return jax.nn.gelu(values, approximate=False)


def self_forward(queries, keys_self, values_self, allowed, valid_mask):
    row_count, head_width = queries.shape
    head_count = head_width // HD
    query_heads = queries.reshape(row_count, head_count, HD)
    key_heads = keys_self.reshape(row_count, head_count, HD)
    value_heads = values_self.reshape(row_count, head_count, HD)
    scores = einsum_f("thd,shd->hts", query_heads, key_heads) * 0.125
    scores = jnp.where(allowed[None], scores, -1000000000.0)
    probs, log_total = softmax_parts(scores)
    attended = einsum_f("hts,shd->thd", probs.astype(jnp.bfloat16), value_heads).reshape(
        row_count, head_width
    )
    attended = jnp.where(valid_mask, attended, 0.0)
    return (attended.astype(jnp.bfloat16), log_total)


def self_backward(queries, keys_self, values_self, allowed, log_total, grad_out):
    row_count, head_width = queries.shape
    head_count = head_width // HD
    query_heads = queries.reshape(row_count, head_count, HD)
    key_heads = keys_self.reshape(row_count, head_count, HD)
    value_heads = values_self.reshape(row_count, head_count, HD)
    scores = einsum_f("thd,shd->hts", query_heads, key_heads) * 0.125
    scores = jnp.where(allowed[None], scores, -1000000000.0)
    probs = jnp.exp(scores - log_total[..., None])
    grad_heads = grad_out.reshape(row_count, head_count, HD)
    grad_values = einsum_f("hts,thd->shd", probs.astype(jnp.bfloat16), grad_heads)
    grad_probs = einsum_f("thd,shd->hts", grad_heads, value_heads)
    grad_scores = (
        probs * (grad_probs - jnp.sum(probs * grad_probs, axis=-1, keepdims=True))
    ).astype(jnp.bfloat16)
    grad_queries = einsum_f("hts,shd->thd", grad_scores, key_heads) * 0.125
    grad_keys = einsum_f("hts,thd->shd", grad_scores, query_heads) * 0.125
    return (
        grad_queries.reshape(row_count, head_width).astype(jnp.bfloat16),
        grad_keys.reshape(row_count, head_width).astype(jnp.bfloat16),
        grad_values.reshape(row_count, head_width).astype(jnp.bfloat16),
    )


def cross_forward(query_heads, memory_pairs, clip_of):
    row_count, head_count, _ = query_heads.shape
    head_width = head_count * HD
    clip_count = memory_pairs.shape[0]

    def per_clip(carry, clip_item):
        attended, log_rows = carry
        clip_index, clip_pairs = clip_item
        key_heads = clip_pairs[:, :head_width].reshape(-1, head_count, HD)
        value_heads = clip_pairs[:, head_width:].reshape(-1, head_count, HD)
        scores = einsum_f("thd,fhd->htf", query_heads, key_heads) * 0.125
        probs, log_total = softmax_parts(scores)
        result = einsum_f("htf,fhd->thd", probs.astype(jnp.bfloat16), value_heads).reshape(
            row_count, head_width
        )
        member = clip_of == clip_index
        return (
            (
                jnp.where(member[:, None], result, attended),
                jnp.where(member[None, :], log_total, log_rows),
            ),
            None,
        )

    start_carry = (
        jnp.zeros((row_count, head_width), jnp.float32),
        jnp.zeros((head_count, row_count), jnp.float32),
    )
    (attended, log_rows), _ = lax.scan(
        per_clip, start_carry, (jnp.arange(clip_count, dtype=jnp.int32), memory_pairs)
    )
    return (attended.astype(jnp.bfloat16), log_rows)


def cross_backward(query_heads, memory_pairs, clip_of, log_rows, grad_out):
    row_count, head_count, _ = query_heads.shape
    head_width = head_count * HD
    clip_count = memory_pairs.shape[0]

    def per_clip(grad_query, clip_item):
        clip_index, clip_pairs = clip_item
        frames = clip_pairs.shape[0]
        member = clip_of == clip_index
        key_heads = clip_pairs[:, :head_width].reshape(frames, head_count, HD)
        value_heads = clip_pairs[:, head_width:].reshape(frames, head_count, HD)
        scores = einsum_f("thd,fhd->htf", query_heads, key_heads) * 0.125
        probs = jnp.where(member[None, :, None], jnp.exp(scores - log_rows[:, :, None]), 0.0)
        grad_heads = jnp.where(member[:, None], grad_out, jnp.zeros_like(grad_out)).reshape(
            row_count, head_count, HD
        )
        grad_values = einsum_f("htf,thd->fhd", probs.astype(jnp.bfloat16), grad_heads)
        grad_probs = einsum_f("thd,fhd->htf", grad_heads, value_heads)
        grad_scores = (
            probs * (grad_probs - jnp.sum(probs * grad_probs, axis=-1, keepdims=True))
        ).astype(jnp.bfloat16)
        grad_query = grad_query + einsum_f("htf,fhd->thd", grad_scores, key_heads) * 0.125
        grad_keys = einsum_f("htf,thd->fhd", grad_scores, query_heads) * 0.125
        grad_pairs = jnp.concatenate(
            [grad_keys.reshape(frames, head_width), grad_values.reshape(frames, head_width)], axis=1
        )
        return (grad_query, grad_pairs.astype(jnp.bfloat16))

    grad_query, grad_pairs = lax.scan(
        per_clip,
        jnp.zeros((row_count, head_count, HD), jnp.float32),
        (jnp.arange(clip_count, dtype=jnp.int32), memory_pairs),
    )
    return (grad_query.reshape(row_count, head_width).astype(jnp.bfloat16), grad_pairs)


def body(
    tokens,
    memory,
    lengths,
    cotangent,
    ln_gain,
    ln_bias,
    self_in,
    self_bias,
    self_out,
    self_out_bias,
    cross_q,
    cross_kv,
    cross_bias,
    cross_out,
    cross_out_bias,
    mlp_in,
    mlp_in_bias,
    mlp_out,
    mlp_out_bias,
):
    row_count = tokens.shape[0]
    clip_count = lengths.shape[0]
    head_width = self_in.shape[2]
    head_count = head_width // HD
    clip_ends = jnp.cumsum(lengths)
    positions = jnp.arange(row_count, dtype=jnp.int32)
    clip_of = jnp.sum((positions[:, None] >= clip_ends[None, :]).astype(jnp.int32), axis=1)
    valid_mask = (clip_of < clip_count)[:, None]
    allowed = (
        (clip_of[:, None] == clip_of[None, :])
        & (positions[None, :] <= positions[:, None])
        & (clip_of[:, None] < clip_count)
    )
    inputs = tokens.astype(jnp.float32)
    normed_one, scale_one = norm_parts(inputs)
    first_in = (normed_one * ln_gain[0] + ln_bias[0]).astype(jnp.bfloat16)
    queries = (matmul(first_in, self_in[0]) + self_bias[0]).astype(jnp.bfloat16)
    keys_self = matmul(first_in, self_in[1]).astype(jnp.bfloat16)
    values_self = (matmul(first_in, self_in[2]) + self_bias[1]).astype(jnp.bfloat16)
    self_att, log_self = self_forward(queries, keys_self, values_self, allowed, valid_mask)
    mixed_one = inputs + lax.psum(matmul(self_att, self_out), "mp") + self_out_bias
    normed_two, scale_two = norm_parts(mixed_one)
    second_in = (normed_two * ln_gain[1] + ln_bias[1]).astype(jnp.bfloat16)
    cross_queries = (matmul(second_in, cross_q) + cross_bias[0]).astype(jnp.bfloat16)
    slab = lax.all_gather(memory, "mp", axis=1, tiled=True)
    slab_keys = einsum_f("cfd,de->cfe", slab, cross_kv[0]).astype(jnp.bfloat16)
    slab_values = (einsum_f("cfd,de->cfe", slab, cross_kv[1]) + cross_bias[1]).astype(jnp.bfloat16)
    memory_pairs = jnp.concatenate([slab_keys, slab_values], axis=2)
    query_heads = cross_queries.reshape(row_count, head_count, HD)
    cross_att, log_cross = cross_forward(query_heads, memory_pairs, clip_of)
    mixed_two = (
        mixed_one
        + lax.psum(matmul(cross_att, cross_out).astype(jnp.bfloat16), "mp").astype(jnp.float32)
        + cross_out_bias
    )
    normed_three, scale_three = norm_parts(mixed_two)
    third_in = (normed_three * ln_gain[2] + ln_bias[2]).astype(jnp.bfloat16)
    hidden = matmul(third_in, mlp_in) + mlp_in_bias
    active, gelu_back = jax.vjp(gelu_exact, hidden)
    active_low = active.astype(jnp.bfloat16)
    mixed = (
        mixed_two
        + lax.psum(matmul(active_low, mlp_out).astype(jnp.bfloat16), "mp").astype(jnp.float32)
        + mlp_out_bias
    ).astype(jnp.bfloat16)
    upstream = cotangent.astype(jnp.float32)
    grad_mlp_out = einsum_f("tf,td->fd", active_low, cotangent)
    grad_mlp_out_bias = jnp.sum(upstream, axis=0)
    grad_active = einsum_f("td,fd->tf", cotangent, mlp_out)
    grad_hidden = gelu_back(grad_active)[0].astype(jnp.bfloat16)
    grad_mlp_in = einsum_f("td,tf->df", third_in, grad_hidden)
    grad_mlp_in_bias = jnp.sum(grad_hidden.astype(jnp.float32), axis=0)
    grad_third = lax.psum(
        einsum_f("tf,df->td", grad_hidden, mlp_in).astype(jnp.bfloat16), "mp"
    ).astype(jnp.float32)
    back_three, gain_three, shift_three = norm_back(
        normed_three, scale_three, ln_gain[2], grad_third
    )
    grad_two = upstream + back_three
    up_two = grad_two.astype(jnp.bfloat16)
    grad_cross_out = einsum_f("tk,td->kd", cross_att, up_two)
    grad_cross_out_bias = jnp.sum(up_two.astype(jnp.float32), axis=0)
    grad_cross_att = einsum_f("td,kd->tk", up_two, cross_out).astype(jnp.bfloat16)
    grad_cross_att = jnp.where(valid_mask, grad_cross_att, jnp.zeros_like(grad_cross_att))
    grad_cross_queries, grad_pairs = cross_backward(
        query_heads, memory_pairs, clip_of, log_cross, grad_cross_att
    )
    grad_cross_q = einsum_f("td,tk->dk", second_in, grad_cross_queries)
    grad_query_bias = jnp.sum(grad_cross_queries.astype(jnp.float32), axis=0)
    grad_keys_cross = grad_pairs[:, :, :head_width]
    grad_values_cross = grad_pairs[:, :, head_width:]
    grad_cross_kv = jnp.stack(
        [
            einsum_f("cfd,cfe->de", slab, grad_keys_cross),
            einsum_f("cfd,cfe->de", slab, grad_values_cross),
        ]
    )
    grad_value_bias = jnp.sum(grad_values_cross.astype(jnp.float32), axis=(0, 1))
    memory_terms = einsum_f("cfe,de->cfd", grad_keys_cross, cross_kv[0]) + einsum_f(
        "cfe,de->cfd", grad_values_cross, cross_kv[1]
    )
    memory_grad = lax.psum_scatter(
        memory_terms.astype(jnp.bfloat16), "mp", scatter_dimension=1, tiled=True
    )
    grad_cross_bias = jnp.stack([grad_query_bias, grad_value_bias])
    grad_second = lax.psum(
        einsum_f("tk,dk->td", grad_cross_queries, cross_q).astype(jnp.bfloat16), "mp"
    ).astype(jnp.float32)
    back_two, gain_two, shift_two = norm_back(normed_two, scale_two, ln_gain[1], grad_second)
    grad_one = grad_two + back_two
    up_one = grad_one.astype(jnp.bfloat16)
    grad_self_out = einsum_f("tk,td->kd", self_att, up_one)
    grad_self_out_bias = jnp.sum(up_one.astype(jnp.float32), axis=0)
    grad_self_att = einsum_f("td,kd->tk", up_one, self_out).astype(jnp.bfloat16)
    grad_self_att = jnp.where(valid_mask, grad_self_att, jnp.zeros_like(grad_self_att))
    grad_queries, grad_keys_self, grad_values_self = self_backward(
        queries, keys_self, values_self, allowed, log_self, grad_self_att
    )
    grad_self_in = jnp.stack(
        [
            einsum_f("td,tk->dk", first_in, grad_queries),
            einsum_f("td,tk->dk", first_in, grad_keys_self),
            einsum_f("td,tk->dk", first_in, grad_values_self),
        ]
    )
    grad_self_bias = jnp.stack(
        [
            jnp.sum(grad_queries.astype(jnp.float32), axis=0),
            jnp.sum(grad_values_self.astype(jnp.float32), axis=0),
        ]
    )
    first_terms = (
        einsum_f("tk,dk->td", grad_queries, self_in[0])
        + einsum_f("tk,dk->td", grad_keys_self, self_in[1])
        + einsum_f("tk,dk->td", grad_values_self, self_in[2])
    )
    grad_first = lax.psum(first_terms.astype(jnp.bfloat16), "mp").astype(jnp.float32)
    back_one, gain_one, shift_one = norm_back(normed_one, scale_one, ln_gain[0], grad_first)
    input_grad = (grad_one + back_one).astype(jnp.bfloat16)
    sum_self_in, sum_self_out, sum_cross_q, sum_cross_kv, sum_cross_out, sum_mlp_in, sum_mlp_out = (
        lax.psum_scatter(grad_self_in, "dp", scatter_dimension=1, tiled=True),
        lax.psum_scatter(grad_self_out, "dp", scatter_dimension=1, tiled=True),
        lax.psum_scatter(grad_cross_q, "dp", scatter_dimension=0, tiled=True),
        lax.psum_scatter(grad_cross_kv, "dp", scatter_dimension=1, tiled=True),
        lax.psum_scatter(grad_cross_out, "dp", scatter_dimension=1, tiled=True),
        lax.psum_scatter(grad_mlp_in, "dp", scatter_dimension=0, tiled=True),
        lax.psum_scatter(grad_mlp_out, "dp", scatter_dimension=1, tiled=True),
    )
    (
        sum_gain,
        sum_shift,
        sum_self_bias,
        sum_self_out_bias,
        sum_cross_bias,
        sum_cross_out_bias,
        sum_mlp_in_bias,
        sum_mlp_out_bias,
    ) = lax.psum(
        (
            jnp.stack([gain_one, gain_two, gain_three]),
            jnp.stack([shift_one, shift_two, shift_three]),
            grad_self_bias,
            grad_self_out_bias,
            grad_cross_bias,
            grad_cross_out_bias,
            grad_mlp_in_bias,
            grad_mlp_out_bias,
        ),
        "dp",
    )
    return (
        mixed,
        input_grad,
        memory_grad,
        sum_gain,
        sum_shift,
        sum_self_in,
        sum_self_bias,
        sum_self_out,
        sum_self_out_bias,
        sum_cross_q,
        sum_cross_kv,
        sum_cross_bias,
        sum_cross_out,
        sum_cross_out_bias,
        sum_mlp_in,
        sum_mlp_in_bias,
        sum_mlp_out,
        sum_mlp_out_bias,
    )


def solution(mesh):
    in_specs = (
        P("dp", None),
        P("dp", "mp", None),
        P("dp"),
        P("dp", None),
        P(),
        P(),
        P(None, None, "mp"),
        P(None, "mp"),
        P("mp", None),
        P(),
        P(None, "mp"),
        P(None, None, "mp"),
        P(None, "mp"),
        P("mp", None),
        P(),
        P(None, "mp"),
        P("mp"),
        P("mp", None),
        P(),
    )
    out_specs = (
        P("dp", None),
        P("dp", None),
        P("dp", "mp", None),
        P(),
        P(),
        P(None, "dp", "mp"),
        P(None, "mp"),
        P("mp", "dp"),
        P(),
        P("dp", "mp"),
        P(None, "dp", "mp"),
        P(None, "mp"),
        P("mp", "dp"),
        P(),
        P("dp", "mp"),
        P("mp"),
        P("mp", "dp"),
        P(),
    )
    shape = dict(mesh.shape)
    run = fused if (shape["dp"], shape["mp"]) == (8, 4) else body
    return jax.shard_map(run, mesh=mesh, in_specs=in_specs, out_specs=out_specs, check_vma=False)
```

```python
import math

import jax
import jax.numpy as jnp
from jax import lax
from jax.experimental import pallas as pl
from jax.experimental.pallas import tpu as pltpu
from jax.sharding import PartitionSpec as P

HD = 64
D, HW, T, TA, FQ, FP, AB, PB = 768, 192, 512, 448, 375, 384, 112, 32
NH = HW // HD
FT, TH = 2 * FP, T // 2
CH, CW = 2 * NH, 2 * HW
BF, F32 = jnp.bfloat16, jnp.float32
VMEM_LIMIT = 62 << 20


def nn(a, b):
    return lax.dot_general(a, b, (((1,), (0,)), ((), ())), preferred_element_type=F32)


def nt(a, b):
    return lax.dot_general(a, b, (((1,), (1,)), ((), ())), preferred_element_type=F32)


def tn(a, b):
    return lax.dot_general(a, b, (((0,), (0,)), ((), ())), preferred_element_type=F32)


def ds(start, size, step=16):
    return pl.ds(pl.multiple_of(start, step), size)


def colsum(values):
    return jnp.sum(values, axis=0, keepdims=True)


def normed(values):
    average = jnp.mean(values, axis=-1, keepdims=True)
    centred = values - average
    variance = jnp.mean(centred * centred, axis=-1, keepdims=True)
    inv = lax.rsqrt(variance + 1e-05)
    return centred * inv, inv


def layer_kernel(
    tok, mem, lens, cot, gains, shifts, w_si, self_bias, w_so, so_bias, w_cq, w_ck, cross_bias, w_co,
    co_bias, w_mi, mi_bias, w_mo, mo_bias,
    mixed_o, igrad_o, mgrad_o, grads_o, small_o,
    T_, G_, len_, qb_, qn_, si, so, cq, ck, co, mi, mo, slab,
    x1, q_, k_, v_, ps_, satt, sat2, m1, x2, cq_, K_, V_, pc_, catt, m2, x3, act, gh,
    ups, dO, dOf, dsb, gkv, gcq, upo, dOs, gqkv,
    oS, oR, stS, stR, ff, gqS, gqR,
    pS, pR, zS, zR, fin,
    mtS, mtR, mtF,
    gb, gR, gFr, gkb, gRb, gkS, gkR, gO, sb, sR, sX, sZ,
    lsem, ssem, rsem,
):
    d, z = lax.axis_index("dp"), lax.axis_index("mp")
    c = lax.rem(d, 2)
    p = z // 2
    chip = d // 2
    native = c == p
    foreign = jnp.logical_not(native)
    flip = lambda a, bit: a + bit * (1 - 2 * lax.rem(a // bit, 2))
    z1, z2 = flip(z, 1), flip(z, 2)
    z3 = flip(z2, 1)
    q = jnp.where(native, z, z2)
    q1 = flip(q, 1)
    block = lax.rem(z, 2)
    low_chip = block == 0
    dc, dx, dy = flip(d, 1), flip(d, 2), flip(d, 4)
    dd = flip(dx, 4)
    C, Zp, Fz, F3, CF = (dc, z), (d, z1), (d, z2), (d, z3), (dc, z2)
    X, Y, XY = (dx, z), (dy, z), (dd, z)
    CZ = (dc, z1)
    plane = ((X, dx // 2), (Y, dy // 2), (XY, dd // 2))
    MESH = pl.DeviceIdType.MESH
    barrier = pltpu.get_barrier_semaphore()
    all_peers = (C, Zp, Fz, F3, CF, CZ, X, Y, XY)
    for peer in all_peers:
        pl.semaphore_signal(barrier, inc=1, device_id=peer, device_id_type=MESH)

    counter = [0, 0]
    drains = []

    def remote(src, dst, dev, when=None):
        i = counter[0]
        counter[0] += 1
        copy = pltpu.make_async_remote_copy(
            src_ref=src, dst_ref=dst, send_sem=ssem.at[i], recv_sem=rsem.at[i],
            device_id=dev, device_id_type=MESH,
        )
        drains.append((copy, when))
        return copy

    def local(src, dst):
        i = counter[1]
        counter[1] += 1
        return pltpu.make_async_copy(src, dst, lsem.at[i])

    def loop(count, fn):
        def step(i, carry):
            fn(i)
            return carry

        lax.fori_loop(0, count, step, 0)

    row = lambda ref: ref[...].astype(F32).reshape(1, D)
    gain = lambda i: gains[i : i + 1, :]
    shift = lambda i: shifts[i : i + 1, :]

    rc_tok = remote(tok, T_, C, "n")
    rc_len = remote(len_, len_, C, "n")
    rc_cot = remote(cot, G_, C, "n")
    rc_qb = remote(qb_, qb_, Fz, "n")
    rc_sat = remote(sat2, satt, CF, "f")
    rc_qn = remote(qb_, qn_, Zp, "n")
    rc_qf = remote(qb_, qn_, Zp, "f")
    weights = {}
    nears = {}

    def weight(name, src, dst, both_quarters):
        size = src.shape[0] // 4
        base = block * src.shape[0] if both_quarters else 0
        at = lambda ref, start: ref.at[ds(start + chip * size, size), :]
        first = remote(at(src, 0), at(dst, base), Fz, "n")
        spread = [remote(at(dst, base), at(dst, base), dev, "f") for dev, _ in plane]
        whole = dst.at[ds(base, src.shape[0]), :] if both_quarters else dst
        weights[name] = (first, spread, local(src, whole))
        if both_quarters:
            near = (1 - block) * src.shape[0]
            nears[name] = (
                remote(at(src, 0), at(dst, base), Zp, "n"),
                remote(at(dst, base), at(dst, base), Zp, "f"),
                [remote(at(dst, near), at(dst, near), dev) for dev, _ in plane],
            )

    for name, src, dst, both_quarters in (
        ("so", w_so, so, False), ("ck", w_ck, ck, True), ("cq", w_cq, cq, True), ("co", w_co, co, True),
        ("mo", w_mo, mo, False), ("mi", w_mi, mi, False), ("si", w_si, si, False),
    ):
        weight(name, src, dst, both_quarters)
    own_tok, own_si = act, gb.at[0, 0 : 3 * HW, :]
    lc_tok, lc_cot, lc_own, lc_own_si = local(tok, T_), local(cot, G_), local(tok, own_tok), local(w_si, own_si)
    rc_mem = remote(mem, slab.at[1], Fz, "f")
    lc_mem = local(mem, slab.at[0])
    rc_mc = [remote(slab.at[s], slab.at[s], C, "n") for s in range(2)]

    def spread_weight(name):
        first, spread, loc = weights[name]
        first.wait_recv()
        for copy in spread:
            copy.start()
        if name in nears:
            nears[name][1].start()

    def spread_near(role):
        for name in ("ck", "cq", "co"):
            nears[name][role].wait_recv()
            for copy in nears[name][2]:
                copy.start()

    def need_weight(name):
        first, spread, loc = weights[name]

        @pl.when(native)
        def _():
            loc.wait()

        @pl.when(foreign)
        def _():
            for copy in spread:
                copy.wait_recv()

        if name in nears:
            for copy in nears[name][2]:
                copy.wait_recv()

    lc_own.start()
    lc_own_si.start()

    @pl.when(native)
    def _():
        lc_mem.start()
        for copy in [weights[n][2] for n in ("so", "ck")] + [lc_tok, lc_cot]:
            copy.start()
        for n in ("cq", "co", "mo", "mi", "si"):
            weights[n][2].start()
        len_[...] = jnp.broadcast_to(lens[...].astype(F32).reshape(1, 1), (8, 128))
        qb_[0:2, 0:HW] = self_bias[...].astype(F32)
        qb_[2:4, 0:HW] = cross_bias[...].astype(F32)
        qb_[4:5, :] = row(mi_bias)

    pl.semaphore_wait(barrier, len(all_peers))

    @pl.when(native)
    def _():
        for name in ("so", "ck"):
            weights[name][0].start()
        for name in ("ck", "cq", "co"):
            nears[name][0].start()
        rc_qb.start()
        rc_qn.start()
        rc_len.start()
        lc_mem.wait()
        rc_mc[0].start()
        rc_tok.start()
        rc_cot.start()

    @pl.when(foreign)
    def _():
        rc_mem.start()

    def ln0(src):
        def part(i):
            rows = ds(i * AB, AB)
            n, _ = normed(src[rows, :].astype(F32))
            x1[rows, :] = (n * gain(0) + shift(0)).astype(BF)

        loop(TA // AB, part)

    def heads_to(ref, rows, values, first=0):
        for h in range(values.shape[1] // HD):
            ref[first + h, rows, :] = values[:, h * HD : (h + 1) * HD].astype(BF)

    def qkv(proj, bias):
        def part(i):
            rows = ds(i * AB, AB)
            values = nt(x1[rows, :], proj[...])
            heads_to(q_, rows, values[:, 0:HW] + bias[0:1, 0:HW].astype(F32))
            heads_to(k_, rows, values[:, HW : 2 * HW])
            heads_to(v_, rows, values[:, 2 * HW :] + bias[1:2, 0:HW].astype(F32))

        loop(TA // AB, part)

    def row_ids(start):
        return (start + lax.broadcasted_iota(jnp.int32, (AB, 1), 0)).astype(F32)

    self_cols = lax.broadcasted_iota(jnp.int32, (1, TA), 1).astype(F32)

    def self_fwd(limit, dst):
        def part(i):
            start = i * AB
            rows = ds(start, AB)
            ids = row_ids(start)
            valid = ids < limit
            allowed = (self_cols <= ids) & valid
            outs = []
            for h in range(NH):
                s = nt(q_[h, rows, :], k_[h]) * 0.125
                s = jnp.where(allowed, s, -1000000000.0)
                e = jnp.exp(s - jnp.max(s, axis=-1, keepdims=True))
                pb = (e * (1.0 / jnp.sum(e, axis=-1, keepdims=True))).astype(BF)
                ps_[h, rows, :] = pb
                if dst is not None:
                    outs.append(nn(pb, v_[h]))
            if dst is not None:
                dst[rows, :] = jnp.where(valid, jnp.concatenate(outs, axis=1), 0.0).astype(BF)

        loop(TA // AB, part)

    lc_own.wait()
    ln0(own_tok)
    lc_own_si.wait()
    qkv(own_si, self_bias)

    @pl.when(foreign)
    def _():
        spread_weight("so")
        spread_weight("ck")

    @pl.when(native)
    def _():
        spread_near(0)

    self_fwd(lens[...].astype(F32).reshape(1, 1), sat2)

    @pl.when(native)
    def _():
        for name in ("cq", "co"):
            weights[name][0].start()
        satt[...] = sat2[...]
        lc_tok.wait()

    @pl.when(foreign)
    def _():
        rc_sat.start()
        spread_weight("cq")
        spread_weight("co")
        rc_tok.wait_recv()
        rc_len.wait_recv()
        rc_qb.wait_recv()
        rc_qf.start()
        rc_sat.wait_recv()

    length = len_[0:1, 0:1]
    valid_rows = row_ids

    size_of = (AB, AB, PB)
    lrows = lambda j: slice(j * AB, j * AB + size_of[j])
    gstart = lambda h, j: h * (TA // 2) + j * AB if j < 2 else TA + h * PB
    grows = lambda h, j: ds(gstart(h, j), size_of[j])
    mine, other = c, 1 - c
    half = lambda t: c + t * (1 - 2 * c)
    slots = {}

    def sum_open(slot, count, chips=True):
        for copy in slots.get(slot, ()):
            copy.wait_send()
            drains[:] = [item for item in drains if item[0] is not copy]
        to_core = [remote(pS.at[slot, lrows(j), :], pR.at[slot, lrows(j), :], C) for j in range(count)]
        if not chips:
            slots[slot] = to_core
            return slot, to_core
        zslot = slot // 2
        to_chip = [remote(zS.at[zslot, lrows(j), :], zR.at[zslot, lrows(j), :], Zp) for j in range(count)]
        slots[slot] = to_core + to_chip
        return slot, to_core, to_chip

    def emit(opened, j, product, between=None):
        slot, to_core, to_chip = opened
        pS[slot, lrows(j), :] = product(grows(other, j)).astype(BF)
        to_core[j].start()
        own = product(grows(mine, j))
        if between is not None:
            between()
        to_core[j].wait_recv()
        zS[slot // 2, lrows(j), :] = (own + pR[slot, lrows(j), :].astype(F32)).astype(BF)
        to_chip[j].start()

    def take(opened, j):
        slot, to_core, to_chip = opened
        to_chip[j].wait_recv()
        return zS[slot // 2, lrows(j), :].astype(F32) + zR[slot // 2, lrows(j), :].astype(F32)

    def share(ref, j):
        copy = remote(ref.at[grows(mine, j), :], ref.at[grows(mine, j), :], C)
        copy.start()
        return copy

    def both(copy, fn):
        def part(t):
            @pl.when(t == 1)
            def _():
                copy.wait_recv()

            fn(half(t))

        loop(2, part)

    def pass_memory():
        @pl.when(native)
        def _():
            rc_mem.wait_recv()
            rc_mc[1].start()
            for name in ("mo", "mi", "si"):
                weights[name][0].start()

    ar1 = sum_open(0, 2)
    need_weight("so")
    emit(ar1, 0, lambda rows: nn(satt[rows, :], so[...]))
    emit(ar1, 1, lambda rows: nn(satt[rows, :], so[...]))
    pass_memory()

    @pl.when(foreign)
    def _():
        spread_near(1)
        rc_qf.wait_recv()

    @pl.when(native)
    def _():
        rc_qn.wait_recv()

    for h in range(CH):
        for s in range(2):
            K_[h, (s + 1) * FP - 16 : (s + 1) * FP, :] = jnp.zeros((16, HD), BF)
            V_[h, (s + 1) * FP - 16 : (s + 1) * FP, :] = jnp.zeros((16, HD), BF)

    def pair_bias(i):
        mine_, near_ = qb_[i : i + 1, 0:HW], qn_[i : i + 1, 0:HW]
        return jnp.where(low_chip, mine_, near_), jnp.where(low_chip, near_, mine_)

    q_bias = jnp.concatenate(pair_bias(2), axis=1)
    v_bias = pair_bias(3)
    need_weight("ck")
    for s in range(2):
        @pl.when(foreign)
        def _():
            rc_mc[s].wait_recv()

        out = slice(s * FP, s * FP + FQ)
        values = nt(slab[s], ck[...])
        for i in range(2):
            heads_to(K_, out, values[:, 2 * i * HW : (2 * i + 1) * HW], i * NH)
            heads_to(V_, out, values[:, (2 * i + 1) * HW : (2 * i + 2) * HW] + v_bias[i], i * NH)

    need_weight("cq")
    frame = lax.broadcasted_iota(jnp.int32, (1, FT), 1)
    frame_ok = lax.rem(frame, FP) < FQ

    def cross_fwd(h_, j):
        rows = ds(gstart(h_, j), AB)
        heads_to(cq_, rows, nt(x2[rows, :], cq[...]) + q_bias)
        outs, tops, totals = [], [], []
        for h in range(CH):
            s = nt(cq_[h, rows, :], K_[h]) * 0.125
            s = jnp.where(frame_ok, s, -3e38)
            top = jnp.max(s, axis=-1, keepdims=True)
            e = jnp.exp(s - top)
            total = jnp.sum(e, axis=-1, keepdims=True)
            pb = (e * (1.0 / total)).astype(BF)
            pc_[h, rows, :] = pb
            outs.append(nn(pb, V_[h]))
            tops.append(top)
            totals.append(total)
        oS[2 * j + h_] = jnp.concatenate(outs, axis=1).astype(BF)
        filler = [jnp.ones((AB, 8 - CH), F32)]
        stats = jnp.concatenate(tops + filler + totals + filler + [jnp.ones((AB, 112), F32)], axis=1)
        stS[2 * j + h_] = jnp.concatenate([stats, jnp.ones((16, 128), F32)], axis=0).T[0:16, :]

    def merge(h_, j):
        i = 2 * j + h_
        start = gstart(h_, j)
        rows = ds(start, AB)
        a, b = stS[i], stR[i]
        low, high = jnp.where(low_chip, a, b), jnp.where(low_chip, b, a)
        top = jnp.maximum(low[0:8], high[0:8])
        w_low, w_high = low[8:16] * jnp.exp(low[0:8] - top), high[8:16] * jnp.exp(high[0:8] - top)
        part = w_low / (w_low + w_high)
        spread_part = jnp.concatenate([part, jnp.ones((120, 128), F32)], axis=0).T[0:AB, :]
        ff[rows, :] = jnp.where(low_chip, spread_part, 1.0 - spread_part)
        wide = jnp.concatenate(
            [jnp.broadcast_to(spread_part[:, h : h + 1], (AB, HD)) for h in range(CH)], axis=1
        )
        me, near = oS[i].astype(F32), oR[i].astype(F32)
        att = jnp.where(low_chip, me, near) * wide + jnp.where(low_chip, near, me) * (1.0 - wide)
        catt[rows, :] = jnp.where(valid_rows(start) < length, att, 0.0).astype(BF)

    def to_near(j, src, dst):
        copy = remote(src.at[2 * j : 2 * j + 2], dst.at[2 * j : 2 * j + 2], Zp)
        copy.start()
        return copy

    def core_sum(opened, j, product):
        slot, to_core = opened
        pS[slot, lrows(j), :] = product(grows(other, j)).astype(BF)
        to_core[j].start()
        own = product(grows(mine, j))
        to_core[j].wait_recv()
        return own + pR[slot, lrows(j), :].astype(F32)

    near_att = []

    @pl.when(foreign)
    def _():
        spread_weight("mo")

    ar2 = sum_open(1, 2, chips=False)
    for j in range(2):
        own = grows(mine, j)
        value = T_[own, :].astype(F32) + take(ar1, j) + row(so_bias)
        m1[lrows(j), :] = value
        n, _ = normed(value)
        x2[own, :] = (n * gain(1) + shift(1)).astype(BF)
        both(share(x2, j), lambda h: cross_fwd(h, j))
        near_att.append((to_near(j, oS, oR), to_near(j, stS, stR)))

        if j == 0:
            @pl.when(foreign)
            def _():
                spread_weight("mi")

    @pl.when(native)
    def _():
        lc_cot.wait()

    @pl.when(foreign)
    def _():
        rc_cot.wait_recv()

    need_weight("mo")

    def grad_active(i):
        rows = ds(i * 128, 128)
        fin[rows, :] = nt(G_[rows, :], mo[...])

    loop(T // 128, grad_active)
    need_weight("mi")
    need_weight("co")

    def mlp(rows):
        hidden = nn(x3[rows, :], mi[...]) + qb_[4:5, :]
        phi = 0.5 * (1.0 + lax.erf(hidden * (0.5**0.5)))
        density = jnp.exp(-0.5 * hidden * hidden) * (1.0 / math.sqrt(2.0 * math.pi))
        act[rows, :] = (hidden * phi).astype(BF)
        gh[rows, :] = (fin[rows, :] * (phi + hidden * density)).astype(BF)

    ar3 = sum_open(0, 3)
    for j in (2, 0, 1):
        own = grows(mine, j)
        if j == 2:
            value = T_[own, :].astype(F32) + row(so_bias) + row(co_bias)
        else:
            for copy in near_att[j]:
                copy.wait_recv()
            loop(2, lambda h: merge(h, j))
            value = core_sum(ar2, j, lambda rows: nn(catt[rows, :], co[...])) + m1[lrows(j), :] + row(co_bias)
        m2[lrows(j), :] = value
        n, _ = normed(value)
        x3[own, :] = (n * gain(2) + shift(2)).astype(BF)
        both(share(x3, j), lambda h: mlp(grows(h, j)))
        emit(ar3, j, lambda rows: nt(gh[rows, :], mi[...]))
        if j == 2:
            @pl.when(foreign)
            def _():
                spread_weight("si")


    gsends = {}

    def plane_send(m):
        gsends[m] = [
            remote(gb.at[m, ds(kk * 192, 192), :], gR.at[m, s], dev)
            for s, (dev, kk) in enumerate(plane)
        ]
        for copy in gsends[m]:
            copy.start()

    lefts, rights = slice(0, D // 2), slice(D // 2, D)
    k_x, k_y, k_xy = (kk for _, kk in plane)
    two_step = {}

    def half_send(m, k, cols, slot, dev):
        return remote(gb.at[m, ds(k * 192, 192), cols], gR.at[m, slot, :, cols], dev)

    def step_one(m):
        two_step[m] = [
            half_send(m, k_xy, lefts, 1, X), half_send(m, k_xy, rights, 1, Y),
            half_send(m, k_x, lefts, 0, X), half_send(m, k_y, rights, 0, Y),
        ]
        for copy in two_step[m]:
            copy.start()

    def step_two(m):
        for i, (k, cols, dev) in enumerate(((k_y, lefts, Y), (k_x, rights, X))):
            rows = ds(k * 192, 192)
            two_step[m][i].wait_recv()
            total = gb[m, rows, cols].astype(F32) + gR[m, 1, :, cols].astype(F32)
            gb[m, rows, cols] = total.astype(BF)
            copy = half_send(m, k, cols, 2, dev)
            copy.start()
            two_step[m].append(copy)

    thirds = [slice(i * 256, (i + 1) * 256) for i in range(3)]
    for cols in thirds:
        gb[0, cols, :] = tn(x3[:, cols], gh[...]).astype(BF)
    step_one(0)
    arm = sum_open(2, 3)
    for j in range(3):
        emit(arm, j, lambda rows: nn(act[rows, :], mo[...]))
    for cols in thirds:
        gb[1, cols, :] = tn(G_[:, cols], act[...]).astype(BF)
    step_one(1)
    mi_sums = colsum(gh[...].astype(F32))

    step_two(0)
    need_weight("si")

    @pl.when(foreign)
    def _():
        ln0(T_)
        qkv(si, qb_)
        self_fwd(length, None)

    zero_row = jnp.zeros((1, D), F32)
    g_gain, g_shift = [zero_row] * 3, [zero_row] * 3
    b_out = [zero_row] * 3

    def norm_back(value, upstream, i):
        n, inv = normed(value)
        a = upstream * gain(i)
        g_gain[i] = g_gain[i] + colsum(upstream * n)
        g_shift[i] = g_shift[i] + colsum(upstream)
        return inv * (a - jnp.mean(a, axis=-1, keepdims=True) - n * jnp.mean(a * n, axis=-1, keepdims=True))

    def third_back(j):
        g = G_[grows(mine, j), :].astype(F32)
        b_out[2] = b_out[2] + colsum(g)
        value = g + norm_back(m2[lrows(j), :], take(ar3, j), 2)
        low = value.astype(BF)
        b_out[1] = b_out[1] + colsum(low.astype(F32))
        fin[lrows(j), :] = value
        return low

    def cross_bwd(h_, j):
        start = gstart(h_, j)
        rows = ds(start, AB)
        valid = valid_rows(start) < length
        grads = jnp.where(valid, nt(ups[rows, :], co[...]), 0.0).astype(BF)
        heads_to(dO, rows, grads)
        weighted = grads.astype(F32) * catt[rows, :].astype(F32)
        outs = []
        for h in range(CH):
            cols = slice(h * HD, (h + 1) * HD)
            factor = ff[rows, h : h + 1]
            dOf[h, rows, :] = (grads[:, cols].astype(F32) * factor).astype(BF)
            delta = jnp.sum(weighted[:, cols], axis=-1, keepdims=True)
            dp_ = nt(dO[h, rows, :], V_[h])
            dsv = (pc_[h, rows, :].astype(F32) * ((dp_ - delta) * factor)).astype(BF)
            dsb[h, rows, :] = dsv
            outs.append(nn(dsv, K_[h]) * 0.125)
        gqS[2 * j + h_] = jnp.concatenate(outs, axis=1).astype(BF)

    outs = []

    def give(slot, out_ref):
        from_n, from_f, to_core, onward = [], [], [], []
        for lo, hi, step, size in ((0, 0, TA // 2, AB), (2 * AB, TA, PB, PB // 2)):
            src = gO.at[slot, ds(lo + block * size, size), :]
            dst = out_ref.at[ds(hi + c * step + block * size, size), :]
            from_n.append(remote(src, dst, Fz, "n"))
            from_f.append(remote(src, dst, CF, "f"))
            both_rows = out_ref.at[ds(hi + c * step, 2 * size), :]
            to_core.append(remote(gO.at[slot, lo : lo + 2 * size, :], both_rows, C, "f"))
            for h in range(2):
                rows = out_ref.at[ds(hi + h * step + block * size, size), :]
                onward.append(remote(rows, rows, Zp, "f"))

        @pl.when(native)
        def _():
            for copy in from_n:
                copy.start()
            for j in range(3):
                out_ref[grows(mine, j), :] = gO[slot, lrows(j), :]

        @pl.when(foreign)
        def _():
            for copy in from_f + to_core:
                copy.start()

        outs.append((from_n, from_f, to_core, onward))

    def pass_on(slot):
        from_n, from_f, to_core, onward = outs[slot]

        @pl.when(foreign)
        def _():
            for copy in from_n + from_f:
                copy.wait_recv()
            for copy in onward:
                copy.start()

    def give_mixed():
        for j in range(3):
            value = m2[lrows(j), :] + take(arm, j) + row(mo_bias)
            gO[0, lrows(j), :] = value.astype(BF)
        give(0, mixed_o)

    ar4 = sum_open(1, 2, chips=False)
    near_queries = []
    for j in range(2):
        ups[grows(mine, j), :] = third_back(j)
        both(share(ups, j), lambda h: cross_bwd(h, j))
        near_queries.append(to_near(j, gqS, gqR))
        if j == 0:
            step_two(1)
            give_mixed()

    finals = {}
    own_piece = ds(chip * 192, 192)
    for m in range(4):
        finals[m] = (
            remote(gb.at[m, own_piece, :], gFr.at[m], Fz, "f"),
            remote(fin.at[m * 96 : (m + 1) * 96, :], grads_o.at[m], C, "n"),
        )

    def piece_sum(m):
        piece = gb[m, own_piece, :].astype(F32)
        if m < 2:
            for copy in two_step[m][2:]:
                copy.wait_recv()
            return piece + gR[m, 0].astype(F32) + gR[m, 2].astype(F32)
        for s in range(3):
            gsends[m][s].wait_recv()
            piece = piece + gR[m, s].astype(F32)
        if m == 2:
            rc_gk.wait_recv()
            piece = piece + jnp.concatenate(
                [jnp.zeros((192, HW), F32), gkR[...].astype(F32), jnp.zeros((192, HW), F32)], axis=1
            )
        return piece

    def piece_out(m):
        @pl.when(foreign)
        def _():
            gb[m, own_piece, :] = piece_sum(m).astype(BF)
            finals[m][0].start()

    def piece_final(m):
        @pl.when(native)
        def _():
            piece = piece_sum(m)
            finals[m][0].wait_recv()
            whole = piece + gFr[m].astype(F32)
            fin[m * 96 : (m + 1) * 96, :] = jnp.where(c == 0, whole[96:192, :], whole[0:96, :])
            finals[m][1].start()
            grads_o[m] = jnp.where(c == 0, whole[0:96, :], whole[96:192, :])

    pad_low = third_back(2)
    b_out[0] = b_out[0] + colsum(pad_low.astype(F32))
    piece_out(0)

    def kv_grad(i):
        rows = ds(i * FP, FP)
        frames = ds(i * FP, FP, 128)
        parts = []
        for first in (0, NH):
            heads = range(first, first + NH)
            parts += [tn(dsb[h, :, frames], cq_[h]) * 0.125 for h in heads]
            parts += [tn(pc_[h, :, frames], dOf[h]) for h in heads]
        gkv[rows, :] = jnp.concatenate(parts, axis=1).astype(BF)

    loop(2, kv_grad)

    def mem_term(s):
        return nn(gkv[ds(s * FP, FP), :], ck[...])[0:FQ]

    my_frames = jnp.where(native, 0, 1)
    mt_core = remote(mtS, mtR, C)
    mt_out = remote(mtF, mgrad_o, CF, "f")
    pick = lambda a, w: (jnp.where(low_chip, a[:, 0:w], a[:, w:]), jnp.where(low_chip, a[:, w:], a[:, 0:w]))
    catt_mine = pick(catt[...], HW)[0]
    for cols in thirds:
        kv_part = tn(slab[0, :, cols], gkv[0:FQ, :]) + tn(slab[1, :, cols], gkv[FP : FP + FQ, :])
        kv_mine, kv_near = pick(kv_part, CW)
        gb[2, cols, HW : 3 * HW] = kv_mine.astype(BF)
        gb[2, cols, 3 * HW :] = tn(ups[:, cols], catt_mine).astype(BF)
        gkb[cols, :] = kv_near.astype(BF)
    near_sends = [
        remote(gkb.at[ds(kk * 192, 192), :], gRb.at[s], dev) for s, (dev, kk) in enumerate(plane)
    ]
    for copy in near_sends:
        copy.start()
    mtS[...] = mem_term(1 - my_frames).astype(BF)
    mt_core.start()
    own_term = mem_term(my_frames)
    mt_core.wait_recv()
    mtF[...] = (own_term + mtR[...].astype(F32)).astype(BF)

    @pl.when(native)
    def _():
        mgrad_o[...] = mtF[...]

    @pl.when(foreign)
    def _():
        mt_out.start()

    rc_gk = remote(gkS, gkR, Zp)
    pass_on(0)
    piece_out(1)

    def self_bwd(start):
        rows = ds(start, AB)
        valid = valid_rows(start) < length
        heads_to(dOs, rows, jnp.where(valid, nt(upo[rows, :], so[...]), 0.0))
        outs = []
        for h in range(NH):
            dp_ = nt(dOs[h, rows, :], v_[h])
            pr = ps_[h, rows, :].astype(F32)
            dsv = (pr * (dp_ - jnp.sum(pr * dp_, axis=-1, keepdims=True))).astype(BF)
            dsb[h, rows, 0:TA] = dsv
            outs.append(nn(dsv, k_[h]) * 0.125)
        gqkv[rows, 0:HW] = jnp.concatenate(outs, axis=1).astype(BF)

    for j in range(2):
        own = grows(mine, j)
        near_queries[j].wait_recv()
        for h in range(2):
            both_rows = ds(gstart(h, j), AB)
            gcq[both_rows, :] = (gqS[2 * j + h].astype(F32) + gqR[2 * j + h].astype(F32)).astype(BF)
        upstream = core_sum(ar4, j, lambda rows: nn(gcq[rows, :], cq[...]))
        value = fin[lrows(j), :] + norm_back(m1[lrows(j), :], upstream, 1)
        low = value.astype(BF)
        b_out[0] = b_out[0] + colsum(low.astype(F32))
        upo[own, :] = low
        fin[TH + j * AB : TH + (j + 1) * AB, :] = value
        both(share(upo, j), lambda h: self_bwd(gstart(h, j)))
    gO[1, lrows(2), :] = pad_low
    kv = [tn(dsb[h, :, 0:TA], q_[h]) * 0.125 for h in range(NH)]
    kv += [tn(ps_[h], dOs[h]) for h in range(NH)]
    gqkv[:, HW:] = jnp.concatenate(kv, axis=1).astype(BF)

    gcq_mine = pick(gcq[...], HW)[0]
    gs = gqkv[...].astype(F32)
    quarter = jnp.concatenate(
        [
            colsum(gs[:, 0:HW]),
            colsum(gs[:, 2 * HW :]),
            colsum(gcq_mine.astype(F32)),
            jnp.zeros((1, HW), F32),
        ],
        axis=1,
    )
    values_sum = pick(colsum(gkv[...].astype(F32)), CW)
    quarters = [jnp.concatenate([jnp.zeros((1, 3 * HW), F32), v[:, HW:]], axis=1) for v in values_sum]

    ids = lax.broadcasted_iota(jnp.int32, (16, 1), 0)
    early, late = slice(0, 16), slice(16, 24)

    def pack(count, values):
        lines = lax.broadcasted_iota(jnp.int32, (count, 1), 0)
        packed = jnp.zeros((count, D), F32)
        for i, line in enumerate(values):
            packed = packed + jnp.where(lines == i, line, 0.0)
        return packed

    def over_cores(part, packed):
        sb[0, part, :] = packed
        copy = remote(sb.at[0, part, :], sR.at[part, :], C)
        copy.start()
        return copy

    def over_plane(part, copy):
        copy.wait_recv()
        sb[1, part, :] = sb[0, part, :] + sR[part, :]
        copies = [remote(sb.at[1, part, :], sX.at[chip, part, :], dev) for dev, _ in plane]
        for copy in copies:
            copy.start()
        sX[chip, part, :] = sb[1, part, :]
        return copies

    def over_chips(part, copies):
        for copy in copies:
            copy.wait_recv()
        sb[2, part, :] = sX[0, part, :] + sX[1, part, :] + sX[2, part, :] + sX[3, part, :]
        copies = [remote(sb.at[2, part, :], sZ.at[z, part, :], dev) for dev in (Zp, Fz, F3)]
        for copy in copies:
            copy.start()
        sZ[z, part, :] = sb[2, part, :]
        return copies

    def whole_sum(part, copies):
        for copy in copies:
            copy.wait_recv()
        return sZ[0, part, :] + sZ[1, part, :] + sZ[2, part, :] + sZ[3, part, :]

    packed = pack(16, [0.5 * v for v in g_gain[1:] + g_shift[1:] + b_out])
    packed = packed + jnp.where(ids == 7 + q, quarter + quarters[0], 0.0)
    packed = packed + jnp.where(ids == 7 + q1, quarters[1], 0.0) + jnp.where(ids == 11 + q, mi_sums, 0.0)
    early_copy = over_cores(early, packed)
    for cols in thirds:
        gb[2, cols, 0:HW] = tn(x2[:, cols], gcq_mine).astype(BF)
    early_copies = over_plane(early, early_copy)
    plane_send(2)
    for cols in thirds:
        left = tn(x1[:, cols], gqkv[...])
        right = tn(upo[:, cols], satt[...])
        gb[3, cols, :] = jnp.concatenate([left, right], axis=1).astype(BF)
    plane_send(3)
    last_core, last_chip = sum_open(0, 2)[1:]
    drains[:] = [item for item in drains if item[0] is not last_chip[1]]
    away, kept = 1 - block, block
    rows_of = lambda h, b: ds(h * (TA // 2) + b * AB, AB)
    last = None
    for step, b in enumerate((away, kept)):
        pS[0, lrows(step), :] = nn(gqkv[rows_of(other, b), :], si[...]).astype(BF)
        last_core[step].start()
        last = nn(gqkv[rows_of(mine, b), :], si[...])
        last_core[step].wait_recv()
        last = last + pR[0, lrows(step), :].astype(F32)
        if step == 0:
            zS[0, lrows(0), :] = last.astype(BF)
            last_chip[0].start()
    last_sum = last

    near_piece = gkb[own_piece, :].astype(F32)
    for s in range(3):
        near_sends[s].wait_recv()
        near_piece = near_piece + gRb[s].astype(F32)
    gkS[...] = near_piece.astype(BF)
    rc_gk.start()
    early_copies = over_chips(early, early_copies)
    piece_out(2)
    piece_final(0)
    piece_final(1)
    own = rows_of(mine, kept)
    last_chip[0].wait_recv()
    last_sum = last_sum + zR[0, lrows(0), :].astype(F32)
    value = fin[ds(TH + kept * AB, AB), :] + norm_back(T_[own, :].astype(F32), last_sum, 0)
    gO[1, 0:AB, :] = value.astype(BF)
    pads_at = lambda b: ds(TA + c * PB + b * (PB // 2), PB // 2)
    pad_src = gO.at[1, ds(2 * AB + block * (PB // 2), PB // 2), :]
    grad_src, grad_dst = gO.at[1, 0:AB, :], igrad_o.at[own, :]
    give_n = [remote(grad_src, grad_dst, dev, "n") for dev in (Fz, Zp)]
    give_f = [remote(grad_src, grad_dst, dev, "f") for dev in (CF, CZ, C)]
    pad_n = remote(pad_src, igrad_o.at[pads_at(block), :], Fz, "n")
    pad_f = remote(pad_src, igrad_o.at[pads_at(block), :], CF, "f")
    pad_c = remote(gO.at[1, 2 * AB : 2 * AB + PB, :], igrad_o.at[grows(mine, 2), :], C, "f")
    onward = []
    for h in range(2):
        for lo, size in ((h * (TA // 2) + block * AB, AB), (TA + h * PB + block * (PB // 2), PB // 2)):
            rows = igrad_o.at[ds(lo, size), :]
            onward.append(remote(rows, rows, Zp, "f"))

    @pl.when(native)
    def _():
        for copy in give_n + [pad_n]:
            copy.start()
        igrad_o[own, :] = gO[1, 0:AB, :]
        igrad_o[grows(mine, 2), :] = pad_low

    @pl.when(foreign)
    def _():
        for copy in give_f + [pad_f, pad_c]:
            copy.start()

    def pass_grad():
        @pl.when(foreign)
        def _():
            give_n[0].wait_recv()
            give_f[0].wait_recv()
            pad_n.wait_recv()
            pad_f.wait_recv()
            for copy in onward:
                copy.start()

    late_copy = over_cores(late, pack(8, [g_gain[0], g_shift[0]]))
    late_copies = over_plane(late, late_copy)
    piece_out(3)
    late_copies = over_chips(late, late_copies)
    pass_grad()
    piece_final(2)
    total = whole_sum(early, early_copies)
    first = whole_sum(late, late_copies)
    small_o[0:1, :] = first[0:1, :]
    small_o[1:3, :] = total[0:2, :]
    small_o[3:4, :] = first[1:2, :]
    small_o[4:9, :] = total[2:7, :]
    small_o[9:10, :] = colsum(jnp.where(ids == 7 + z, total, 0.0))
    small_o[10:11, :] = colsum(jnp.where(ids == 11 + z, total, 0.0))
    small_o[11:16, :] = jnp.zeros((5, D), F32)

    piece_final(3)

    @pl.when(foreign)
    def _():
        for m in range(4):
            finals[m][1].wait_recv()
        mt_out.wait_recv()
        for copy in outs[0][3] + onward:
            copy.wait_recv()

    @pl.when(native)
    def _():
        for copy in outs[0][2] + [give_n[1]] + give_f[1:] + [pad_c]:
            copy.wait_recv()

    for copy, when in drains:
        if when is None:
            copy.wait_send()

    @pl.when(native)
    def _():
        for copy, when in drains:
            if when == "n":
                copy.wait_send()

    @pl.when(foreign)
    def _():
        for copy, when in drains:
            if when == "f":
                copy.wait_send()


def finish_kernel(
    mixed_i, igrad_i, mgrad_i, grads, small,
    mixed_o, igrad_o, mgrad_o, gain_o, shift_o, si_o, sb_o, so_o, sob_o, cq_o, ck_o, cb_o, co_o, cob_o,
    mi_o, mib_o, mo_o, mob_o,
):
    mixed_o[...] = mixed_i[...]
    igrad_o[...] = igrad_i[...]
    mgrad_o[...] = mgrad_i[...]
    gain_o[...] = small[0:3, :]
    shift_o[...] = small[3:6, :]
    for i in range(3):
        si_o[i] = grads[3, :, i * HW : (i + 1) * HW]
    for i in range(2):
        sb_o[i : i + 1, :] = small[9:10, i * HW : (i + 1) * HW]
        cb_o[i : i + 1, :] = small[9:10, (i + 2) * HW : (i + 3) * HW]
        ck_o[i] = grads[2, :, (i + 1) * HW : (i + 2) * HW]
    so_o[...] = grads[3, :, 3 * HW :].T
    cq_o[...] = grads[2, :, 0:HW]
    co_o[...] = grads[2, :, 3 * HW :].T
    sob_o[...] = small[6]
    cob_o[...] = small[7]
    mob_o[...] = small[8]
    mib_o[...] = small[10]
    mi_o[...] = grads[0]
    mo_o[...] = grads[1]


def fused(
    tokens, memory, lengths, cotangent, ln_gain, ln_bias, self_in, self_bias, self_out,
    self_out_bias, cross_q, cross_kv, cross_bias, cross_out, cross_out_bias, mlp_in,
    mlp_in_bias, mlp_out, mlp_out_bias,
):
    vmem = pltpu.VMEM
    heads, frames = vmem((NH, TA, HD), BF), vmem((CH, FT, HD), BF)
    rows, low_rows, own_rows = vmem((T, D), BF), vmem((TA, D), BF), vmem((TH, D), F32)
    att = vmem((TA, HW), BF)
    probs, sums, memo = vmem((CH, TA, FT), BF), vmem((3, TH, D), BF), vmem((FQ, D), BF)
    chip_sums = vmem((2, TH, D), BF)
    heads6, two = vmem((CH, TA, HD), BF), vmem((4, AB, CW), BF)
    wide_w, att6 = vmem((CW, D), BF), vmem((TA, CW), BF)
    scratch = [
        rows, rows, vmem((8, 128), F32), vmem((8, D), F32), vmem((8, D), F32),
        vmem((3 * HW, D), BF), vmem((HW, D), BF), wide_w, vmem((2 * CW, D), BF), wide_w,
        vmem((D, D), BF), vmem((D, D), BF), vmem((2, FQ, D), BF),
        low_rows, heads, heads, heads, vmem((NH, TA, TA), BF), att, att, own_rows, low_rows,
        heads6, frames, frames, probs, att6, own_rows, rows, rows, rows,
        low_rows, heads6, heads6, probs, vmem((FT, 2 * CW), BF), att6, low_rows, heads, vmem((TA, 3 * HW), BF),
        two, two, vmem((4, 16, 128), F32), vmem((4, 16, 128), F32), vmem((TA, 128), F32), two, two,
        sums, sums, chip_sums, chip_sums, vmem((T, D), F32),
        memo, memo, memo,
        vmem((4, D, D), BF), vmem((4, 3, 192, D), BF), vmem((4, 192, D), BF),
        vmem((D, CW), BF), vmem((3, 192, CW), BF), vmem((192, CW), BF), vmem((192, CW), BF),
        vmem((2, TH, D), BF), vmem((3, 24, D), F32), vmem((24, D), F32),
        vmem((4, 24, D), F32), vmem((4, 24, D), F32),
        pltpu.SemaphoreType.DMA((16,)), pltpu.SemaphoreType.DMA((200,)), pltpu.SemaphoreType.DMA((200,)),
    ]
    hbm, on_chip = pl.BlockSpec(memory_space=pl.ANY), pl.BlockSpec(memory_space=pltpu.VMEM)
    shape = jax.ShapeDtypeStruct
    wide = [shape((T, D), BF), shape((T, D), BF), shape((FQ, D), BF)]
    h, v = hbm, on_chip
    parts = pl.pallas_call(
        layer_kernel,
        out_shape=wide + [shape((4, 96, D), F32), shape((16, D), F32)],
        in_specs=[h, h, v, h, v, v, h, v, h, v, h, h, v, h, v, h, v, h, v],
        out_specs=[on_chip] * 5,
        scratch_shapes=scratch,
        compiler_params=pltpu.CompilerParams(
            collective_id=0, has_side_effects=True, vmem_limit_bytes=VMEM_LIMIT
        ),
    )(
        tokens, memory[0], lengths, cotangent, ln_gain, ln_bias,
        jnp.swapaxes(self_in, 1, 2).reshape(3 * HW, D), self_bias, self_out, self_out_bias,
        cross_q.T, jnp.swapaxes(cross_kv, 1, 2).reshape(2 * HW, D), cross_bias, cross_out, cross_out_bias,
        mlp_in, mlp_in_bias, mlp_out, mlp_out_bias,
    )
    vec = shape((D,), F32)
    outs = list(pl.pallas_call(
        finish_kernel,
        out_shape=wide
        + [
            shape((3, D), F32), shape((3, D), F32), shape((3, 96, HW), F32), shape((2, HW), F32),
            shape((HW, 96), F32), vec, shape((96, HW), F32), shape((2, 96, HW), F32), shape((2, HW), F32),
            shape((HW, 96), F32), vec, shape((96, D), F32), vec, shape((96, D), F32), vec,
        ],
        in_specs=[on_chip] * 5,
        out_specs=[on_chip] * 18,
    )(*parts))
    outs[2] = outs[2][None]
    outs[16] = outs[16].T
    return tuple(outs)


def matmul(left, right):
    return jnp.dot(left, right, preferred_element_type=jnp.float32)


def einsum_f(form, left, right):
    return jnp.einsum(form, left, right, preferred_element_type=jnp.float32)


def norm_parts(values):
    average = jnp.mean(values, axis=-1, keepdims=True)
    centred = values - average
    variance = jnp.mean(centred * centred, axis=-1, keepdims=True)
    scale_inv = lax.rsqrt(variance + 1e-05)
    return (centred * scale_inv, scale_inv)


def norm_back(normed, scale_inv, gain, upstream):
    scaled = upstream * gain
    inner = (
        scaled
        - jnp.mean(scaled, axis=-1, keepdims=True)
        - normed * jnp.mean(scaled * normed, axis=-1, keepdims=True)
    )
    return (scale_inv * inner, jnp.sum(upstream * normed, axis=0), jnp.sum(upstream, axis=0))


def softmax_parts(scores):
    row_max = jnp.max(scores, axis=-1, keepdims=True)
    shifted = jnp.exp(scores - row_max)
    totals = jnp.sum(shifted, axis=-1, keepdims=True)
    return (shifted / totals, row_max[..., 0] + jnp.log(totals[..., 0]))


def gelu_exact(values):
    return jax.nn.gelu(values, approximate=False)


def self_forward(queries, keys_self, values_self, allowed, valid_mask):
    row_count, head_width = queries.shape
    head_count = head_width // HD
    query_heads = queries.reshape(row_count, head_count, HD)
    key_heads = keys_self.reshape(row_count, head_count, HD)
    value_heads = values_self.reshape(row_count, head_count, HD)
    scores = einsum_f("thd,shd->hts", query_heads, key_heads) * 0.125
    scores = jnp.where(allowed[None], scores, -1000000000.0)
    probs, log_total = softmax_parts(scores)
    attended = einsum_f("hts,shd->thd", probs.astype(jnp.bfloat16), value_heads).reshape(
        row_count, head_width
    )
    attended = jnp.where(valid_mask, attended, 0.0)
    return (attended.astype(jnp.bfloat16), log_total)


def self_backward(queries, keys_self, values_self, allowed, log_total, grad_out):
    row_count, head_width = queries.shape
    head_count = head_width // HD
    query_heads = queries.reshape(row_count, head_count, HD)
    key_heads = keys_self.reshape(row_count, head_count, HD)
    value_heads = values_self.reshape(row_count, head_count, HD)
    scores = einsum_f("thd,shd->hts", query_heads, key_heads) * 0.125
    scores = jnp.where(allowed[None], scores, -1000000000.0)
    probs = jnp.exp(scores - log_total[..., None])
    grad_heads = grad_out.reshape(row_count, head_count, HD)
    grad_values = einsum_f("hts,thd->shd", probs.astype(jnp.bfloat16), grad_heads)
    grad_probs = einsum_f("thd,shd->hts", grad_heads, value_heads)
    grad_scores = (
        probs * (grad_probs - jnp.sum(probs * grad_probs, axis=-1, keepdims=True))
    ).astype(jnp.bfloat16)
    grad_queries = einsum_f("hts,shd->thd", grad_scores, key_heads) * 0.125
    grad_keys = einsum_f("hts,thd->shd", grad_scores, query_heads) * 0.125
    return (
        grad_queries.reshape(row_count, head_width).astype(jnp.bfloat16),
        grad_keys.reshape(row_count, head_width).astype(jnp.bfloat16),
        grad_values.reshape(row_count, head_width).astype(jnp.bfloat16),
    )


def cross_forward(query_heads, memory_pairs, clip_of):
    row_count, head_count, _ = query_heads.shape
    head_width = head_count * HD
    clip_count = memory_pairs.shape[0]

    def per_clip(carry, clip_item):
        attended, log_rows = carry
        clip_index, clip_pairs = clip_item
        key_heads = clip_pairs[:, :head_width].reshape(-1, head_count, HD)
        value_heads = clip_pairs[:, head_width:].reshape(-1, head_count, HD)
        scores = einsum_f("thd,fhd->htf", query_heads, key_heads) * 0.125
        probs, log_total = softmax_parts(scores)
        result = einsum_f("htf,fhd->thd", probs.astype(jnp.bfloat16), value_heads).reshape(
            row_count, head_width
        )
        member = clip_of == clip_index
        return (
            (
                jnp.where(member[:, None], result, attended),
                jnp.where(member[None, :], log_total, log_rows),
            ),
            None,
        )

    start_carry = (
        jnp.zeros((row_count, head_width), jnp.float32),
        jnp.zeros((head_count, row_count), jnp.float32),
    )
    (attended, log_rows), _ = lax.scan(
        per_clip, start_carry, (jnp.arange(clip_count, dtype=jnp.int32), memory_pairs)
    )
    return (attended.astype(jnp.bfloat16), log_rows)


def cross_backward(query_heads, memory_pairs, clip_of, log_rows, grad_out):
    row_count, head_count, _ = query_heads.shape
    head_width = head_count * HD
    clip_count = memory_pairs.shape[0]

    def per_clip(grad_query, clip_item):
        clip_index, clip_pairs = clip_item
        frames = clip_pairs.shape[0]
        member = clip_of == clip_index
        key_heads = clip_pairs[:, :head_width].reshape(frames, head_count, HD)
        value_heads = clip_pairs[:, head_width:].reshape(frames, head_count, HD)
        scores = einsum_f("thd,fhd->htf", query_heads, key_heads) * 0.125
        probs = jnp.where(member[None, :, None], jnp.exp(scores - log_rows[:, :, None]), 0.0)
        grad_heads = jnp.where(member[:, None], grad_out, jnp.zeros_like(grad_out)).reshape(
            row_count, head_count, HD
        )
        grad_values = einsum_f("htf,thd->fhd", probs.astype(jnp.bfloat16), grad_heads)
        grad_probs = einsum_f("thd,fhd->htf", grad_heads, value_heads)
        grad_scores = (
            probs * (grad_probs - jnp.sum(probs * grad_probs, axis=-1, keepdims=True))
        ).astype(jnp.bfloat16)
        grad_query = grad_query + einsum_f("htf,fhd->thd", grad_scores, key_heads) * 0.125
        grad_keys = einsum_f("htf,thd->fhd", grad_scores, query_heads) * 0.125
        grad_pairs = jnp.concatenate(
            [grad_keys.reshape(frames, head_width), grad_values.reshape(frames, head_width)], axis=1
        )
        return (grad_query, grad_pairs.astype(jnp.bfloat16))

    grad_query, grad_pairs = lax.scan(
        per_clip,
        jnp.zeros((row_count, head_count, HD), jnp.float32),
        (jnp.arange(clip_count, dtype=jnp.int32), memory_pairs),
    )
    return (grad_query.reshape(row_count, head_width).astype(jnp.bfloat16), grad_pairs)


def body(
    tokens,
    memory,
    lengths,
    cotangent,
    ln_gain,
    ln_bias,
    self_in,
    self_bias,
    self_out,
    self_out_bias,
    cross_q,
    cross_kv,
    cross_bias,
    cross_out,
    cross_out_bias,
    mlp_in,
    mlp_in_bias,
    mlp_out,
    mlp_out_bias,
):
    row_count = tokens.shape[0]
    clip_count = lengths.shape[0]
    head_width = self_in.shape[2]
    head_count = head_width // HD
    clip_ends = jnp.cumsum(lengths)
    positions = jnp.arange(row_count, dtype=jnp.int32)
    clip_of = jnp.sum((positions[:, None] >= clip_ends[None, :]).astype(jnp.int32), axis=1)
    valid_mask = (clip_of < clip_count)[:, None]
    allowed = (
        (clip_of[:, None] == clip_of[None, :])
        & (positions[None, :] <= positions[:, None])
        & (clip_of[:, None] < clip_count)
    )
    inputs = tokens.astype(jnp.float32)
    normed_one, scale_one = norm_parts(inputs)
    first_in = (normed_one * ln_gain[0] + ln_bias[0]).astype(jnp.bfloat16)
    queries = (matmul(first_in, self_in[0]) + self_bias[0]).astype(jnp.bfloat16)
    keys_self = matmul(first_in, self_in[1]).astype(jnp.bfloat16)
    values_self = (matmul(first_in, self_in[2]) + self_bias[1]).astype(jnp.bfloat16)
    self_att, log_self = self_forward(queries, keys_self, values_self, allowed, valid_mask)
    mixed_one = inputs + lax.psum(matmul(self_att, self_out), "mp") + self_out_bias
    normed_two, scale_two = norm_parts(mixed_one)
    second_in = (normed_two * ln_gain[1] + ln_bias[1]).astype(jnp.bfloat16)
    cross_queries = (matmul(second_in, cross_q) + cross_bias[0]).astype(jnp.bfloat16)
    slab = lax.all_gather(memory, "mp", axis=1, tiled=True)
    slab_keys = einsum_f("cfd,de->cfe", slab, cross_kv[0]).astype(jnp.bfloat16)
    slab_values = (einsum_f("cfd,de->cfe", slab, cross_kv[1]) + cross_bias[1]).astype(jnp.bfloat16)
    memory_pairs = jnp.concatenate([slab_keys, slab_values], axis=2)
    query_heads = cross_queries.reshape(row_count, head_count, HD)
    cross_att, log_cross = cross_forward(query_heads, memory_pairs, clip_of)
    mixed_two = (
        mixed_one
        + lax.psum(matmul(cross_att, cross_out).astype(jnp.bfloat16), "mp").astype(jnp.float32)
        + cross_out_bias
    )
    normed_three, scale_three = norm_parts(mixed_two)
    third_in = (normed_three * ln_gain[2] + ln_bias[2]).astype(jnp.bfloat16)
    hidden = matmul(third_in, mlp_in) + mlp_in_bias
    active, gelu_back = jax.vjp(gelu_exact, hidden)
    active_low = active.astype(jnp.bfloat16)
    mixed = (
        mixed_two
        + lax.psum(matmul(active_low, mlp_out).astype(jnp.bfloat16), "mp").astype(jnp.float32)
        + mlp_out_bias
    ).astype(jnp.bfloat16)
    upstream = cotangent.astype(jnp.float32)
    grad_mlp_out = einsum_f("tf,td->fd", active_low, cotangent)
    grad_mlp_out_bias = jnp.sum(upstream, axis=0)
    grad_active = einsum_f("td,fd->tf", cotangent, mlp_out)
    grad_hidden = gelu_back(grad_active)[0].astype(jnp.bfloat16)
    grad_mlp_in = einsum_f("td,tf->df", third_in, grad_hidden)
    grad_mlp_in_bias = jnp.sum(grad_hidden.astype(jnp.float32), axis=0)
    grad_third = lax.psum(
        einsum_f("tf,df->td", grad_hidden, mlp_in).astype(jnp.bfloat16), "mp"
    ).astype(jnp.float32)
    back_three, gain_three, shift_three = norm_back(
        normed_three, scale_three, ln_gain[2], grad_third
    )
    grad_two = upstream + back_three
    up_two = grad_two.astype(jnp.bfloat16)
    grad_cross_out = einsum_f("tk,td->kd", cross_att, up_two)
    grad_cross_out_bias = jnp.sum(up_two.astype(jnp.float32), axis=0)
    grad_cross_att = einsum_f("td,kd->tk", up_two, cross_out).astype(jnp.bfloat16)
    grad_cross_att = jnp.where(valid_mask, grad_cross_att, jnp.zeros_like(grad_cross_att))
    grad_cross_queries, grad_pairs = cross_backward(
        query_heads, memory_pairs, clip_of, log_cross, grad_cross_att
    )
    grad_cross_q = einsum_f("td,tk->dk", second_in, grad_cross_queries)
    grad_query_bias = jnp.sum(grad_cross_queries.astype(jnp.float32), axis=0)
    grad_keys_cross = grad_pairs[:, :, :head_width]
    grad_values_cross = grad_pairs[:, :, head_width:]
    grad_cross_kv = jnp.stack(
        [
            einsum_f("cfd,cfe->de", slab, grad_keys_cross),
            einsum_f("cfd,cfe->de", slab, grad_values_cross),
        ]
    )
    grad_value_bias = jnp.sum(grad_values_cross.astype(jnp.float32), axis=(0, 1))
    memory_terms = einsum_f("cfe,de->cfd", grad_keys_cross, cross_kv[0]) + einsum_f(
        "cfe,de->cfd", grad_values_cross, cross_kv[1]
    )
    memory_grad = lax.psum_scatter(
        memory_terms.astype(jnp.bfloat16), "mp", scatter_dimension=1, tiled=True
    )
    grad_cross_bias = jnp.stack([grad_query_bias, grad_value_bias])
    grad_second = lax.psum(
        einsum_f("tk,dk->td", grad_cross_queries, cross_q).astype(jnp.bfloat16), "mp"
    ).astype(jnp.float32)
    back_two, gain_two, shift_two = norm_back(normed_two, scale_two, ln_gain[1], grad_second)
    grad_one = grad_two + back_two
    up_one = grad_one.astype(jnp.bfloat16)
    grad_self_out = einsum_f("tk,td->kd", self_att, up_one)
    grad_self_out_bias = jnp.sum(up_one.astype(jnp.float32), axis=0)
    grad_self_att = einsum_f("td,kd->tk", up_one, self_out).astype(jnp.bfloat16)
    grad_self_att = jnp.where(valid_mask, grad_self_att, jnp.zeros_like(grad_self_att))
    grad_queries, grad_keys_self, grad_values_self = self_backward(
        queries, keys_self, values_self, allowed, log_self, grad_self_att
    )
    grad_self_in = jnp.stack(
        [
            einsum_f("td,tk->dk", first_in, grad_queries),
            einsum_f("td,tk->dk", first_in, grad_keys_self),
            einsum_f("td,tk->dk", first_in, grad_values_self),
        ]
    )
    grad_self_bias = jnp.stack(
        [
            jnp.sum(grad_queries.astype(jnp.float32), axis=0),
            jnp.sum(grad_values_self.astype(jnp.float32), axis=0),
        ]
    )
    first_terms = (
        einsum_f("tk,dk->td", grad_queries, self_in[0])
        + einsum_f("tk,dk->td", grad_keys_self, self_in[1])
        + einsum_f("tk,dk->td", grad_values_self, self_in[2])
    )
    grad_first = lax.psum(first_terms.astype(jnp.bfloat16), "mp").astype(jnp.float32)
    back_one, gain_one, shift_one = norm_back(normed_one, scale_one, ln_gain[0], grad_first)
    input_grad = (grad_one + back_one).astype(jnp.bfloat16)
    sum_self_in, sum_self_out, sum_cross_q, sum_cross_kv, sum_cross_out, sum_mlp_in, sum_mlp_out = (
        lax.psum_scatter(grad_self_in, "dp", scatter_dimension=1, tiled=True),
        lax.psum_scatter(grad_self_out, "dp", scatter_dimension=1, tiled=True),
        lax.psum_scatter(grad_cross_q, "dp", scatter_dimension=0, tiled=True),
        lax.psum_scatter(grad_cross_kv, "dp", scatter_dimension=1, tiled=True),
        lax.psum_scatter(grad_cross_out, "dp", scatter_dimension=1, tiled=True),
        lax.psum_scatter(grad_mlp_in, "dp", scatter_dimension=0, tiled=True),
        lax.psum_scatter(grad_mlp_out, "dp", scatter_dimension=1, tiled=True),
    )
    (
        sum_gain,
        sum_shift,
        sum_self_bias,
        sum_self_out_bias,
        sum_cross_bias,
        sum_cross_out_bias,
        sum_mlp_in_bias,
        sum_mlp_out_bias,
    ) = lax.psum(
        (
            jnp.stack([gain_one, gain_two, gain_three]),
            jnp.stack([shift_one, shift_two, shift_three]),
            grad_self_bias,
            grad_self_out_bias,
            grad_cross_bias,
            grad_cross_out_bias,
            grad_mlp_in_bias,
            grad_mlp_out_bias,
        ),
        "dp",
    )
    return (
        mixed,
        input_grad,
        memory_grad,
        sum_gain,
        sum_shift,
        sum_self_in,
        sum_self_bias,
        sum_self_out,
        sum_self_out_bias,
        sum_cross_q,
        sum_cross_kv,
        sum_cross_bias,
        sum_cross_out,
        sum_cross_out_bias,
        sum_mlp_in,
        sum_mlp_in_bias,
        sum_mlp_out,
        sum_mlp_out_bias,
    )


def solution(mesh):
    in_specs = (
        P("dp", None),
        P("dp", "mp", None),
        P("dp"),
        P("dp", None),
        P(),
        P(),
        P(None, None, "mp"),
        P(None, "mp"),
        P("mp", None),
        P(),
        P(None, "mp"),
        P(None, None, "mp"),
        P(None, "mp"),
        P("mp", None),
        P(),
        P(None, "mp"),
        P("mp"),
        P("mp", None),
        P(),
    )
    out_specs = (
        P("dp", None),
        P("dp", None),
        P("dp", "mp", None),
        P(),
        P(),
        P(None, "dp", "mp"),
        P(None, "mp"),
        P("mp", "dp"),
        P(),
        P("dp", "mp"),
        P(None, "dp", "mp"),
        P(None, "mp"),
        P("mp", "dp"),
        P(),
        P("dp", "mp"),
        P("mp"),
        P("mp", "dp"),
        P(),
    )
    shape = dict(mesh.shape)
    run = fused if (shape["dp"], shape["mp"]) == (8, 4) else body
    return jax.shard_map(run, mesh=mesh, in_specs=in_specs, out_specs=out_specs, check_vma=False)
```
